512 devices in a mesh: blk: 32 (over x_hi, z), aux: 16 (over x_lo, y, core).
Axes of the slice: x: 4 (x_hi: 2, x_lo: 2; x = x_hi * 2 + x_lo), y: 4, z: 16, core: 2. Of those that a mesh axis runs over, the one named last changes fastest.
Arguments:
- tensor: bfloat16 [16, 64, 3, 128, 128], P('aux', 'blk'), may hold values from -0.25 to 0.25
- intersection: int32 [64, 2], P('blk'), may hold values 0 or 1
- counts: int32 [64], replicated, may hold values from 64 to 128
- d_occ: bfloat16 [64, 5, 128, 128], P('blk'), as said below
- d_virt: bfloat16 [64, 5, 128, 128], P('blk'), as said below
Outputs:
- response: float32 [16, 16], P('aux')
The draws below stay inside these ranges and needn't reach their ends.
Inputs may be any that keep to these rules, and one draw needn't show every extreme that they name: d_occ and d_virt are symmetric: block v of row block m is the transpose of block 4 - v of row block (m + v - 2) mod 64. `d_virt`: symmetric in the same way as d_occ.
All inputs are finite; a program needn't handle non-finite values. No bound on the sum of `intersection` on one device may be relied on, other than what follows from the above.
Results may differ from the reference program's by a relative error of at most 0.0028.
Values may be sent and summed in bfloat16 or wider, within the bound.
A program may use at most 64 MiB of HBM per device.

```python
import jax
import jax.numpy as jnp
from jax import lax

BS = 128
WB = 3
WD = 5
WX = 7
NB = 64
NAUX = 16


def symmetric_band(key):
    shape = (NB, WD, BS, BS)
    scale = (2.0 / (WD * BS)) ** 0.5
    raw = jax.random.normal(key, shape, jnp.float32) * scale
    blocks = []
    for v in range(WD):
        mirror = jnp.roll(raw[:, WD - 1 - v], -(v - WD // 2), axis=0)
        blocks.append(0.5 * (raw[:, v] + jnp.swapaxes(mirror, 1, 2)))
    return jnp.stack(blocks, axis=1)


def draw_d_occ(key, part):
    key = jax.random.fold_in(key, 11)
    return symmetric_band(key).astype(jnp.bfloat16)


def draw_d_virt(key, part):
    key = jax.random.fold_in(key, 23)
    return symmetric_band(key).astype(jnp.bfloat16)


def with_ends(values, stream_key, smallest, top_value):
    longest = values.shape.index(max(values.shape))
    spots = []
    for shift in (0, 1):
        where = [jax.random.randint(jax.random.fold_in(stream_key, axis), (), 0, length) for axis, length in enumerate(values.shape)]
        where[longest] = (where[longest] + shift) % values.shape[longest]
        spots.append(tuple(where))
    return values.at[spots[0]].set(smallest).at[spots[1]].set(top_value)


def shard_levels(rng, extent, cuts, smallest, largest):
    level, own = 1.0, jax.random.fold_in(rng, 6)
    for position, parts in cuts:
        heights = jnp.exp(jax.random.uniform(jax.random.fold_in(own, position), (parts,), jnp.float32, smallest / len(cuts), largest / len(cuts)))
        level = level * jnp.repeat(heights, extent[position] // parts).reshape([-1 if axis == position else 1 for axis in range(len(extent))])
    return level


def scatter_about(key, extent, deviation, most, split=(), held_as=jnp.bfloat16):
    factor_of = shard_levels(key, extent, split, -0.22, 0.18) if split else 1.0
    result = jax.random.normal(key, extent, jnp.float32) * deviation * factor_of
    return jnp.minimum(jnp.maximum(result, -most), most).astype(held_as)


def setup_inputs(seed: int = 0) -> dict:
    arg_keys = jax.random.split(jax.random.key(seed), 6)
    tensor = scatter_about(arg_keys[0], (NAUX, NB, WB, BS, BS), ((NB * 7 * BS * BS) ** -0.25), 0.25, ((0, 16), (1, 32)))
    intersection = with_ends((jax.random.randint(arg_keys[1], (NB, 2), 0, 3) < 2).astype(jnp.int32), jax.random.fold_in(arg_keys[1], 1), 0, 1)
    counts = with_ends(jax.random.randint(arg_keys[2], (NB,), BS // 2, BS + 1), jax.random.fold_in(arg_keys[2], 1), BS // 2, BS).astype(jnp.int32)
    d_occ = draw_d_occ(jax.random.fold_in(arg_keys[5], 71), 0)
    d_virt = draw_d_virt(jax.random.fold_in(arg_keys[5], 71), 0)
    return {"tensor": tensor, "intersection": intersection, "counts": counts, "d_occ": d_occ, "d_virt": d_virt}


def masked_row(tensor, intersection, counts, row):
    nblocks = counts.shape[0]
    raw = lax.dynamic_index_in_dim(tensor, row, 1, keepdims=False)
    flags = lax.dynamic_index_in_dim(intersection, row, 0, keepdims=False)
    keep_flags = jnp.concatenate([flags[:1], jnp.ones((1,), jnp.int32), flags[1:]])
    neighbour = (row + jnp.arange(WB, dtype=jnp.int32) - WB // 2) % nblocks
    col_count = counts[neighbour]
    own_count = lax.dynamic_index_in_dim(counts, row, 0, keepdims=False)
    lane_ids = jnp.arange(BS, dtype=jnp.int32)
    factor = (keep_flags[:, None, None] > 0) & (lane_ids[None, :, None] < own_count) & (lane_ids[None, None, :] < col_count[:, None, None])
    return raw * factor.astype(raw.dtype)[None]


def reference(tensor, intersection, counts, d_occ, d_virt):
    nblocks = counts.shape[0]

    def step(carry, row):
        own = masked_row(tensor, intersection, counts, row).astype(jnp.float32)
        x_parts = [None] * WX
        for w in range(WB):
            vrow = lax.dynamic_index_in_dim(d_virt, (row + w - 1) % nblocks, 0, keepdims=False).astype(jnp.float32)
            for d in range(WD):
                update = jnp.einsum("pij,jk->pik", own[:, w], vrow[d])
                x_parts[w + d] = update if x_parts[w + d] is None else x_parts[w + d] + update
        xrow = jnp.stack(x_parts, axis=1).astype(jnp.bfloat16).astype(jnp.float32)
        orow = lax.dynamic_index_in_dim(d_occ, row, 0, keepdims=False).astype(jnp.float32)
        z_parts = [None] * WX
        for v in range(WD):
            other = masked_row(tensor, intersection, counts, (row + v - WD // 2) % nblocks).astype(jnp.float32)
            for w in range(WB):
                update = jnp.einsum("ij,pjk->pik", orow[v], other[:, w])
                z_parts[v + w] = update if z_parts[v + w] is None else z_parts[v + w] + update
        zrow = jnp.stack(z_parts, axis=1)
        carry = carry + jnp.einsum("ptij,qtij->pq", xrow, zrow, precision=lax.Precision.HIGHEST)
        return carry, None

    begin = jnp.zeros((NAUX, NAUX), jnp.float32)
    total, _ = lax.scan(step, begin, jnp.arange(nblocks, dtype=jnp.int32))
    return total
```

```python
import functools

import jax
import jax.numpy as jnp
from jax import lax
from jax.experimental import pallas as pl
from jax.experimental.pallas import tpu as pltpu
from jax.sharding import PartitionSpec as P

MESH = pl.DeviceIdType.MESH
BS = 128
PACK = 16


def kernel(
    n_blk,
    n_aux,
    inter_hbm,
    counts_hbm,
    tensor_ref,
    docc_ref,
    dvirt_ref,
    out_ref,
    inter_ref,
    counts_ref,
    raw,
    omat,
    dmat,
    corner,
    ball,
    w_own,
    all_b,
    all_w,
    row_out,
    row_in,
    sum_out,
    sum_in,
    load_sem,
    rim_send,
    rim_recv,
    a2a_send,
    a2a_recv,
    known,
):
    b = lax.axis_index("blk")
    q = lax.axis_index("aux")
    nblocks = counts_ref.shape[0]
    rows = raw.shape[0]
    share = rows // n_aux
    team = n_aux // 2
    strip = 3 * BS // team
    seat = lax.rem(q, team)
    left = lax.rem(b + n_blk - 1, n_blk)
    right = lax.rem(b + 1, n_blk)
    own = ball.at[pl.ds(rows, rows)]

    def tile(ref, i, j):
        return ref.at[
            pl.ds(pl.multiple_of(i * BS, BS), BS), pl.ds(pl.multiple_of(j * BS, BS), BS)
        ]

    barrier = pltpu.get_barrier_semaphore()

    def greet_blk(i, carry):
        there = lax.rem(b + i, n_blk)
        pl.semaphore_signal(barrier, inc=1, device_id={"blk": there}, device_id_type=MESH)
        return carry

    def greet_aux(i, carry):
        there = lax.rem(q + i, n_aux)
        pl.semaphore_signal(barrier, inc=1, device_id={"aux": there}, device_id_type=MESH)
        return carry

    loads = [
        pltpu.make_async_copy(tensor_ref, raw, load_sem.at[0]),
        pltpu.make_async_copy(inter_hbm, inter_ref, load_sem.at[3]),
        pltpu.make_async_copy(counts_hbm, counts_ref, load_sem.at[4]),
    ]
    for load in loads:
        load.start()

    def stored(ref, m, v):
        return ref.at[pl.ds((5 * m + v) * BS, BS)]

    for m in range(2):
        for c in range(4):
            pltpu.make_async_copy(
                stored(dvirt_ref, m, c + 1 - m), tile(dmat, 3 + m, c), load_sem.at[1]
            ).start()
        pltpu.make_async_copy(stored(dvirt_ref, m, 4 * m), corner.at[m], load_sem.at[1]).start()
        for v in range(5):
            pltpu.make_async_copy(
                stored(docc_ref, m, v), tile(omat, m, m + v), load_sem.at[2]
            ).start()

    greet_blk(1, 0)
    greet_blk(n_blk - 1, 0)
    lax.fori_loop(1, n_aux, greet_aux, 0)

    zero = jnp.zeros((BS, BS), jnp.bfloat16)
    for c in range(4):
        for r in range(8):
            if not 0 <= r - c <= 4:
                tile(dmat, r, c)[...] = zero
    for m in range(2):
        tile(omat, m, 5 - 5 * m)[...] = zero

    for load in loads:
        load.wait()
    row_ids = lax.broadcasted_iota(jnp.int32, (BS, BS), 0)
    col_ids = lax.broadcasted_iota(jnp.int32, (BS, BS), 1)

    for m in range(2):
        row = 2 * b + m
        own_count = counts_ref[row]
        for w in range(3):
            col_count = counts_ref[lax.rem(row + w - 1 + nblocks, nblocks)]
            if w != 1:
                col_count = col_count * inter_ref[m, w // 2]
            keep = (row_ids < own_count) & (col_ids < col_count)
            at = pl.ds((m * 3 + w) * BS, BS)
            block = jnp.where(keep, raw[at, :].astype(jnp.float32), 0.0)
            own[at, :] = block.astype(jnp.bfloat16)

    pltpu.make_async_copy(dvirt_ref, dvirt_ref, load_sem.at[1]).wait()

    def turn(block):
        return block[...].astype(jnp.float32).T.astype(jnp.bfloat16)

    tile(dmat, 1, 1)[...] = turn(corner.at[0])
    tile(dmat, 2, 1)[...] = turn(tile(dmat, 3, 0))
    tile(dmat, 5, 1)[...] = turn(tile(dmat, 3, 3))
    tile(dmat, 2, 2)[...] = turn(tile(dmat, 4, 0))
    tile(dmat, 5, 2)[...] = turn(tile(dmat, 4, 3))
    tile(dmat, 6, 2)[...] = turn(corner.at[1])
    pl.semaphore_wait(barrier, 2 + n_aux - 1)

    def tell(step):
        if step < known.shape[0]:
            for there in (b + 2**step, b + n_blk - 2**step):
                pl.semaphore_signal(
                    known.at[step],
                    inc=1,
                    device_id={"blk": lax.rem(there, n_blk)},
                    device_id_type=MESH,
                )

    def learn(step):
        if step < known.shape[0]:
            pl.semaphore_wait(known.at[step], 2)

    def to_blk(src, dst, sem, there):
        return pltpu.make_async_remote_copy(
            src_ref=src,
            dst_ref=dst,
            send_sem=rim_send.at[sem],
            recv_sem=rim_recv.at[sem],
            device_id={"blk": there},
            device_id_type=MESH,
        )

    def band(r, c):
        return dmat.at[
            pl.ds(pl.multiple_of(r * BS + seat * strip, PACK), strip), pl.ds(c * BS, BS)
        ]

    rims = [
        to_blk(band(2, 2), band(0, 0), 0, right),
        to_blk(band(3, 1), band(5, 3), 1, left),
        to_blk(own, ball.at[pl.ds(0, rows)], 2, right),
        to_blk(own, ball.at[pl.ds(2 * rows, rows)], 3, left),
    ]
    for rim in rims:
        rim.start()
    tell(0)

    def scatter(src, first, dst, sem):
        def piece(there):
            return src.at[pl.ds(pl.multiple_of(first + there * share, PACK), share)]

        def send(i, carry):
            there = lax.rem(q + i, n_aux)
            pltpu.make_async_remote_copy(
                src_ref=piece(there),
                dst_ref=dst.at[q],
                send_sem=a2a_send.at[sem],
                recv_sem=a2a_recv.at[sem],
                device_id={"aux": there},
                device_id_type=MESH,
            ).start()
            return carry

        lax.fori_loop(1, n_aux, send, 0)
        dst[q] = piece(q)[...]

    def scattered(dst, sem):
        pltpu.make_async_copy(
            dst.at[pl.ds(0, n_aux - 1)], dst.at[pl.ds(0, n_aux - 1)], sem
        ).wait()

    scatter(ball, rows, all_b, 0)

    def hand(i, carry):
        there = q - seat + lax.rem(seat + i, team)
        for r, c in ((0, 0), (5, 3)):
            pltpu.make_async_remote_copy(
                src_ref=band(r, c),
                dst_ref=band(r, c),
                send_sem=a2a_send.at[4],
                recv_sem=a2a_recv.at[4],
                device_id={"aux": there},
                device_id_type=MESH,
            ).start()
        return carry

    rims[0].wait_recv()
    rims[1].wait_recv()
    lax.fori_loop(1, team, hand, 0)
    learn(0)
    tell(1)

    pltpu.make_async_copy(docc_ref, docc_ref, load_sem.at[2]).wait()
    handed = dmat.at[pl.ds(0, (team - 1) * strip), pl.ds(0, 2 * BS)]
    pltpu.make_async_copy(handed, handed, a2a_recv.at[4]).wait()
    learn(1)
    tell(2)

    def part(pair):
        blocks = [ball[pl.ds((6 * pair + i) * BS, BS), :] for i in range(6)]
        b_pair = jnp.concatenate(
            [
                jnp.concatenate(blocks[:3] + [zero], axis=1),
                jnp.concatenate([zero] + blocks[3:], axis=1),
            ],
            axis=0,
        )
        at = pl.ds(2 * pair * BS, 4 * BS)
        x_pair = jnp.dot(b_pair, dmat[at, :], preferred_element_type=jnp.float32)
        return jnp.dot(
            omat[:, pl.ds(2 * pair * BS, 2 * BS)],
            x_pair.astype(jnp.bfloat16),
            preferred_element_type=jnp.float32,
        )

    total = part(1)
    rims[2].wait_recv()
    total = total + part(0)
    rims[3].wait_recv()
    learn(2)
    tell(3)
    total = total + part(2)
    total = total.astype(jnp.bfloat16)
    for m in range(2):
        for w in range(3):
            w_own[pl.ds((m * 3 + w) * BS, BS), :] = total[
                m * BS : (m + 1) * BS, (m + w) * BS : (m + w + 1) * BS
            ]

    scatter(w_own, 0, all_w, 1)
    scattered(all_b, a2a_recv.at[0])
    groups = range(share // PACK)
    size = n_aux * PACK

    def flat(ref):
        return jnp.concatenate(
            [ref[:, pl.ds(g * PACK, PACK), :].reshape(size, BS) for g in groups], axis=1
        )

    b_turned = flat(all_b).astype(jnp.float32).T.astype(jnp.bfloat16)
    scattered(all_w, a2a_recv.at[1])
    gram = jnp.dot(flat(all_w), b_turned, preferred_element_type=jnp.float32)
    same = (lax.broadcasted_iota(jnp.int32, (size, size), 0) & (PACK - 1)) == (
        lax.broadcasted_iota(jnp.int32, (size, size), 1) & (PACK - 1)
    )
    gram = jnp.sum(jnp.where(same, gram, 0.0).reshape(n_aux, PACK, size), axis=1)
    fold = (
        lax.broadcasted_iota(jnp.int32, (size, BS), 0) // PACK
        == lax.broadcasted_iota(jnp.int32, (size, BS), 1)
    ).astype(jnp.float32)
    gram = jnp.dot(
        gram, fold, precision=lax.Precision.HIGHEST, preferred_element_type=jnp.float32
    )
    for p in range(n_aux):
        row_out[p] = gram[p : p + 1, :]

    def send_row(i, carry):
        there = lax.rem(q + i, n_aux)
        pltpu.make_async_remote_copy(
            src_ref=row_out.at[there],
            dst_ref=row_in.at[q],
            send_sem=a2a_send.at[2],
            recv_sem=a2a_recv.at[2],
            device_id={"aux": there},
            device_id_type=MESH,
        ).start()
        return carry

    lax.fori_loop(1, n_aux, send_row, 0)
    row_in[q] = row_out[q]
    scattered(row_in, a2a_recv.at[2])
    sum_out[...] = jnp.sum(row_in[...], axis=0)
    learn(3)

    def send_sum(i, carry):
        there = lax.rem(b + i, n_blk)
        pltpu.make_async_remote_copy(
            src_ref=sum_out,
            dst_ref=sum_in.at[b],
            send_sem=a2a_send.at[3],
            recv_sem=a2a_recv.at[3],
            device_id={"blk": there},
            device_id_type=MESH,
        ).start()
        return carry

    lax.fori_loop(1, n_blk, send_sum, 0)
    sum_in[b] = sum_out[...]
    pltpu.make_async_copy(
        sum_in.at[pl.ds(0, n_blk - 1)], sum_in.at[pl.ds(0, n_blk - 1)], a2a_recv.at[3]
    ).wait()
    out_ref[...] = jnp.sum(sum_in[...], axis=0)[:, : out_ref.shape[1]]

    for rim in rims:
        rim.wait_send()
    scattered(all_b, a2a_send.at[0])
    scattered(all_w, a2a_send.at[1])
    scattered(row_in, a2a_send.at[2])
    pltpu.make_async_copy(handed, handed, a2a_send.at[4]).wait()
    pltpu.make_async_copy(
        sum_in.at[pl.ds(0, n_blk - 1)], sum_in.at[pl.ds(0, n_blk - 1)], a2a_send.at[3]
    ).wait()


def solution(mesh):
    n_blk, n_aux = mesh.shape["blk"], mesh.shape["aux"]
    rows = 2 * 3 * BS
    share = rows // n_aux
    steps = n_blk.bit_length() - 2
    hbm = pl.BlockSpec(memory_space=pltpu.HBM)

    def on_device(tensor, intersection, counts, d_occ, d_virt):
        return pl.pallas_call(
            functools.partial(kernel, n_blk, n_aux),
            out_shape=jax.ShapeDtypeStruct((1, n_aux), jnp.float32),
            in_specs=[hbm] * 5,
            out_specs=pl.BlockSpec(memory_space=pltpu.VMEM),
            scratch_shapes=[
                pltpu.SMEM(intersection.shape, jnp.int32),
                pltpu.SMEM(counts.shape, jnp.int32),
                pltpu.VMEM((rows, BS), jnp.bfloat16),
                pltpu.VMEM((2 * BS, 6 * BS), jnp.bfloat16),
                pltpu.VMEM((8 * BS, 4 * BS), jnp.bfloat16),
                pltpu.VMEM((2, BS, BS), jnp.bfloat16),
                pltpu.VMEM((3 * rows, BS), jnp.bfloat16),
                pltpu.VMEM((rows, BS), jnp.bfloat16),
                pltpu.VMEM((n_aux, share, BS), jnp.bfloat16),
                pltpu.VMEM((n_aux, share, BS), jnp.bfloat16),
                pltpu.VMEM((n_aux, 1, BS), jnp.float32),
                pltpu.VMEM((n_aux, 1, BS), jnp.float32),
                pltpu.VMEM((1, BS), jnp.float32),
                pltpu.VMEM((n_blk, 1, BS), jnp.float32),
                pltpu.SemaphoreType.DMA((5,)),
                pltpu.SemaphoreType.DMA((4,)),
                pltpu.SemaphoreType.DMA((4,)),
                pltpu.SemaphoreType.DMA((5,)),
                pltpu.SemaphoreType.DMA((5,)),
                pltpu.SemaphoreType.REGULAR((steps,)),
            ],
            compiler_params=pltpu.CompilerParams(
                collective_id=0,
                has_side_effects=True,
                vmem_limit_bytes=65536 * 1000,
            ),
        )(
            intersection,
            counts,
            tensor.reshape(rows, BS),
            d_occ.reshape(2 * 5 * BS, BS),
            d_virt.reshape(2 * 5 * BS, BS),
        )

    return jax.shard_map(
        on_device,
        mesh=mesh,
        in_specs=(
            P("aux", "blk", None, None, None),
            P("blk", None),
            P(),
            P("blk", None, None, None),
            P("blk", None, None, None),
        ),
        out_specs=P("aux", None),
        check_vma=False,
    )
```

```python
import functools

import jax
import jax.numpy as jnp
from jax import lax
from jax.experimental import pallas as pl
from jax.experimental.pallas import tpu as pltpu
from jax.sharding import PartitionSpec as P

MESH = pl.DeviceIdType.MESH
BS = 128
PACK = 16


def kernel(
    n_blk,
    n_aux,
    inter_hbm,
    counts_hbm,
    tensor_ref,
    docc_ref,
    dvirt_ref,
    out_ref,
    inter_ref,
    counts_ref,
    raw,
    omat,
    dmat,
    corner,
    ball,
    relay,
    w_own,
    all_b,
    all_w,
    row_out,
    row_in,
    sum_out,
    sum_in,
    load_sem,
    rim_send,
    rim_recv,
    a2a_send,
    a2a_recv,
    known,
    relay_send,
    relay_recv,
):
    b = lax.axis_index("blk")
    q = lax.axis_index("aux")
    nblocks = counts_ref.shape[0]
    rows = raw.shape[0]
    share = rows // n_aux
    team = n_aux // 2
    strip = 3 * BS // team
    seat = lax.rem(q, team)
    left = lax.rem(b + n_blk - 1, n_blk)
    right = lax.rem(b + 1, n_blk)
    own = ball.at[pl.ds(rows, rows)]

    n_z = n_blk // 2
    z = lax.rem(b, n_z)
    top = z == n_z - 1
    wraps = (z == 0) | top
    across = lax.rem(q + n_aux // 2, n_aux)

    def other_half(there):
        return lax.rem(there + n_z, n_blk)

    far_side = jnp.where(top, right, left)
    between = [
        {"aux": across},
        {"blk": other_half(b), "aux": across},
    ]
    beyond = [
        {"blk": far_side, "aux": across},
        {"blk": other_half(far_side), "aux": across},
    ]

    def tile(ref, i, j):
        return ref.at[
            pl.ds(pl.multiple_of(i * BS, BS), BS), pl.ds(pl.multiple_of(j * BS, BS), BS)
        ]

    barrier = pltpu.get_barrier_semaphore()

    def greet_blk(i, carry):
        there = lax.rem(b + i, n_blk)
        pl.semaphore_signal(barrier, inc=1, device_id={"blk": there}, device_id_type=MESH)
        return carry

    def greet_aux(i, carry):
        there = lax.rem(q + i, n_aux)
        pl.semaphore_signal(barrier, inc=1, device_id={"aux": there}, device_id_type=MESH)
        return carry

    loads = [
        pltpu.make_async_copy(tensor_ref, raw, load_sem.at[0]),
        pltpu.make_async_copy(inter_hbm, inter_ref, load_sem.at[3]),
        pltpu.make_async_copy(counts_hbm, counts_ref, load_sem.at[4]),
    ]
    for load in loads:
        load.start()

    def stored(ref, m, v):
        return ref.at[pl.ds((5 * m + v) * BS, BS)]

    for m in range(2):
        for c in range(4):
            pltpu.make_async_copy(
                stored(dvirt_ref, m, c + 1 - m), tile(dmat, 3 + m, c), load_sem.at[1]
            ).start()
        pltpu.make_async_copy(stored(dvirt_ref, m, 4 * m), corner.at[m], load_sem.at[1]).start()
        for v in range(5):
            pltpu.make_async_copy(
                stored(docc_ref, m, v), tile(omat, m, m + v), load_sem.at[2]
            ).start()

    greet_blk(1, 0)
    greet_blk(n_blk - 1, 0)
    lax.fori_loop(1, n_aux, greet_aux, 0)

    @pl.when(wraps)
    def _():
        for there in [between[1]] + beyond:
            pl.semaphore_signal(barrier, inc=1, device_id=there, device_id_type=MESH)


    zero = jnp.zeros((BS, BS), jnp.bfloat16)
    for c in range(4):
        for r in range(8):
            if not 0 <= r - c <= 4:
                tile(dmat, r, c)[...] = zero
    for m in range(2):
        tile(omat, m, 5 - 5 * m)[...] = zero

    for load in loads:
        load.wait()
    row_ids = lax.broadcasted_iota(jnp.int32, (BS, BS), 0)
    col_ids = lax.broadcasted_iota(jnp.int32, (BS, BS), 1)

    for m in range(2):
        row = 2 * b + m
        own_count = counts_ref[row]
        for w in range(3):
            col_count = counts_ref[lax.rem(row + w - 1 + nblocks, nblocks)]
            if w != 1:
                col_count = col_count * inter_ref[m, w // 2]
            keep = (row_ids < own_count) & (col_ids < col_count)
            at = pl.ds((m * 3 + w) * BS, BS)
            block = jnp.where(keep, raw[at, :].astype(jnp.float32), 0.0)
            own[at, :] = block.astype(jnp.bfloat16)

    pltpu.make_async_copy(dvirt_ref, dvirt_ref, load_sem.at[1]).wait()

    def turn(block):
        return block[...].astype(jnp.float32).T.astype(jnp.bfloat16)

    tile(dmat, 1, 1)[...] = turn(corner.at[0])
    tile(dmat, 2, 1)[...] = turn(tile(dmat, 3, 0))
    tile(dmat, 5, 1)[...] = turn(tile(dmat, 3, 3))
    tile(dmat, 2, 2)[...] = turn(tile(dmat, 4, 0))
    tile(dmat, 5, 2)[...] = turn(tile(dmat, 4, 3))
    tile(dmat, 6, 2)[...] = turn(corner.at[1])
    pl.semaphore_wait(barrier, 2 + n_aux - 1 + jnp.where(wraps, 3, 0))

    def tell(step):
        if step < known.shape[0]:
            for there in (b + 2**step, b + n_blk - 2**step):
                pl.semaphore_signal(
                    known.at[step],
                    inc=1,
                    device_id={"blk": lax.rem(there, n_blk)},
                    device_id_type=MESH,
                )

    def learn(step):
        if step < known.shape[0]:
            pl.semaphore_wait(known.at[step], 2)

    def to_blk(src, dst, sem, there):
        return pltpu.make_async_remote_copy(
            src_ref=src,
            dst_ref=dst,
            send_sem=rim_send.at[sem],
            recv_sem=rim_recv.at[sem],
            device_id={"blk": there},
            device_id_type=MESH,
        )

    def band(r, c):
        return dmat.at[
            pl.ds(pl.multiple_of(r * BS + seat * strip, PACK), strip), pl.ds(c * BS, BS)
        ]

    rims = [
        to_blk(band(2, 2), band(0, 0), 0, right),
        to_blk(band(3, 1), band(5, 3), 1, left),
        to_blk(own, ball.at[pl.ds(0, rows)], 2, right),
        to_blk(own, ball.at[pl.ds(2 * rows, rows)], 3, left),
    ]
    rims[0].start()
    rims[1].start()
    pl.when(jnp.logical_not(top))(rims[2].start)
    pl.when(z != 0)(rims[3].start)
    part_rows = rows // 2

    def pass_on(src, dst, send, recv, there):
        pltpu.make_async_remote_copy(
            src_ref=src,
            dst_ref=dst,
            send_sem=send,
            recv_sem=recv,
            device_id=there,
            device_id_type=MESH,
        ).start()

    def outward(side):
        for k in range(2):
            pass_on(
                own.at[pl.ds(k * part_rows, part_rows)],
                relay.at[k],
                rim_send.at[side],
                relay_recv.at[k],
                between[k],
            )

    def onward(side):
        for k in range(2):
            pltpu.make_async_copy(relay.at[k], relay.at[k], relay_recv.at[k]).wait()
            pass_on(
                relay.at[k],
                ball.at[pl.ds((side - 2) * 2 * rows + k * part_rows, part_rows)],
                relay_send,
                rim_recv.at[side],
                beyond[k],
            )

    pl.when(top)(functools.partial(outward, 2))
    pl.when(z == 0)(functools.partial(outward, 3))
    tell(0)

    def scatter(src, first, dst, sem):
        def piece(there):
            return src.at[pl.ds(pl.multiple_of(first + there * share, PACK), share)]

        def send(i, carry):
            there = lax.rem(q + i, n_aux)
            pltpu.make_async_remote_copy(
                src_ref=piece(there),
                dst_ref=dst.at[q],
                send_sem=a2a_send.at[sem],
                recv_sem=a2a_recv.at[sem],
                device_id={"aux": there},
                device_id_type=MESH,
            ).start()
            return carry

        lax.fori_loop(1, n_aux, send, 0)
        dst[q] = piece(q)[...]

    def scattered(dst, sem):
        pltpu.make_async_copy(
            dst.at[pl.ds(0, n_aux - 1)], dst.at[pl.ds(0, n_aux - 1)], sem
        ).wait()

    def hand(i, carry):
        there = q - seat + lax.rem(seat + i, team)
        for r, c in ((0, 0), (5, 3)):
            pltpu.make_async_remote_copy(
                src_ref=band(r, c),
                dst_ref=band(r, c),
                send_sem=a2a_send.at[4],
                recv_sem=a2a_recv.at[4],
                device_id={"aux": there},
                device_id_type=MESH,
            ).start()
        return carry

    rims[0].wait_recv()
    rims[1].wait_recv()
    lax.fori_loop(1, team, hand, 0)
    pl.when(top)(functools.partial(onward, 2))
    pl.when(z == 0)(functools.partial(onward, 3))
    scatter(ball, rows, all_b, 0)
    learn(0)
    tell(1)

    pltpu.make_async_copy(docc_ref, docc_ref, load_sem.at[2]).wait()
    handed = dmat.at[pl.ds(0, (team - 1) * strip), pl.ds(0, 2 * BS)]
    pltpu.make_async_copy(handed, handed, a2a_recv.at[4]).wait()
    learn(1)
    tell(2)

    def part(pair):
        blocks = [ball[pl.ds((6 * pair + i) * BS, BS), :] for i in range(6)]
        b_pair = jnp.concatenate(
            [
                jnp.concatenate(blocks[:3] + [zero], axis=1),
                jnp.concatenate([zero] + blocks[3:], axis=1),
            ],
            axis=0,
        )
        at = pl.ds(2 * pair * BS, 4 * BS)
        x_pair = jnp.dot(b_pair, dmat[at, :], preferred_element_type=jnp.float32)
        return jnp.dot(
            omat[:, pl.ds(2 * pair * BS, 2 * BS)],
            x_pair.astype(jnp.bfloat16),
            preferred_element_type=jnp.float32,
        )

    total = part(1)
    rims[2].wait_recv()
    total = total + part(0)
    rims[3].wait_recv()
    learn(2)
    tell(3)
    total = total + part(2)
    total = total.astype(jnp.bfloat16)
    for m in range(2):
        for w in range(3):
            w_own[pl.ds((m * 3 + w) * BS, BS), :] = total[
                m * BS : (m + 1) * BS, (m + w) * BS : (m + w + 1) * BS
            ]

    scatter(w_own, 0, all_w, 1)
    scattered(all_b, a2a_recv.at[0])
    groups = range(share // PACK)
    size = n_aux * PACK

    def flat(ref):
        return jnp.concatenate(
            [ref[:, pl.ds(g * PACK, PACK), :].reshape(size, BS) for g in groups], axis=1
        )

    b_turned = flat(all_b).astype(jnp.float32).T.astype(jnp.bfloat16)
    scattered(all_w, a2a_recv.at[1])
    gram = jnp.dot(flat(all_w), b_turned, preferred_element_type=jnp.float32)
    same = (lax.broadcasted_iota(jnp.int32, (size, size), 0) & (PACK - 1)) == (
        lax.broadcasted_iota(jnp.int32, (size, size), 1) & (PACK - 1)
    )
    gram = jnp.sum(jnp.where(same, gram, 0.0).reshape(n_aux, PACK, size), axis=1)
    fold = (
        lax.broadcasted_iota(jnp.int32, (size, BS), 0) // PACK
        == lax.broadcasted_iota(jnp.int32, (size, BS), 1)
    ).astype(jnp.float32)
    gram = jnp.dot(
        gram, fold, precision=lax.Precision.HIGHEST, preferred_element_type=jnp.float32
    )
    for p in range(n_aux):
        row_out[p] = gram[p : p + 1, :]

    def send_row(i, carry):
        there = lax.rem(q + i, n_aux)
        pltpu.make_async_remote_copy(
            src_ref=row_out.at[there],
            dst_ref=row_in.at[q],
            send_sem=a2a_send.at[2],
            recv_sem=a2a_recv.at[2],
            device_id={"aux": there},
            device_id_type=MESH,
        ).start()
        return carry

    lax.fori_loop(1, n_aux, send_row, 0)
    row_in[q] = row_out[q]
    scattered(row_in, a2a_recv.at[2])
    sum_out[...] = jnp.sum(row_in[...], axis=0)
    learn(3)

    def send_sum(i, carry):
        there = lax.rem(b + i, n_blk)
        pltpu.make_async_remote_copy(
            src_ref=sum_out,
            dst_ref=sum_in.at[b],
            send_sem=a2a_send.at[3],
            recv_sem=a2a_recv.at[3],
            device_id={"blk": there},
            device_id_type=MESH,
        ).start()
        return carry

    lax.fori_loop(1, n_blk, send_sum, 0)
    sum_in[b] = sum_out[...]
    pltpu.make_async_copy(
        sum_in.at[pl.ds(0, n_blk - 1)], sum_in.at[pl.ds(0, n_blk - 1)], a2a_recv.at[3]
    ).wait()
    out_ref[...] = jnp.sum(sum_in[...], axis=0)[:, : out_ref.shape[1]]

    for rim in rims:
        rim.wait_send()

    @pl.when(wraps)
    def _():
        pltpu.make_async_copy(relay, relay, relay_send).wait()

    scattered(all_b, a2a_send.at[0])
    scattered(all_w, a2a_send.at[1])
    scattered(row_in, a2a_send.at[2])
    pltpu.make_async_copy(handed, handed, a2a_send.at[4]).wait()
    pltpu.make_async_copy(
        sum_in.at[pl.ds(0, n_blk - 1)], sum_in.at[pl.ds(0, n_blk - 1)], a2a_send.at[3]
    ).wait()


def solution(mesh):
    n_blk, n_aux = mesh.shape["blk"], mesh.shape["aux"]
    rows = 2 * 3 * BS
    share = rows // n_aux
    steps = n_blk.bit_length() - 2
    hbm = pl.BlockSpec(memory_space=pltpu.HBM)

    def on_device(tensor, intersection, counts, d_occ, d_virt):
        return pl.pallas_call(
            functools.partial(kernel, n_blk, n_aux),
            out_shape=jax.ShapeDtypeStruct((1, n_aux), jnp.float32),
            in_specs=[hbm] * 5,
            out_specs=pl.BlockSpec(memory_space=pltpu.VMEM),
            scratch_shapes=[
                pltpu.SMEM(intersection.shape, jnp.int32),
                pltpu.SMEM(counts.shape, jnp.int32),
                pltpu.VMEM((rows, BS), jnp.bfloat16),
                pltpu.VMEM((2 * BS, 6 * BS), jnp.bfloat16),
                pltpu.VMEM((8 * BS, 4 * BS), jnp.bfloat16),
                pltpu.VMEM((2, BS, BS), jnp.bfloat16),
                pltpu.VMEM((3 * rows, BS), jnp.bfloat16),
                pltpu.VMEM((2, rows // 2, BS), jnp.bfloat16),
                pltpu.VMEM((rows, BS), jnp.bfloat16),
                pltpu.VMEM((n_aux, share, BS), jnp.bfloat16),
                pltpu.VMEM((n_aux, share, BS), jnp.bfloat16),
                pltpu.VMEM((n_aux, 1, BS), jnp.float32),
                pltpu.VMEM((n_aux, 1, BS), jnp.float32),
                pltpu.VMEM((1, BS), jnp.float32),
                pltpu.VMEM((n_blk, 1, BS), jnp.float32),
                pltpu.SemaphoreType.DMA((5,)),
                pltpu.SemaphoreType.DMA((4,)),
                pltpu.SemaphoreType.DMA((4,)),
                pltpu.SemaphoreType.DMA((5,)),
                pltpu.SemaphoreType.DMA((5,)),
                pltpu.SemaphoreType.REGULAR((steps,)),
                pltpu.SemaphoreType.DMA,
                pltpu.SemaphoreType.DMA((2,)),
            ],
            compiler_params=pltpu.CompilerParams(
                collective_id=0,
                has_side_effects=True,
                vmem_limit_bytes=65536 * 1000,
            ),
        )(
            intersection,
            counts,
            tensor.reshape(rows, BS),
            d_occ.reshape(2 * 5 * BS, BS),
            d_virt.reshape(2 * 5 * BS, BS),
        )

    return jax.shard_map(
        on_device,
        mesh=mesh,
        in_specs=(
            P("aux", "blk", None, None, None),
            P("blk", None),
            P(),
            P("blk", None, None, None),
            P("blk", None, None, None),
        ),
        out_specs=P("aux", None),
        check_vma=False,
    )
```

```python
import functools

import jax
import jax.numpy as jnp
from jax import lax
from jax.experimental import pallas as pl
from jax.experimental.pallas import tpu as pltpu
from jax.sharding import PartitionSpec as P

MESH = pl.DeviceIdType.MESH
BS = 128
PACK = 16


def kernel(
    n_blk,
    n_aux,
    inter_hbm,
    counts_hbm,
    tensor_ref,
    docc_ref,
    dvirt_ref,
    out_ref,
    inter_ref,
    counts_ref,
    raw,
    omat,
    dmat,
    corner,
    ball,
    w_own,
    all_b,
    all_w,
    row_out,
    row_in,
    sum_out,
    sum_in,
    load_sem,
    rim_send,
    rim_recv,
    a2a_send,
    a2a_recv,
    known,
):
    b = lax.axis_index("blk")
    q = lax.axis_index("aux")
    nblocks = counts_ref.shape[0]
    rows = raw.shape[0]
    share = rows // n_aux
    left = lax.rem(b + n_blk - 1, n_blk)
    right = lax.rem(b + 1, n_blk)
    own = ball.at[pl.ds(rows, rows)]

    def tile(ref, i, j):
        return ref.at[
            pl.ds(pl.multiple_of(i * BS, BS), BS), pl.ds(pl.multiple_of(j * BS, BS), BS)
        ]

    barrier = pltpu.get_barrier_semaphore()

    def greet_blk(i, carry):
        there = lax.rem(b + i, n_blk)
        pl.semaphore_signal(barrier, inc=1, device_id={"blk": there}, device_id_type=MESH)
        return carry

    def greet_aux(i, carry):
        there = lax.rem(q + i, n_aux)
        pl.semaphore_signal(barrier, inc=1, device_id={"aux": there}, device_id_type=MESH)
        return carry

    loads = [
        pltpu.make_async_copy(tensor_ref, raw, load_sem.at[0]),
        pltpu.make_async_copy(inter_hbm, inter_ref, load_sem.at[3]),
        pltpu.make_async_copy(counts_hbm, counts_ref, load_sem.at[4]),
    ]
    for load in loads:
        load.start()

    def stored(ref, m, v):
        return ref.at[pl.ds((5 * m + v) * BS, BS)]

    for m in range(2):
        for c in range(4):
            pltpu.make_async_copy(
                stored(dvirt_ref, m, c + 1 - m), tile(dmat, 3 + m, c), load_sem.at[1]
            ).start()
        pltpu.make_async_copy(stored(dvirt_ref, m, 4 * m), corner.at[m], load_sem.at[1]).start()
        for v in range(5):
            pltpu.make_async_copy(
                stored(docc_ref, m, v), tile(omat, m, m + v), load_sem.at[2]
            ).start()

    greet_blk(1, 0)
    greet_blk(n_blk - 1, 0)
    lax.fori_loop(1, n_aux, greet_aux, 0)

    zero = jnp.zeros((BS, BS), jnp.bfloat16)
    for c in range(4):
        for r in range(8):
            if not 0 <= r - c <= 4:
                tile(dmat, r, c)[...] = zero
    for m in range(2):
        tile(omat, m, 5 - 5 * m)[...] = zero

    for load in loads:
        load.wait()
    row_ids = lax.broadcasted_iota(jnp.int32, (BS, BS), 0)
    col_ids = lax.broadcasted_iota(jnp.int32, (BS, BS), 1)

    for m in range(2):
        row = 2 * b + m
        own_count = counts_ref[row]
        for w in range(3):
            col_count = counts_ref[lax.rem(row + w - 1 + nblocks, nblocks)]
            if w != 1:
                col_count = col_count * inter_ref[m, w // 2]
            keep = (row_ids < own_count) & (col_ids < col_count)
            at = pl.ds((m * 3 + w) * BS, BS)
            block = jnp.where(keep, raw[at, :].astype(jnp.float32), 0.0)
            own[at, :] = block.astype(jnp.bfloat16)

    pltpu.make_async_copy(dvirt_ref, dvirt_ref, load_sem.at[1]).wait()

    def turn(block):
        return block[...].astype(jnp.float32).T.astype(jnp.bfloat16)

    tile(dmat, 1, 1)[...] = turn(corner.at[0])
    tile(dmat, 2, 1)[...] = turn(tile(dmat, 3, 0))
    tile(dmat, 5, 1)[...] = turn(tile(dmat, 3, 3))
    tile(dmat, 2, 2)[...] = turn(tile(dmat, 4, 0))
    tile(dmat, 5, 2)[...] = turn(tile(dmat, 4, 3))
    tile(dmat, 6, 2)[...] = turn(corner.at[1])
    pl.semaphore_wait(barrier, 2 + n_aux - 1)

    def tell(step):
        if step < known.shape[0]:
            for there in (b + 2**step, b + n_blk - 2**step):
                pl.semaphore_signal(
                    known.at[step],
                    inc=1,
                    device_id={"blk": lax.rem(there, n_blk)},
                    device_id_type=MESH,
                )

    def learn(step):
        if step < known.shape[0]:
            pl.semaphore_wait(known.at[step], 2)

    def to_blk(src, dst, sem, there):
        return pltpu.make_async_remote_copy(
            src_ref=src,
            dst_ref=dst,
            send_sem=rim_send.at[sem],
            recv_sem=rim_recv.at[sem],
            device_id={"blk": there},
            device_id_type=MESH,
        )

    def band(r, c):
        return dmat.at[pl.ds(r * BS, 3 * BS), pl.ds(c * BS, BS)]

    rims = [
        to_blk(band(2, 2), band(0, 0), 0, right),
        to_blk(band(3, 1), band(5, 3), 1, left),
        to_blk(own, ball.at[pl.ds(0, rows)], 2, right),
        to_blk(own, ball.at[pl.ds(2 * rows, rows)], 3, left),
    ]
    for rim in rims:
        rim.start()
    tell(0)

    def scatter(src, first, dst, sem):
        def piece(there):
            return src.at[pl.ds(pl.multiple_of(first + there * share, PACK), share)]

        def send(i, carry):
            there = lax.rem(q + i, n_aux)
            pltpu.make_async_remote_copy(
                src_ref=piece(there),
                dst_ref=dst.at[q],
                send_sem=a2a_send.at[sem],
                recv_sem=a2a_recv.at[sem],
                device_id={"aux": there},
                device_id_type=MESH,
            ).start()
            return carry

        lax.fori_loop(1, n_aux, send, 0)
        dst[q] = piece(q)[...]

    def scattered(dst, sem):
        pltpu.make_async_copy(
            dst.at[pl.ds(0, n_aux - 1)], dst.at[pl.ds(0, n_aux - 1)], sem
        ).wait()

    scatter(ball, rows, all_b, 0)

    learn(0)
    tell(1)

    pltpu.make_async_copy(docc_ref, docc_ref, load_sem.at[2]).wait()
    rims[0].wait_recv()
    rims[1].wait_recv()
    learn(1)
    tell(2)

    def part(pair):
        blocks = [ball[pl.ds((6 * pair + i) * BS, BS), :] for i in range(6)]
        b_pair = jnp.concatenate(
            [
                jnp.concatenate(blocks[:3] + [zero], axis=1),
                jnp.concatenate([zero] + blocks[3:], axis=1),
            ],
            axis=0,
        )
        at = pl.ds(2 * pair * BS, 4 * BS)
        x_pair = jnp.dot(b_pair, dmat[at, :], preferred_element_type=jnp.float32)
        return jnp.dot(
            omat[:, pl.ds(2 * pair * BS, 2 * BS)],
            x_pair.astype(jnp.bfloat16),
            preferred_element_type=jnp.float32,
        )

    total = part(1)
    rims[2].wait_recv()
    total = total + part(0)
    rims[3].wait_recv()
    learn(2)
    tell(3)
    total = total + part(2)
    total = total.astype(jnp.bfloat16)
    for m in range(2):
        for w in range(3):
            w_own[pl.ds((m * 3 + w) * BS, BS), :] = total[
                m * BS : (m + 1) * BS, (m + w) * BS : (m + w + 1) * BS
            ]

    scatter(w_own, 0, all_w, 1)
    scattered(all_b, a2a_recv.at[0])
    groups = range(share // PACK)
    size = n_aux * PACK

    def flat(ref):
        return jnp.concatenate(
            [ref[:, pl.ds(g * PACK, PACK), :].reshape(size, BS) for g in groups], axis=1
        )

    b_turned = (
        jnp.swapaxes(flat(all_b).astype(jnp.float32).reshape(n_aux, PACK, share // PACK * BS), 0, 1)
        .reshape(size, share // PACK * BS)
        .T.astype(jnp.bfloat16)
    )
    scattered(all_w, a2a_recv.at[1])
    gram = jnp.dot(flat(all_w), b_turned, preferred_element_type=jnp.float32)
    same = (lax.broadcasted_iota(jnp.int32, (size, size), 0) & (PACK - 1)) == (
        lax.broadcasted_iota(jnp.int32, (size, size), 1) // n_aux
    )
    gram = jnp.where(same, gram, 0.0)
    lanes = min(size, BS)
    gram = functools.reduce(jnp.add, [gram[:, c : c + lanes] for c in range(0, size, lanes)])
    gram = jnp.sum(gram.reshape(n_aux, PACK, lanes), axis=1)
    turn_by = lanes // 2
    while turn_by >= n_aux:
        gram = gram + pltpu.roll(gram, turn_by, 1)
        turn_by //= 2
    if lanes < BS:
        gram = jnp.concatenate([gram] * (BS // lanes), axis=1)
    for p in range(n_aux):
        row_out[p] = gram[p : p + 1, :]

    def send_row(i, carry):
        there = lax.rem(q + i, n_aux)
        pltpu.make_async_remote_copy(
            src_ref=row_out.at[there],
            dst_ref=row_in.at[q],
            send_sem=a2a_send.at[2],
            recv_sem=a2a_recv.at[2],
            device_id={"aux": there},
            device_id_type=MESH,
        ).start()
        return carry

    lax.fori_loop(1, n_aux, send_row, 0)
    row_in[q] = row_out[q]
    scattered(row_in, a2a_recv.at[2])
    sum_out[...] = jnp.sum(row_in[...], axis=0)
    learn(3)

    def send_sum(i, carry):
        there = lax.rem(i, 2) * (n_blk // 2) + i // 2

        @pl.when(there != b)
        def _():
            pltpu.make_async_remote_copy(
                src_ref=sum_out,
                dst_ref=sum_in.at[b],
                send_sem=a2a_send.at[3],
                recv_sem=a2a_recv.at[3],
                device_id={"blk": there},
                device_id_type=MESH,
            ).start()

        return carry

    lax.fori_loop(0, n_blk, send_sum, 0)
    sum_in[b] = sum_out[...]
    pltpu.make_async_copy(
        sum_in.at[pl.ds(0, n_blk - 1)], sum_in.at[pl.ds(0, n_blk - 1)], a2a_recv.at[3]
    ).wait()
    out_ref[...] = jnp.sum(sum_in[...], axis=0)[:, : out_ref.shape[1]]

    for rim in rims:
        rim.wait_send()
    scattered(all_b, a2a_send.at[0])
    scattered(all_w, a2a_send.at[1])
    scattered(row_in, a2a_send.at[2])
    pltpu.make_async_copy(
        sum_in.at[pl.ds(0, n_blk - 1)], sum_in.at[pl.ds(0, n_blk - 1)], a2a_send.at[3]
    ).wait()


def solution(mesh):
    n_blk, n_aux = mesh.shape["blk"], mesh.shape["aux"]
    rows = 2 * 3 * BS
    share = rows // n_aux
    steps = n_blk.bit_length() - 2
    hbm = pl.BlockSpec(memory_space=pltpu.HBM)

    def on_device(tensor, intersection, counts, d_occ, d_virt):
        return pl.pallas_call(
            functools.partial(kernel, n_blk, n_aux),
            out_shape=jax.ShapeDtypeStruct((1, n_aux), jnp.float32),
            in_specs=[hbm] * 5,
            out_specs=pl.BlockSpec(memory_space=pltpu.VMEM),
            scratch_shapes=[
                pltpu.SMEM(intersection.shape, jnp.int32),
                pltpu.SMEM(counts.shape, jnp.int32),
                pltpu.VMEM((rows, BS), jnp.bfloat16),
                pltpu.VMEM((2 * BS, 6 * BS), jnp.bfloat16),
                pltpu.VMEM((8 * BS, 4 * BS), jnp.bfloat16),
                pltpu.VMEM((2, BS, BS), jnp.bfloat16),
                pltpu.VMEM((3 * rows, BS), jnp.bfloat16),
                pltpu.VMEM((rows, BS), jnp.bfloat16),
                pltpu.VMEM((n_aux, share, BS), jnp.bfloat16),
                pltpu.VMEM((n_aux, share, BS), jnp.bfloat16),
                pltpu.VMEM((n_aux, 1, BS), jnp.float32),
                pltpu.VMEM((n_aux, 1, BS), jnp.float32),
                pltpu.VMEM((1, BS), jnp.float32),
                pltpu.VMEM((n_blk, 1, BS), jnp.float32),
                pltpu.SemaphoreType.DMA((5,)),
                pltpu.SemaphoreType.DMA((4,)),
                pltpu.SemaphoreType.DMA((4,)),
                pltpu.SemaphoreType.DMA((5,)),
                pltpu.SemaphoreType.DMA((5,)),
                pltpu.SemaphoreType.REGULAR((steps,)),
            ],
            compiler_params=pltpu.CompilerParams(
                collective_id=0,
                has_side_effects=True,
                vmem_limit_bytes=65536 * 1000,
            ),
        )(
            intersection,
            counts,
            tensor.reshape(rows, BS),
            d_occ.reshape(2 * 5 * BS, BS),
            d_virt.reshape(2 * 5 * BS, BS),
        )

    return jax.shard_map(
        on_device,
        mesh=mesh,
        in_specs=(
            P("aux", "blk", None, None, None),
            P("blk", None),
            P(),
            P("blk", None, None, None),
            P("blk", None, None, None),
        ),
        out_specs=P("aux", None),
        check_vma=False,
    )
```

```python
import functools

import jax
import jax.numpy as jnp
from jax import lax
from jax.experimental import pallas as pl
from jax.experimental.pallas import tpu as pltpu
from jax.sharding import PartitionSpec as P

MESH = pl.DeviceIdType.MESH
BS = 128
PACK = 16


def kernel(
    n_blk,
    n_aux,
    inter_hbm,
    counts_hbm,
    tensor_ref,
    docc_ref,
    dvirt_ref,
    out_ref,
    inter_ref,
    counts_ref,
    raw,
    omat,
    dmat,
    corner,
    ball,
    w_own,
    all_b,
    all_w,
    row_out,
    row_in,
    sum_out,
    sum_in,
    load_sem,
    rim_send,
    rim_recv,
    a2a_send,
    a2a_recv,
    known,
):
    b = lax.axis_index("blk")
    q = lax.axis_index("aux")
    nblocks = counts_ref.shape[0]
    rows = raw.shape[0]
    share = rows // n_aux
    left = lax.rem(b + n_blk - 1, n_blk)
    right = lax.rem(b + 1, n_blk)
    own = ball.at[pl.ds(rows, rows)]

    barrier = pltpu.get_barrier_semaphore()

    def greet_blk(i, carry):
        there = lax.rem(b + i, n_blk)
        pl.semaphore_signal(barrier, inc=1, device_id={"blk": there}, device_id_type=MESH)
        return carry

    def greet_aux(i, carry):
        there = lax.rem(q + i, n_aux)
        pl.semaphore_signal(barrier, inc=1, device_id={"aux": there}, device_id_type=MESH)
        return carry

    loads = [
        pltpu.make_async_copy(tensor_ref, raw, load_sem.at[0]),
        pltpu.make_async_copy(inter_hbm, inter_ref, load_sem.at[3]),
        pltpu.make_async_copy(counts_hbm, counts_ref, load_sem.at[4]),
    ]
    for load in loads:
        load.start()

    greet_blk(1, 0)
    greet_blk(n_blk - 1, 0)
    lax.fori_loop(1, n_aux, greet_aux, 0)

    prepare = [
        pltpu.make_async_copy(dvirt_ref.at[0, pl.ds(1, 4)], dmat.at[3], load_sem.at[1]),
        pltpu.make_async_copy(dvirt_ref.at[1, pl.ds(0, 4)], dmat.at[4], load_sem.at[1]),
        pltpu.make_async_copy(dvirt_ref.at[0, 0], corner.at[0], load_sem.at[1]),
        pltpu.make_async_copy(dvirt_ref.at[1, 4], corner.at[1], load_sem.at[1]),
        pltpu.make_async_copy(docc_ref.at[0], omat.at[0, pl.ds(0, 5)], load_sem.at[2]),
        pltpu.make_async_copy(docc_ref.at[1], omat.at[1, pl.ds(1, 5)], load_sem.at[2]),
    ]
    for load in prepare:
        load.start()

    for load in loads:
        load.wait()
    row_ids = lax.broadcasted_iota(jnp.int32, (BS, BS), 0)
    col_ids = lax.broadcasted_iota(jnp.int32, (BS, BS), 1)

    for m in range(2):
        row = 2 * b + m
        own_count = counts_ref[row]
        for w in range(3):
            col_count = counts_ref[lax.rem(row + w - 1 + nblocks, nblocks)]
            if w != 1:
                col_count = col_count * inter_ref[m, w // 2]
            keep = (row_ids < own_count) & (col_ids < col_count)
            at = pl.ds((m * 3 + w) * BS, BS)
            block = jnp.where(keep, raw[at, :].astype(jnp.float32), 0.0)
            own[at, :] = block.astype(jnp.bfloat16)

    pltpu.make_async_copy(dvirt_ref, dvirt_ref, load_sem.at[1]).wait()

    def turn(block):
        return block[...].astype(jnp.float32).T.astype(jnp.bfloat16)

    dmat[5, 1] = turn(dmat.at[3, 3])
    dmat[2, 2] = turn(dmat.at[4, 0])
    pl.semaphore_wait(barrier, 2 + n_aux - 1)

    def tell(step):
        if step < known.shape[0]:
            for there in (b + 2**step, b + n_blk - 2**step):
                pl.semaphore_signal(
                    known.at[step],
                    inc=1,
                    device_id={"blk": lax.rem(there, n_blk)},
                    device_id_type=MESH,
                )

    def learn(step):
        if step < known.shape[0]:
            pl.semaphore_wait(known.at[step], 2)

    def to_blk(src, dst, sem, there):
        return pltpu.make_async_remote_copy(
            src_ref=src,
            dst_ref=dst,
            send_sem=rim_send.at[sem],
            recv_sem=rim_recv.at[sem],
            device_id={"blk": there},
            device_id_type=MESH,
        )

    def band(r, c):
        return dmat.at[pl.ds(r, 3), c]

    rims = [
        to_blk(band(2, 2), band(0, 0), 0, right),
        to_blk(band(3, 1), band(5, 3), 1, left),
        to_blk(own, ball.at[pl.ds(0, rows)], 2, right),
        to_blk(own, ball.at[pl.ds(2 * rows, rows)], 3, left),
    ]
    for rim in rims:
        rim.start()
    tell(0)

    def scatter(src, first, dst, sem):
        def piece(there):
            return src.at[pl.ds(pl.multiple_of(first + there * share, PACK), share)]

        def send(i, carry):
            there = lax.rem(q + i, n_aux)
            pltpu.make_async_remote_copy(
                src_ref=piece(there),
                dst_ref=dst.at[q],
                send_sem=a2a_send.at[sem],
                recv_sem=a2a_recv.at[sem],
                device_id={"aux": there},
                device_id_type=MESH,
            ).start()
            return carry

        lax.fori_loop(1, n_aux, send, 0)
        dst[q] = piece(q)[...]

    def scattered(dst, sem):
        pltpu.make_async_copy(
            dst.at[pl.ds(0, n_aux - 1)], dst.at[pl.ds(0, n_aux - 1)], sem
        ).wait()

    scatter(ball, rows, all_b, 0)

    dmat[1, 1] = turn(corner.at[0])
    dmat[2, 1] = turn(dmat.at[3, 0])
    dmat[5, 2] = turn(dmat.at[4, 3])
    dmat[6, 2] = turn(corner.at[1])
    zero = jnp.zeros((BS, BS), jnp.bfloat16)
    for c in range(4):
        for r in range(8):
            if not 0 <= r - c <= 4:
                dmat[r, c] = zero
    for m in range(2):
        omat[m, 5 - 5 * m] = zero

    learn(0)
    tell(1)

    pltpu.make_async_copy(docc_ref, docc_ref, load_sem.at[2]).wait()
    rims[0].wait_recv()
    rims[1].wait_recv()
    learn(1)
    tell(2)

    def grid(blocks):
        return jnp.concatenate([jnp.concatenate(row, axis=1) for row in blocks], axis=0)

    def part(pair):
        blocks = [ball[pl.ds((6 * pair + i) * BS, BS), :] for i in range(6)]
        b_pair = grid([blocks[:3] + [zero], [zero] + blocks[3:]])
        d_pair = grid([[dmat[2 * pair + r, c] for c in range(4)] for r in range(4)])
        x_pair = jnp.dot(b_pair, d_pair, preferred_element_type=jnp.float32)
        return jnp.dot(
            grid([[omat[m, 2 * pair + n] for n in range(2)] for m in range(2)]),
            x_pair.astype(jnp.bfloat16),
            preferred_element_type=jnp.float32,
        )

    total = part(1)
    rims[2].wait_recv()
    total = total + part(0)
    rims[3].wait_recv()
    learn(2)
    tell(3)
    total = total + part(2)
    total = total.astype(jnp.bfloat16)
    for m in range(2):
        for w in range(3):
            w_own[pl.ds((m * 3 + w) * BS, BS), :] = total[
                m * BS : (m + 1) * BS, (m + w) * BS : (m + w + 1) * BS
            ]

    scatter(w_own, 0, all_w, 1)
    scattered(all_b, a2a_recv.at[0])
    groups = range(share // PACK)
    size = n_aux * PACK

    def flat(ref):
        return jnp.concatenate(
            [ref[:, pl.ds(g * PACK, PACK), :].reshape(size, BS) for g in groups], axis=1
        )

    b_turned = (
        jnp.swapaxes(flat(all_b).astype(jnp.float32).reshape(n_aux, PACK, share // PACK * BS), 0, 1)
        .reshape(size, share // PACK * BS)
        .T.astype(jnp.bfloat16)
    )
    scattered(all_w, a2a_recv.at[1])
    gram = jnp.dot(flat(all_w), b_turned, preferred_element_type=jnp.float32)
    same = (lax.broadcasted_iota(jnp.int32, (size, size), 0) & (PACK - 1)) == (
        lax.broadcasted_iota(jnp.int32, (size, size), 1) // n_aux
    )
    gram = jnp.where(same, gram, 0.0)
    lanes = min(size, BS)
    gram = functools.reduce(jnp.add, [gram[:, c : c + lanes] for c in range(0, size, lanes)])
    gram = jnp.sum(gram.reshape(n_aux, PACK, lanes), axis=1)
    turn_by = lanes // 2
    while turn_by >= n_aux:
        gram = gram + pltpu.roll(gram, turn_by, 1)
        turn_by //= 2
    if lanes < BS:
        gram = jnp.concatenate([gram] * (BS // lanes), axis=1)
    for p in range(n_aux):
        row_out[p] = gram[p : p + 1, :]

    def send_row(i, carry):
        there = lax.rem(i + 1, n_aux)

        @pl.when(there != q)
        def _():
            pltpu.make_async_remote_copy(
                src_ref=row_out.at[there],
                dst_ref=row_in.at[q],
                send_sem=a2a_send.at[2],
                recv_sem=a2a_recv.at[2],
                device_id={"aux": there},
                device_id_type=MESH,
            ).start()

        return carry

    lax.fori_loop(0, n_aux, send_row, 0)
    row_in[q] = row_out[q]
    scattered(row_in, a2a_recv.at[2])
    sum_out[...] = jnp.sum(row_in[...], axis=0)
    learn(3)

    def send_sum(i, carry):
        there = lax.rem(i, 2) * (n_blk // 2) + i // 2

        @pl.when(there != b)
        def _():
            pltpu.make_async_remote_copy(
                src_ref=sum_out,
                dst_ref=sum_in.at[b],
                send_sem=a2a_send.at[3],
                recv_sem=a2a_recv.at[3],
                device_id={"blk": there},
                device_id_type=MESH,
            ).start()

        return carry

    lax.fori_loop(0, n_blk, send_sum, 0)
    sum_in[b] = sum_out[...]
    pltpu.make_async_copy(
        sum_in.at[pl.ds(0, n_blk - 1)], sum_in.at[pl.ds(0, n_blk - 1)], a2a_recv.at[3]
    ).wait()
    out_ref[...] = jnp.sum(sum_in[...], axis=0)[:, : out_ref.shape[1]]

    for rim in rims:
        rim.wait_send()
    scattered(all_b, a2a_send.at[0])
    scattered(all_w, a2a_send.at[1])
    scattered(row_in, a2a_send.at[2])
    pltpu.make_async_copy(
        sum_in.at[pl.ds(0, n_blk - 1)], sum_in.at[pl.ds(0, n_blk - 1)], a2a_send.at[3]
    ).wait()


def solution(mesh):
    n_blk, n_aux = mesh.shape["blk"], mesh.shape["aux"]
    rows = 2 * 3 * BS
    share = rows // n_aux
    steps = n_blk.bit_length() - 2
    hbm = pl.BlockSpec(memory_space=pltpu.HBM)

    def on_device(tensor, intersection, counts, d_occ, d_virt):
        return pl.pallas_call(
            functools.partial(kernel, n_blk, n_aux),
            out_shape=jax.ShapeDtypeStruct((1, n_aux), jnp.float32),
            in_specs=[hbm] * 5,
            out_specs=pl.BlockSpec(memory_space=pltpu.VMEM),
            scratch_shapes=[
                pltpu.SMEM(intersection.shape, jnp.int32),
                pltpu.SMEM(counts.shape, jnp.int32),
                pltpu.VMEM((rows, BS), jnp.bfloat16),
                pltpu.VMEM((2, 6, BS, BS), jnp.bfloat16),
                pltpu.VMEM((8, 4, BS, BS), jnp.bfloat16),
                pltpu.VMEM((2, BS, BS), jnp.bfloat16),
                pltpu.VMEM((3 * rows, BS), jnp.bfloat16),
                pltpu.VMEM((rows, BS), jnp.bfloat16),
                pltpu.VMEM((n_aux, share, BS), jnp.bfloat16),
                pltpu.VMEM((n_aux, share, BS), jnp.bfloat16),
                pltpu.VMEM((n_aux, 1, BS), jnp.float32),
                pltpu.VMEM((n_aux, 1, BS), jnp.float32),
                pltpu.VMEM((1, BS), jnp.float32),
                pltpu.VMEM((n_blk, 1, BS), jnp.float32),
                pltpu.SemaphoreType.DMA((5,)),
                pltpu.SemaphoreType.DMA((4,)),
                pltpu.SemaphoreType.DMA((4,)),
                pltpu.SemaphoreType.DMA((5,)),
                pltpu.SemaphoreType.DMA((5,)),
                pltpu.SemaphoreType.REGULAR((steps,)),
            ],
            compiler_params=pltpu.CompilerParams(
                collective_id=0,
                has_side_effects=True,
                vmem_limit_bytes=65536 * 1000,
            ),
        )(
            intersection,
            counts,
            tensor.reshape(rows, BS),
            d_occ,
            d_virt,
        )

    return jax.shard_map(
        on_device,
        mesh=mesh,
        in_specs=(
            P("aux", "blk", None, None, None),
            P("blk", None),
            P(),
            P("blk", None, None, None),
            P("blk", None, None, None),
        ),
        out_specs=P("aux", None),
        check_vma=False,
    )
```

```python
import functools

import jax
import jax.numpy as jnp
from jax import lax
from jax.experimental import pallas as pl
from jax.experimental.pallas import tpu as pltpu
from jax.sharding import PartitionSpec as P

MESH = pl.DeviceIdType.MESH
BS = 128
PACK = 16


def kernel(
    n_blk,
    n_aux,
    inter_hbm,
    counts_hbm,
    tensor_ref,
    docc_ref,
    dvirt_ref,
    out_ref,
    inter_ref,
    counts_ref,
    raw,
    omat,
    dmat,
    corner,
    ball,
    w_own,
    all_b,
    all_w,
    row_out,
    row_in,
    sum_out,
    sum_in,
    load_sem,
    rim_send,
    rim_recv,
    a2a_send,
    a2a_recv,
    known,
):
    b = lax.axis_index("blk")
    q = lax.axis_index("aux")
    nblocks = counts_ref.shape[0]
    rows = raw.shape[0]
    share = rows // n_aux
    left = (b - 1) & (n_blk - 1)
    right = (b + 1) & (n_blk - 1)
    own = ball.at[pl.ds(rows, rows)]

    barrier = pltpu.get_barrier_semaphore()

    def greet(axis, there):
        pl.semaphore_signal(barrier, inc=1, device_id={axis: there}, device_id_type=MESH)

    loads = [
        pltpu.make_async_copy(tensor_ref, raw, load_sem.at[0]),
        pltpu.make_async_copy(inter_hbm, inter_ref, load_sem.at[3]),
        pltpu.make_async_copy(counts_hbm, counts_ref, load_sem.at[4]),
    ]
    for load in loads:
        load.start()

    greet("blk", right)
    greet("blk", left)
    for i in range(1, n_aux):
        greet("aux", q ^ i)

    prepare = [
        pltpu.make_async_copy(dvirt_ref.at[0, pl.ds(1, 4)], dmat.at[3], load_sem.at[1]),
        pltpu.make_async_copy(dvirt_ref.at[1, pl.ds(0, 4)], dmat.at[4], load_sem.at[1]),
        pltpu.make_async_copy(dvirt_ref.at[0, 0], corner.at[0], load_sem.at[1]),
        pltpu.make_async_copy(dvirt_ref.at[1, 4], corner.at[1], load_sem.at[1]),
        pltpu.make_async_copy(docc_ref.at[0], omat.at[0, pl.ds(0, 5)], load_sem.at[2]),
        pltpu.make_async_copy(docc_ref.at[1], omat.at[1, pl.ds(1, 5)], load_sem.at[2]),
    ]
    for load in prepare:
        load.start()

    for load in loads:
        load.wait()
    row_ids = lax.broadcasted_iota(jnp.int32, (BS, BS), 0)
    col_ids = lax.broadcasted_iota(jnp.int32, (BS, BS), 1)

    for m in range(2):
        row = 2 * b + m
        own_count = counts_ref[row]
        for w in range(3):
            col_count = counts_ref[lax.rem(row + w - 1 + nblocks, nblocks)]
            if w != 1:
                col_count = col_count * inter_ref[m, w // 2]
            keep = (row_ids < own_count) & (col_ids < col_count)
            at = pl.ds((m * 3 + w) * BS, BS)
            block = jnp.where(keep, raw[at, :].astype(jnp.float32), 0.0)
            own[at, :] = block.astype(jnp.bfloat16)

    pltpu.make_async_copy(dvirt_ref, dvirt_ref, load_sem.at[1]).wait()

    def turn(block):
        return block[...].astype(jnp.float32).T.astype(jnp.bfloat16)

    dmat[5, 1] = turn(dmat.at[3, 3])
    dmat[2, 2] = turn(dmat.at[4, 0])
    pl.semaphore_wait(barrier, 2 + n_aux - 1)

    def tell(step):
        if step < known.shape[0]:
            for there in (b + 2**step, b - 2**step):
                pl.semaphore_signal(
                    known.at[step],
                    inc=1,
                    device_id={"blk": there & (n_blk - 1)},
                    device_id_type=MESH,
                )

    def learn(step):
        if step < known.shape[0]:
            pl.semaphore_wait(known.at[step], 2)

    def to_blk(src, dst, sem, there):
        return pltpu.make_async_remote_copy(
            src_ref=src,
            dst_ref=dst,
            send_sem=rim_send.at[sem],
            recv_sem=rim_recv.at[sem],
            device_id={"blk": there},
            device_id_type=MESH,
        )

    def band(r, c):
        return dmat.at[pl.ds(r, 3), c]

    rims = [
        to_blk(band(2, 2), band(0, 0), 0, right),
        to_blk(band(3, 1), band(5, 3), 1, left),
        to_blk(own, ball.at[pl.ds(0, rows)], 2, right),
        to_blk(own, ball.at[pl.ds(2 * rows, rows)], 3, left),
    ]
    for rim in rims:
        rim.start()
    tell(0)

    def scatter(src, first, dst, sem):
        def piece(there):
            return src.at[pl.ds(pl.multiple_of(first + there * share, PACK), share)]

        for i in range(1, n_aux):
            there = q ^ i
            pltpu.make_async_remote_copy(
                src_ref=piece(there),
                dst_ref=dst.at[q],
                send_sem=a2a_send.at[sem],
                recv_sem=a2a_recv.at[sem],
                device_id={"aux": there},
                device_id_type=MESH,
            ).start()
        dst[q] = piece(q)[...]

    def scattered(dst, sem):
        pltpu.make_async_copy(
            dst.at[pl.ds(0, n_aux - 1)], dst.at[pl.ds(0, n_aux - 1)], sem
        ).wait()

    scatter(ball, rows, all_b, 0)

    dmat[1, 1] = turn(corner.at[0])
    dmat[2, 1] = turn(dmat.at[3, 0])
    dmat[5, 2] = turn(dmat.at[4, 3])
    dmat[6, 2] = turn(corner.at[1])
    zero = jnp.zeros((BS, BS), jnp.bfloat16)
    for c in range(4):
        for r in range(8):
            if not 0 <= r - c <= 4:
                dmat[r, c] = zero
    for m in range(2):
        omat[m, 5 - 5 * m] = zero

    learn(0)
    tell(1)

    pltpu.make_async_copy(docc_ref, docc_ref, load_sem.at[2]).wait()
    rims[0].wait_recv()
    rims[1].wait_recv()
    learn(1)
    tell(2)

    def grid(blocks):
        return jnp.concatenate([jnp.concatenate(row, axis=1) for row in blocks], axis=0)

    def part(pair):
        blocks = [ball[pl.ds((6 * pair + i) * BS, BS), :] for i in range(6)]
        b_pair = grid([blocks[:3] + [zero], [zero] + blocks[3:]])
        d_pair = grid([[dmat[2 * pair + r, c] for c in range(4)] for r in range(4)])
        x_pair = jnp.dot(b_pair, d_pair, preferred_element_type=jnp.float32)
        return jnp.dot(
            grid([[omat[m, 2 * pair + n] for n in range(2)] for m in range(2)]),
            x_pair.astype(jnp.bfloat16),
            preferred_element_type=jnp.float32,
        )

    total = part(1)
    rims[2].wait_recv()
    total = total + part(0)
    rims[3].wait_recv()
    learn(2)
    tell(3)
    total = total + part(2)
    total = total.astype(jnp.bfloat16)
    for m in range(2):
        for w in range(3):
            w_own[pl.ds((m * 3 + w) * BS, BS), :] = total[
                m * BS : (m + 1) * BS, (m + w) * BS : (m + w + 1) * BS
            ]

    scatter(w_own, 0, all_w, 1)
    scattered(all_b, a2a_recv.at[0])
    groups = range(share // PACK)
    size = n_aux * PACK

    def flat(ref):
        return jnp.concatenate(
            [ref[:, pl.ds(g * PACK, PACK), :].reshape(size, BS) for g in groups], axis=1
        )

    b_turned = (
        jnp.swapaxes(flat(all_b).astype(jnp.float32).reshape(n_aux, PACK, share // PACK * BS), 0, 1)
        .reshape(size, share // PACK * BS)
        .T.astype(jnp.bfloat16)
    )
    scattered(all_w, a2a_recv.at[1])
    gram = jnp.dot(flat(all_w), b_turned, preferred_element_type=jnp.float32)
    same = (lax.broadcasted_iota(jnp.int32, (size, size), 0) & (PACK - 1)) == (
        lax.broadcasted_iota(jnp.int32, (size, size), 1) // n_aux
    )
    gram = jnp.where(same, gram, 0.0)
    lanes = min(size, BS)
    gram = functools.reduce(jnp.add, [gram[:, c : c + lanes] for c in range(0, size, lanes)])
    gram = jnp.sum(gram.reshape(n_aux, PACK, lanes), axis=1)
    turn_by = lanes // 2
    while turn_by >= n_aux:
        gram = gram + pltpu.roll(gram, turn_by, 1)
        turn_by //= 2
    if lanes < BS:
        gram = jnp.concatenate([gram] * (BS // lanes), axis=1)
    for p in range(n_aux):
        row_out[p] = gram[p : p + 1, :]

    for i in range(1, n_aux):
        pltpu.make_async_remote_copy(
            src_ref=row_out.at[q ^ i],
            dst_ref=row_in.at[q],
            send_sem=a2a_send.at[2],
            recv_sem=a2a_recv.at[2],
            device_id={"aux": q ^ i},
            device_id_type=MESH,
        ).start()
    row_in[q] = row_out[q]
    scattered(row_in, a2a_recv.at[2])
    sum_out[...] = jnp.sum(row_in[...], axis=0)
    learn(3)

    for i in range(n_blk - 1, 0, -1):
        pltpu.make_async_remote_copy(
            src_ref=sum_out,
            dst_ref=sum_in.at[b],
            send_sem=a2a_send.at[3],
            recv_sem=a2a_recv.at[3],
            device_id={"blk": b ^ i},
            device_id_type=MESH,
        ).start()
    sum_in[b] = sum_out[...]
    pltpu.make_async_copy(
        sum_in.at[pl.ds(0, n_blk - 1)], sum_in.at[pl.ds(0, n_blk - 1)], a2a_recv.at[3]
    ).wait()
    out_ref[...] = jnp.sum(sum_in[...], axis=0)[:, : out_ref.shape[1]]

    for rim in rims:
        rim.wait_send()
    scattered(all_b, a2a_send.at[0])
    scattered(all_w, a2a_send.at[1])
    scattered(row_in, a2a_send.at[2])
    pltpu.make_async_copy(
        sum_in.at[pl.ds(0, n_blk - 1)], sum_in.at[pl.ds(0, n_blk - 1)], a2a_send.at[3]
    ).wait()


def solution(mesh):
    n_blk, n_aux = mesh.shape["blk"], mesh.shape["aux"]
    rows = 2 * 3 * BS
    share = rows // n_aux
    steps = n_blk.bit_length() - 2
    hbm = pl.BlockSpec(memory_space=pltpu.HBM)

    def on_device(tensor, intersection, counts, d_occ, d_virt):
        return pl.pallas_call(
            functools.partial(kernel, n_blk, n_aux),
            out_shape=jax.ShapeDtypeStruct((1, n_aux), jnp.float32),
            in_specs=[hbm] * 5,
            out_specs=pl.BlockSpec(memory_space=pltpu.VMEM),
            scratch_shapes=[
                pltpu.SMEM(intersection.shape, jnp.int32),
                pltpu.SMEM(counts.shape, jnp.int32),
                pltpu.VMEM((rows, BS), jnp.bfloat16),
                pltpu.VMEM((2, 6, BS, BS), jnp.bfloat16),
                pltpu.VMEM((8, 4, BS, BS), jnp.bfloat16),
                pltpu.VMEM((2, BS, BS), jnp.bfloat16),
                pltpu.VMEM((3 * rows, BS), jnp.bfloat16),
                pltpu.VMEM((rows, BS), jnp.bfloat16),
                pltpu.VMEM((n_aux, share, BS), jnp.bfloat16),
                pltpu.VMEM((n_aux, share, BS), jnp.bfloat16),
                pltpu.VMEM((n_aux, 1, BS), jnp.float32),
                pltpu.VMEM((n_aux, 1, BS), jnp.float32),
                pltpu.VMEM((1, BS), jnp.float32),
                pltpu.VMEM((n_blk, 1, BS), jnp.float32),
                pltpu.SemaphoreType.DMA((5,)),
                pltpu.SemaphoreType.DMA((4,)),
                pltpu.SemaphoreType.DMA((4,)),
                pltpu.SemaphoreType.DMA((5,)),
                pltpu.SemaphoreType.DMA((5,)),
                pltpu.SemaphoreType.REGULAR((steps,)),
            ],
            compiler_params=pltpu.CompilerParams(
                collective_id=0,
                has_side_effects=True,
                vmem_limit_bytes=56550000,
            ),
        )(
            intersection,
            counts,
            tensor.reshape(rows, BS),
            d_occ,
            d_virt,
        )

    return jax.shard_map(
        on_device,
        mesh=mesh,
        in_specs=(
            P("aux", "blk", None, None, None),
            P("blk", None),
            P(),
            P("blk", None, None, None),
            P("blk", None, None, None),
        ),
        out_specs=P("aux", None),
        check_vma=False,
    )
```

```python
import functools

import jax
import jax.numpy as jnp
from jax import lax
from jax.experimental import pallas as pl
from jax.experimental.pallas import tpu as pltpu
from jax.sharding import PartitionSpec as P

MESH = pl.DeviceIdType.MESH
BS = 128
PACK = 16


def kernel(
    n_blk,
    n_aux,
    inter_hbm,
    counts_hbm,
    tensor_ref,
    docc_ref,
    dvirt_ref,
    out_ref,
    inter_ref,
    counts_ref,
    raw,
    omat,
    dmat,
    corner,
    ball,
    w_own,
    all_b,
    all_w,
    row_out,
    row_in,
    sum_out,
    sum_in,
    load_sem,
    rim_send,
    rim_recv,
    a2a_send,
    a2a_recv,
    known,
):
    b = lax.axis_index("blk")
    q = lax.axis_index("aux")
    core = q & 1
    nblocks = counts_ref.shape[0]
    rows = raw.shape[0]
    share = rows // n_aux
    left = (b - 1) & (n_blk - 1)
    right = (b + 1) & (n_blk - 1)
    own = ball.at[pl.ds(rows, rows)]

    barrier = pltpu.get_barrier_semaphore()

    def greet(axis, there):
        pl.semaphore_signal(barrier, inc=1, device_id={axis: there}, device_id_type=MESH)

    loads = [
        pltpu.make_async_copy(tensor_ref, raw, load_sem.at[0]),
        pltpu.make_async_copy(inter_hbm, inter_ref, load_sem.at[3]),
        pltpu.make_async_copy(counts_hbm, counts_ref, load_sem.at[4]),
    ]
    for load in loads:
        load.start()

    greet("blk", right)
    greet("blk", left)
    for i in range(1, n_aux):
        greet("aux", q ^ i)

    prepare = [
        pltpu.make_async_copy(dvirt_ref.at[0, pl.ds(1, 4)], dmat.at[3], load_sem.at[1]),
        pltpu.make_async_copy(dvirt_ref.at[1, pl.ds(0, 4)], dmat.at[4], load_sem.at[1]),
        pltpu.make_async_copy(dvirt_ref.at[0, 0], corner.at[0], load_sem.at[1]),
        pltpu.make_async_copy(dvirt_ref.at[1, 4], corner.at[1], load_sem.at[1]),
        pltpu.make_async_copy(docc_ref.at[0], omat.at[0, pl.ds(0, 5)], load_sem.at[2]),
        pltpu.make_async_copy(docc_ref.at[1], omat.at[1, pl.ds(1, 5)], load_sem.at[2]),
    ]
    for load in prepare:
        load.start()

    for load in loads:
        load.wait()
    row_ids = lax.broadcasted_iota(jnp.int32, (BS, BS), 0)
    col_ids = lax.broadcasted_iota(jnp.int32, (BS, BS), 1)

    for m in range(2):
        row = 2 * b + m
        own_count = counts_ref[row]
        for w in range(3):
            col_count = counts_ref[lax.rem(row + w - 1 + nblocks, nblocks)]
            if w != 1:
                col_count = col_count * inter_ref[m, w // 2]
            keep = (row_ids < own_count) & (col_ids < col_count)
            at = pl.ds((m * 3 + w) * BS, BS)
            block = jnp.where(keep, raw[at, :].astype(jnp.float32), 0.0)
            own[at, :] = block.astype(jnp.bfloat16)

    pltpu.make_async_copy(dvirt_ref, dvirt_ref, load_sem.at[1]).wait()

    def turn(block):
        return block[...].astype(jnp.float32).T.astype(jnp.bfloat16)

    dmat[5, 1] = turn(dmat.at[3, 3])
    dmat[2, 2] = turn(dmat.at[4, 0])
    pl.semaphore_wait(barrier, 2 + n_aux - 1)

    def tell(step):
        if step < known.shape[0]:
            for there in (b + 2**step, b - 2**step):
                pl.semaphore_signal(
                    known.at[step],
                    inc=1,
                    device_id={"blk": there & (n_blk - 1)},
                    device_id_type=MESH,
                )

    def learn(step):
        if step < known.shape[0]:
            pl.semaphore_wait(known.at[step], 2)

    def to_blk(src, dst, sem, there):
        return pltpu.make_async_remote_copy(
            src_ref=src,
            dst_ref=dst,
            send_sem=rim_send.at[sem],
            recv_sem=rim_recv.at[sem],
            device_id={"blk": there},
            device_id_type=MESH,
        )

    def band(r, c):
        return dmat.at[pl.ds(r, 3), c]

    rims = [
        to_blk(band(2, 2), band(0, 0), 0, right),
        to_blk(band(3, 1), band(5, 3), 1, left),
        to_blk(own, ball.at[pl.ds(0, rows)], 2, right),
        to_blk(own, ball.at[pl.ds(2 * rows, rows)], 3, left),
    ]

    def leave(order):
        for k in order:
            rims[k].start()

    pl.when(core == 0)(functools.partial(leave, (0, 1, 2, 3)))
    pl.when(core == 1)(functools.partial(leave, (1, 0, 3, 2)))
    tell(0)

    cross = n_aux // 2
    across_and_along = [cross]
    for i in list(range(2, cross, 2)) + list(range(1, cross, 2)):
        across_and_along += [i, cross + i]

    def scatter(src, first, dst, sem):
        def piece(there):
            return src.at[pl.ds(pl.multiple_of(first + there * share, PACK), share)]

        for i in across_and_along:
            there = q ^ i if i == cross else q ^ i ^ (core * cross)
            pltpu.make_async_remote_copy(
                src_ref=piece(there),
                dst_ref=dst.at[q],
                send_sem=a2a_send.at[sem],
                recv_sem=a2a_recv.at[sem],
                device_id={"aux": there},
                device_id_type=MESH,
            ).start()
        dst[q] = piece(q)[...]

    def scattered(dst, sem):
        pltpu.make_async_copy(
            dst.at[pl.ds(0, n_aux - 1)], dst.at[pl.ds(0, n_aux - 1)], sem
        ).wait()

    scatter(ball, rows, all_b, 0)

    dmat[1, 1] = turn(corner.at[0])
    dmat[2, 1] = turn(dmat.at[3, 0])
    dmat[5, 2] = turn(dmat.at[4, 3])
    dmat[6, 2] = turn(corner.at[1])
    zero = jnp.zeros((BS, BS), jnp.bfloat16)
    for c in range(4):
        for r in range(8):
            if not 0 <= r - c <= 4:
                dmat[r, c] = zero
    for m in range(2):
        omat[m, 5 - 5 * m] = zero

    learn(0)
    tell(1)

    pltpu.make_async_copy(docc_ref, docc_ref, load_sem.at[2]).wait()
    rims[0].wait_recv()
    rims[1].wait_recv()
    learn(1)
    tell(2)

    def grid(blocks):
        return jnp.concatenate([jnp.concatenate(row, axis=1) for row in blocks], axis=0)

    def part(pair):
        blocks = [
            ball[pl.ds(pl.multiple_of((6 * pair + i) * BS, BS), BS), :] for i in range(6)
        ]
        b_pair = grid([blocks[:3] + [zero], [zero] + blocks[3:]])
        d_pair = grid([[dmat[2 * pair + r, c] for c in range(4)] for r in range(4)])
        x_pair = jnp.dot(b_pair, d_pair, preferred_element_type=jnp.float32)
        return jnp.dot(
            grid([[omat[m, 2 * pair + n] for n in range(2)] for m in range(2)]),
            x_pair.astype(jnp.bfloat16),
            preferred_element_type=jnp.float32,
        )

    total = part(1)
    pl.when(core == 0)(rims[2].wait_recv)
    pl.when(core == 1)(rims[3].wait_recv)
    total = total + part(2 * core)
    pl.when(core == 1)(rims[2].wait_recv)
    pl.when(core == 0)(rims[3].wait_recv)
    learn(2)
    tell(3)
    total = total + part(2 - 2 * core)
    total = total.astype(jnp.bfloat16)
    for m in range(2):
        for w in range(3):
            w_own[pl.ds((m * 3 + w) * BS, BS), :] = total[
                m * BS : (m + 1) * BS, (m + w) * BS : (m + w + 1) * BS
            ]

    scatter(w_own, 0, all_w, 1)
    scattered(all_b, a2a_recv.at[0])
    groups = range(share // PACK)
    size = n_aux * PACK

    def flat(ref):
        return jnp.concatenate(
            [ref[:, pl.ds(g * PACK, PACK), :].reshape(size, BS) for g in groups], axis=1
        )

    b_turned = (
        jnp.swapaxes(flat(all_b).astype(jnp.float32).reshape(n_aux, PACK, share // PACK * BS), 0, 1)
        .reshape(size, share // PACK * BS)
        .T.astype(jnp.bfloat16)
    )
    scattered(all_w, a2a_recv.at[1])
    gram = jnp.dot(flat(all_w), b_turned, preferred_element_type=jnp.float32)
    same = (lax.broadcasted_iota(jnp.int32, (size, size), 0) & (PACK - 1)) == (
        lax.broadcasted_iota(jnp.int32, (size, size), 1) // n_aux
    )
    gram = jnp.where(same, gram, 0.0)
    lanes = min(size, BS)
    gram = functools.reduce(jnp.add, [gram[:, c : c + lanes] for c in range(0, size, lanes)])
    gram = jnp.sum(gram.reshape(n_aux, PACK, lanes), axis=1)
    turn_by = lanes // 2
    while turn_by >= n_aux:
        gram = gram + pltpu.roll(gram, turn_by, 1)
        turn_by //= 2
    if lanes < BS:
        gram = jnp.concatenate([gram] * (BS // lanes), axis=1)
    for p in range(n_aux):
        row_out[p] = gram[p : p + 1, :]

    for i in range(1, n_aux):
        pltpu.make_async_remote_copy(
            src_ref=row_out.at[q ^ i],
            dst_ref=row_in.at[q],
            send_sem=a2a_send.at[2],
            recv_sem=a2a_recv.at[2],
            device_id={"aux": q ^ i},
            device_id_type=MESH,
        ).start()
    row_in[q] = row_out[q]
    scattered(row_in, a2a_recv.at[2])
    sum_out[...] = jnp.sum(row_in[...], axis=0)
    learn(3)

    for i in range(n_blk - 1, 0, -1):
        pltpu.make_async_remote_copy(
            src_ref=sum_out,
            dst_ref=sum_in.at[b],
            send_sem=a2a_send.at[3],
            recv_sem=a2a_recv.at[3],
            device_id={"blk": b ^ i},
            device_id_type=MESH,
        ).start()
    sum_in[b] = sum_out[...]
    pltpu.make_async_copy(
        sum_in.at[pl.ds(0, n_blk - 1)], sum_in.at[pl.ds(0, n_blk - 1)], a2a_recv.at[3]
    ).wait()
    out_ref[...] = jnp.sum(sum_in[...], axis=0)[:, : out_ref.shape[1]]

    for rim in rims:
        rim.wait_send()
    scattered(all_b, a2a_send.at[0])
    scattered(all_w, a2a_send.at[1])
    scattered(row_in, a2a_send.at[2])
    pltpu.make_async_copy(
        sum_in.at[pl.ds(0, n_blk - 1)], sum_in.at[pl.ds(0, n_blk - 1)], a2a_send.at[3]
    ).wait()


def solution(mesh):
    n_blk, n_aux = mesh.shape["blk"], mesh.shape["aux"]
    rows = 2 * 3 * BS
    share = rows // n_aux
    steps = n_blk.bit_length() - 2
    hbm = pl.BlockSpec(memory_space=pltpu.HBM)

    def on_device(tensor, intersection, counts, d_occ, d_virt):
        return pl.pallas_call(
            functools.partial(kernel, n_blk, n_aux),
            out_shape=jax.ShapeDtypeStruct((1, n_aux), jnp.float32),
            in_specs=[hbm] * 5,
            out_specs=pl.BlockSpec(memory_space=pltpu.VMEM),
            scratch_shapes=[
                pltpu.SMEM(intersection.shape, jnp.int32),
                pltpu.SMEM(counts.shape, jnp.int32),
                pltpu.VMEM((rows, BS), jnp.bfloat16),
                pltpu.VMEM((2, 6, BS, BS), jnp.bfloat16),
                pltpu.VMEM((8, 4, BS, BS), jnp.bfloat16),
                pltpu.VMEM((2, BS, BS), jnp.bfloat16),
                pltpu.VMEM((3 * rows, BS), jnp.bfloat16),
                pltpu.VMEM((rows, BS), jnp.bfloat16),
                pltpu.VMEM((n_aux, share, BS), jnp.bfloat16),
                pltpu.VMEM((n_aux, share, BS), jnp.bfloat16),
                pltpu.VMEM((n_aux, 1, BS), jnp.float32),
                pltpu.VMEM((n_aux, 1, BS), jnp.float32),
                pltpu.VMEM((1, BS), jnp.float32),
                pltpu.VMEM((n_blk, 1, BS), jnp.float32),
                pltpu.SemaphoreType.DMA((5,)),
                pltpu.SemaphoreType.DMA((4,)),
                pltpu.SemaphoreType.DMA((4,)),
                pltpu.SemaphoreType.DMA((5,)),
                pltpu.SemaphoreType.DMA((5,)),
                pltpu.SemaphoreType.REGULAR((steps,)),
            ],
            compiler_params=pltpu.CompilerParams(
                collective_id=0,
                has_side_effects=True,
                vmem_limit_bytes=56550000,
            ),
        )(
            intersection,
            counts,
            tensor.reshape(rows, BS),
            d_occ,
            d_virt,
        )

    return jax.shard_map(
        on_device,
        mesh=mesh,
        in_specs=(
            P("aux", "blk", None, None, None),
            P("blk", None),
            P(),
            P("blk", None, None, None),
            P("blk", None, None, None),
        ),
        out_specs=P("aux", None),
        check_vma=False,
    )
```

```python
import functools

import jax
import jax.numpy as jnp
from jax import lax
from jax.experimental import pallas as pl
from jax.experimental.pallas import tpu as pltpu
from jax.sharding import PartitionSpec as P

MESH = pl.DeviceIdType.MESH
BS = 128
PACK = 16
TEAM = 2


def kernel(
    n_blk,
    n_aux,
    inter_hbm,
    counts_hbm,
    tensor_ref,
    docc_ref,
    dvirt_ref,
    out_ref,
    inter_ref,
    counts_ref,
    raw,
    omat,
    dmat,
    corner,
    ball,
    w_own,
    all_b,
    all_w,
    row_out,
    row_in,
    sum_out,
    sum_in,
    load_sem,
    rim_send,
    rim_recv,
    a2a_send,
    a2a_recv,
    known,
    hand_send,
    hand_recv,
):
    b = lax.axis_index("blk")
    q = lax.axis_index("aux")
    seat = q & (TEAM - 1)
    nblocks = counts_ref.shape[0]
    rows = raw.shape[0]
    share = rows // n_aux
    left = (b - 1) & (n_blk - 1)
    right = (b + 1) & (n_blk - 1)
    own = ball.at[pl.ds(rows, rows)]

    barrier = pltpu.get_barrier_semaphore()

    def greet(axis, there):
        pl.semaphore_signal(barrier, inc=1, device_id={axis: there}, device_id_type=MESH)

    loads = [
        pltpu.make_async_copy(tensor_ref, raw, load_sem.at[0]),
        pltpu.make_async_copy(inter_hbm, inter_ref, load_sem.at[3]),
        pltpu.make_async_copy(counts_hbm, counts_ref, load_sem.at[4]),
    ]
    for load in loads:
        load.start()

    greet("blk", right)
    greet("blk", left)
    for i in range(1, n_aux):
        greet("aux", q ^ i)

    prepare = [
        pltpu.make_async_copy(dvirt_ref.at[0, pl.ds(1, 4)], dmat.at[3], load_sem.at[1]),
        pltpu.make_async_copy(dvirt_ref.at[1, pl.ds(0, 4)], dmat.at[4], load_sem.at[1]),
        pltpu.make_async_copy(dvirt_ref.at[0, 0], corner.at[0], load_sem.at[1]),
        pltpu.make_async_copy(dvirt_ref.at[1, 4], corner.at[1], load_sem.at[1]),
        pltpu.make_async_copy(docc_ref.at[0], omat.at[0, pl.ds(0, 5)], load_sem.at[2]),
        pltpu.make_async_copy(docc_ref.at[1], omat.at[1, pl.ds(1, 5)], load_sem.at[2]),
    ]
    for load in prepare:
        load.start()

    for load in loads:
        load.wait()
    row_ids = lax.broadcasted_iota(jnp.int32, (BS, BS), 0)
    col_ids = lax.broadcasted_iota(jnp.int32, (BS, BS), 1)

    for m in range(2):
        row = 2 * b + m
        own_count = counts_ref[row]
        for w in range(3):
            col_count = counts_ref[lax.rem(row + w - 1 + nblocks, nblocks)]
            if w != 1:
                col_count = col_count * inter_ref[m, w // 2]
            keep = (row_ids < own_count) & (col_ids < col_count)
            at = pl.ds((m * 3 + w) * BS, BS)
            block = jnp.where(keep, raw[at, :].astype(jnp.float32), 0.0)
            own[at, :] = block.astype(jnp.bfloat16)

    pltpu.make_async_copy(dvirt_ref, dvirt_ref, load_sem.at[1]).wait()

    def turn(block):
        return block[...].astype(jnp.float32).T.astype(jnp.bfloat16)

    dmat[5, 1] = turn(dmat.at[3, 3])
    dmat[2, 2] = turn(dmat.at[4, 0])
    pl.semaphore_wait(barrier, 2 + n_aux - 1)

    def tell(step):
        if step < known.shape[0]:
            for there in (b + 2**step, b - 2**step):
                pl.semaphore_signal(
                    known.at[step],
                    inc=1,
                    device_id={"blk": there & (n_blk - 1)},
                    device_id_type=MESH,
                )

    def learn(step):
        if step < known.shape[0]:
            pl.semaphore_wait(known.at[step], 2)

    def to_blk(src, dst, sem, there):
        return pltpu.make_async_remote_copy(
            src_ref=src,
            dst_ref=dst,
            send_sem=rim_send.at[sem],
            recv_sem=rim_recv.at[sem],
            device_id={"blk": there},
            device_id_type=MESH,
        )

    def band(r, c):
        strip = BS // TEAM
        return dmat.at[pl.ds(r, 3), c, pl.ds(pl.multiple_of(seat * strip, PACK), strip)]

    rims = [
        to_blk(band(2, 2), band(0, 0), 0, right),
        to_blk(band(3, 1), band(5, 3), 1, left),
        to_blk(own, ball.at[pl.ds(0, rows)], 2, right),
        to_blk(own, ball.at[pl.ds(2 * rows, rows)], 3, left),
    ]
    for rim in rims:
        rim.start()
    tell(0)

    def scatter(src, first, dst, sem):
        def piece(there):
            return src.at[pl.ds(pl.multiple_of(first + there * share, PACK), share)]

        for i in range(1, n_aux):
            there = q ^ i
            pltpu.make_async_remote_copy(
                src_ref=piece(there),
                dst_ref=dst.at[q],
                send_sem=a2a_send.at[sem],
                recv_sem=a2a_recv.at[sem],
                device_id={"aux": there},
                device_id_type=MESH,
            ).start()
        dst[q] = piece(q)[...]

    def scattered(dst, sem):
        pltpu.make_async_copy(
            dst.at[pl.ds(0, n_aux - 1)], dst.at[pl.ds(0, n_aux - 1)], sem
        ).wait()


    dmat[1, 1] = turn(corner.at[0])
    dmat[2, 1] = turn(dmat.at[3, 0])
    dmat[5, 2] = turn(dmat.at[4, 3])
    dmat[6, 2] = turn(corner.at[1])
    zero = jnp.zeros((BS, BS), jnp.bfloat16)
    for c in range(4):
        for r in range(8):
            if not 0 <= r - c <= 4:
                dmat[r, c] = zero
    for m in range(2):
        omat[m, 5 - 5 * m] = zero

    learn(0)
    tell(1)

    pltpu.make_async_copy(docc_ref, docc_ref, load_sem.at[2]).wait()
    handed = []
    for side, rim in enumerate((band(0, 0), band(5, 3))):
        rims[side].wait_recv()
        for i in range(1, TEAM):
            handed.append(
                pltpu.make_async_remote_copy(
                    src_ref=rim,
                    dst_ref=rim,
                    send_sem=hand_send.at[side, i - 1],
                    recv_sem=hand_recv.at[side, i - 1],
                    device_id={"aux": q ^ i},
                    device_id_type=MESH,
                )
            )
            handed[-1].start()
    scatter(ball, rows, all_b, 0)
    learn(1)
    tell(2)
    for copy in handed:
        copy.wait_recv()

    def grid(blocks):
        return jnp.concatenate([jnp.concatenate(row, axis=1) for row in blocks], axis=0)

    def part(pair):
        blocks = [ball[pl.ds((6 * pair + i) * BS, BS), :] for i in range(6)]
        b_pair = grid([blocks[:3] + [zero], [zero] + blocks[3:]])
        d_pair = grid([[dmat[2 * pair + r, c] for c in range(4)] for r in range(4)])
        x_pair = jnp.dot(b_pair, d_pair, preferred_element_type=jnp.float32)
        return jnp.dot(
            grid([[omat[m, 2 * pair + n] for n in range(2)] for m in range(2)]),
            x_pair.astype(jnp.bfloat16),
            preferred_element_type=jnp.float32,
        )

    total = part(1)
    rims[2].wait_recv()
    total = total + part(0)
    rims[3].wait_recv()
    learn(2)
    tell(3)
    total = total + part(2)
    total = total.astype(jnp.bfloat16)
    for m in range(2):
        for w in range(3):
            w_own[pl.ds((m * 3 + w) * BS, BS), :] = total[
                m * BS : (m + 1) * BS, (m + w) * BS : (m + w + 1) * BS
            ]

    scatter(w_own, 0, all_w, 1)
    scattered(all_b, a2a_recv.at[0])
    groups = range(share // PACK)
    size = n_aux * PACK

    def flat(ref):
        return jnp.concatenate(
            [ref[:, pl.ds(g * PACK, PACK), :].reshape(size, BS) for g in groups], axis=1
        )

    b_turned = (
        jnp.swapaxes(flat(all_b).astype(jnp.float32).reshape(n_aux, PACK, share // PACK * BS), 0, 1)
        .reshape(size, share // PACK * BS)
        .T.astype(jnp.bfloat16)
    )
    scattered(all_w, a2a_recv.at[1])
    gram = jnp.dot(flat(all_w), b_turned, preferred_element_type=jnp.float32)
    same = (lax.broadcasted_iota(jnp.int32, (size, size), 0) & (PACK - 1)) == (
        lax.broadcasted_iota(jnp.int32, (size, size), 1) // n_aux
    )
    gram = jnp.where(same, gram, 0.0)
    lanes = min(size, BS)
    gram = functools.reduce(jnp.add, [gram[:, c : c + lanes] for c in range(0, size, lanes)])
    gram = jnp.sum(gram.reshape(n_aux, PACK, lanes), axis=1)
    turn_by = lanes // 2
    while turn_by >= n_aux:
        gram = gram + pltpu.roll(gram, turn_by, 1)
        turn_by //= 2
    if lanes < BS:
        gram = jnp.concatenate([gram] * (BS // lanes), axis=1)
    for p in range(n_aux):
        row_out[p] = gram[p : p + 1, :]

    for i in range(1, n_aux):
        pltpu.make_async_remote_copy(
            src_ref=row_out.at[q ^ i],
            dst_ref=row_in.at[q],
            send_sem=a2a_send.at[2],
            recv_sem=a2a_recv.at[2],
            device_id={"aux": q ^ i},
            device_id_type=MESH,
        ).start()
    row_in[q] = row_out[q]
    scattered(row_in, a2a_recv.at[2])
    sum_out[...] = jnp.sum(row_in[...], axis=0)
    learn(3)

    for i in range(n_blk - 1, 0, -1):
        pltpu.make_async_remote_copy(
            src_ref=sum_out,
            dst_ref=sum_in.at[b],
            send_sem=a2a_send.at[3],
            recv_sem=a2a_recv.at[3],
            device_id={"blk": b ^ i},
            device_id_type=MESH,
        ).start()
    sum_in[b] = sum_out[...]
    pltpu.make_async_copy(
        sum_in.at[pl.ds(0, n_blk - 1)], sum_in.at[pl.ds(0, n_blk - 1)], a2a_recv.at[3]
    ).wait()
    out_ref[...] = jnp.sum(sum_in[...], axis=0)[:, : out_ref.shape[1]]

    for copy in rims + handed:
        copy.wait_send()
    scattered(all_b, a2a_send.at[0])
    scattered(all_w, a2a_send.at[1])
    scattered(row_in, a2a_send.at[2])
    pltpu.make_async_copy(
        sum_in.at[pl.ds(0, n_blk - 1)], sum_in.at[pl.ds(0, n_blk - 1)], a2a_send.at[3]
    ).wait()


def solution(mesh):
    n_blk, n_aux = mesh.shape["blk"], mesh.shape["aux"]
    rows = 2 * 3 * BS
    share = rows // n_aux
    steps = n_blk.bit_length() - 2
    hbm = pl.BlockSpec(memory_space=pltpu.HBM)

    def on_device(tensor, intersection, counts, d_occ, d_virt):
        return pl.pallas_call(
            functools.partial(kernel, n_blk, n_aux),
            out_shape=jax.ShapeDtypeStruct((1, n_aux), jnp.float32),
            in_specs=[hbm] * 5,
            out_specs=pl.BlockSpec(memory_space=pltpu.VMEM),
            scratch_shapes=[
                pltpu.SMEM(intersection.shape, jnp.int32),
                pltpu.SMEM(counts.shape, jnp.int32),
                pltpu.VMEM((rows, BS), jnp.bfloat16),
                pltpu.VMEM((2, 6, BS, BS), jnp.bfloat16),
                pltpu.VMEM((8, 4, BS, BS), jnp.bfloat16),
                pltpu.VMEM((2, BS, BS), jnp.bfloat16),
                pltpu.VMEM((3 * rows, BS), jnp.bfloat16),
                pltpu.VMEM((rows, BS), jnp.bfloat16),
                pltpu.VMEM((n_aux, share, BS), jnp.bfloat16),
                pltpu.VMEM((n_aux, share, BS), jnp.bfloat16),
                pltpu.VMEM((n_aux, 1, BS), jnp.float32),
                pltpu.VMEM((n_aux, 1, BS), jnp.float32),
                pltpu.VMEM((1, BS), jnp.float32),
                pltpu.VMEM((n_blk, 1, BS), jnp.float32),
                pltpu.SemaphoreType.DMA((5,)),
                pltpu.SemaphoreType.DMA((4,)),
                pltpu.SemaphoreType.DMA((4,)),
                pltpu.SemaphoreType.DMA((5,)),
                pltpu.SemaphoreType.DMA((5,)),
                pltpu.SemaphoreType.REGULAR((steps,)),
                pltpu.SemaphoreType.DMA((2, TEAM - 1)),
                pltpu.SemaphoreType.DMA((2, TEAM - 1)),
            ],
            compiler_params=pltpu.CompilerParams(
                collective_id=0,
                has_side_effects=True,
                vmem_limit_bytes=56550000,
            ),
        )(
            intersection,
            counts,
            tensor.reshape(rows, BS),
            d_occ,
            d_virt,
        )

    return jax.shard_map(
        on_device,
        mesh=mesh,
        in_specs=(
            P("aux", "blk", None, None, None),
            P("blk", None),
            P(),
            P("blk", None, None, None),
            P("blk", None, None, None),
        ),
        out_specs=P("aux", None),
        check_vma=False,
    )
```

```python
import functools

import jax
import jax.numpy as jnp
from jax import lax
from jax.experimental import pallas as pl
from jax.experimental.pallas import tpu as pltpu
from jax.sharding import PartitionSpec as P

MESH = pl.DeviceIdType.MESH
BS = 128
PACK = 16
TEAM = 2
TRANSPOSED = (((1,), (1,)), ((), ()))


def kernel(
    n_blk,
    n_aux,
    inter_hbm,
    counts_hbm,
    tensor_ref,
    docc_ref,
    dvirt_ref,
    out_ref,
    inter_ref,
    counts_ref,
    raw,
    omat,
    dmat,
    corner,
    ball,
    w_own,
    all_b,
    all_w,
    row_out,
    row_in,
    sum_out,
    sum_in,
    load_sem,
    rim_send,
    rim_recv,
    a2a_send,
    a2a_recv,
    known,
    hand_send,
    hand_recv,
):
    b = lax.axis_index("blk")
    q = lax.axis_index("aux")
    seat = q & (TEAM - 1)
    nblocks = counts_ref.shape[0]
    rows = raw.shape[0]
    half = n_aux // 2
    place = q & (half - 1)
    share = rows // half
    z = b & (n_blk // 2 - 1)
    wraps = (z == 0) | (z == n_blk // 2 - 1)
    left = (b - 1) & (n_blk - 1)
    right = (b + 1) & (n_blk - 1)
    own = ball.at[pl.ds(rows, rows)]

    barrier = pltpu.get_barrier_semaphore()

    def greet(axis, there):
        pl.semaphore_signal(barrier, inc=1, device_id={axis: there}, device_id_type=MESH)

    loads = [
        pltpu.make_async_copy(tensor_ref, raw, load_sem.at[0]),
        pltpu.make_async_copy(inter_hbm, inter_ref, load_sem.at[3]),
        pltpu.make_async_copy(counts_hbm, counts_ref, load_sem.at[4]),
    ]
    for load in loads:
        load.start()

    greet("blk", right)
    greet("blk", left)
    for i in range(1, n_aux):
        greet("aux", q ^ i)

    prepare = [
        pltpu.make_async_copy(dvirt_ref.at[0, pl.ds(1, 4)], dmat.at[3], load_sem.at[1]),
        pltpu.make_async_copy(dvirt_ref.at[1, pl.ds(0, 4)], dmat.at[4], load_sem.at[1]),
        pltpu.make_async_copy(dvirt_ref.at[0, 0], corner.at[0], load_sem.at[1]),
        pltpu.make_async_copy(dvirt_ref.at[1, 4], corner.at[1], load_sem.at[1]),
        pltpu.make_async_copy(docc_ref.at[0], omat.at[0, pl.ds(0, 5)], load_sem.at[2]),
        pltpu.make_async_copy(docc_ref.at[1], omat.at[1, pl.ds(1, 5)], load_sem.at[2]),
    ]
    for load in prepare:
        load.start()

    for load in loads:
        load.wait()
    row_ids = lax.broadcasted_iota(jnp.int32, (BS, BS), 0)
    col_ids = lax.broadcasted_iota(jnp.int32, (BS, BS), 1)

    for m in range(2):
        row = 2 * b + m
        own_count = counts_ref[row]
        for w in range(3):
            col_count = counts_ref[lax.rem(row + w - 1 + nblocks, nblocks)]
            if w != 1:
                col_count = col_count * inter_ref[m, w // 2]
            keep = (row_ids < own_count) & (col_ids < col_count)
            at = pl.ds((m * 3 + w) * BS, BS)
            block = jnp.where(keep, raw[at, :].astype(jnp.float32), 0.0)
            own[at, :] = block.astype(jnp.bfloat16)

    pltpu.make_async_copy(dvirt_ref, dvirt_ref, load_sem.at[1]).wait()

    def turn(block):
        return block[...].astype(jnp.float32).T.astype(jnp.bfloat16)

    dmat[5, 1] = turn(dmat.at[3, 3])
    dmat[2, 2] = turn(dmat.at[4, 0])
    pl.semaphore_wait(barrier, 2 + n_aux - 1)

    def tell(step):
        if step < known.shape[0]:
            for there in (b + 2**step, b - 2**step):
                pl.semaphore_signal(
                    known.at[step],
                    inc=1,
                    device_id={"blk": there & (n_blk - 1)},
                    device_id_type=MESH,
                )

    def learn(step):
        if step < known.shape[0]:
            pl.semaphore_wait(known.at[step], 2)

    def to_blk(src, dst, sem, there):
        return pltpu.make_async_remote_copy(
            src_ref=src,
            dst_ref=dst,
            send_sem=rim_send.at[sem],
            recv_sem=rim_recv.at[sem],
            device_id={"blk": there},
            device_id_type=MESH,
        )

    def band(r, c):
        strip = BS // TEAM
        return dmat.at[pl.ds(r, 3), c, pl.ds(pl.multiple_of(seat * strip, PACK), strip)]

    rims = [
        to_blk(band(2, 2), band(0, 0), 0, right),
        to_blk(band(3, 1), band(5, 3), 1, left),
        to_blk(own, ball.at[pl.ds(0, rows)], 2, right),
        to_blk(own, ball.at[pl.ds(2 * rows, rows)], 3, left),
    ]
    for rim in rims:
        rim.start()
    tell(0)

    def scatter(src, first, dst, slot, sem, partners):
        for i in partners:
            there = q ^ i
            at = pl.multiple_of(first + (there & (half - 1)) * share, PACK)
            pltpu.make_async_remote_copy(
                src_ref=src.at[pl.ds(at, share)],
                dst_ref=dst.at[slot],
                send_sem=a2a_send.at[sem],
                recv_sem=a2a_recv.at[sem],
                device_id={"aux": there},
                device_id_type=MESH,
            ).start()

    def keep_own(src, first, dst, slot):
        dst[slot] = src[pl.ds(pl.multiple_of(first + place * share, PACK), share), :]

    def scattered(dst, sem):
        others = dst.at[pl.ds(0, dst.shape[0] - 1)]
        pltpu.make_async_copy(others, others, sem).wait()

    def scatter_tensor(partners):
        scatter(ball, rows, all_b, q, 0, partners)

    dmat[1, 1] = turn(corner.at[0])
    dmat[2, 1] = turn(dmat.at[3, 0])
    dmat[5, 2] = turn(dmat.at[4, 3])
    dmat[6, 2] = turn(corner.at[1])
    zero = jnp.zeros((BS, BS), jnp.bfloat16)
    for c in range(4):
        for r in range(8):
            if not 0 <= r - c <= 4:
                dmat[r, c] = zero
    for m in range(2):
        omat[m, 5 - 5 * m] = zero

    learn(0)
    tell(1)

    pltpu.make_async_copy(docc_ref, docc_ref, load_sem.at[2]).wait()
    handed = []
    for side, rim in enumerate((band(0, 0), band(5, 3))):
        rims[side].wait_recv()
        for i in range(1, TEAM):
            handed.append(
                pltpu.make_async_remote_copy(
                    src_ref=rim,
                    dst_ref=rim,
                    send_sem=hand_send.at[side, i - 1],
                    recv_sem=hand_recv.at[side, i - 1],
                    device_id={"aux": q ^ i},
                    device_id_type=MESH,
                )
            )
            handed[-1].start()
    scatter_tensor(range(1, half))
    pl.when(jnp.logical_not(wraps))(lambda: scatter_tensor(range(half, n_aux)))
    keep_own(ball, rows, all_b, q)
    learn(1)
    tell(2)
    for copy in handed:
        copy.wait_recv()

    def grid(blocks):
        return jnp.concatenate([jnp.concatenate(row, axis=1) for row in blocks], axis=0)

    def part(pair):
        blocks = [ball[pl.ds((6 * pair + i) * BS, BS), :] for i in range(6)]
        b_pair = grid([blocks[:3] + [zero], [zero] + blocks[3:]])
        d_pair = grid([[dmat[2 * pair + r, c] for c in range(4)] for r in range(4)])
        x_pair = jnp.dot(b_pair, d_pair, preferred_element_type=jnp.float32)
        return jnp.dot(
            grid([[omat[m, 2 * pair + n] for n in range(2)] for m in range(2)]),
            x_pair.astype(jnp.bfloat16),
            preferred_element_type=jnp.float32,
        )

    total = part(1)
    rims[2].wait_recv()
    total = total + part(0)
    rims[3].wait_recv()
    pl.when(wraps)(lambda: scatter_tensor(range(half, n_aux)))
    learn(2)
    tell(3)
    total = total + part(2)
    total = total.astype(jnp.bfloat16)
    for m in range(2):
        for w in range(3):
            w_own[pl.ds((m * 3 + w) * BS, BS), :] = total[
                m * BS : (m + 1) * BS, (m + w) * BS : (m + w + 1) * BS
            ]

    scatter(w_own, 0, all_w, place, 1, range(1, half))
    keep_own(w_own, 0, all_w, place)
    groups = range(share // PACK)
    size = n_aux * PACK

    def flat(ref):
        return jnp.concatenate(
            [ref[:, pl.ds(g * PACK, PACK), :].reshape(ref.shape[0] * PACK, BS) for g in groups],
            axis=1,
        )

    fold = (
        lax.broadcasted_iota(jnp.int32, (size, BS), 0) // PACK
        == lax.broadcasted_iota(jnp.int32, (size, BS), 1)
    ).astype(jnp.bfloat16)
    scattered(all_b, a2a_recv.at[0])
    scattered(all_w, a2a_recv.at[1])
    gram = lax.dot_general(
        flat(all_w), flat(all_b), TRANSPOSED, preferred_element_type=jnp.float32
    )
    same = (lax.broadcasted_iota(jnp.int32, gram.shape, 0) & (PACK - 1)) == (
        lax.broadcasted_iota(jnp.int32, gram.shape, 1) & (PACK - 1)
    )
    gram = jnp.sum(jnp.where(same, gram, 0.0).reshape(half, PACK, size), axis=1)
    terms = []
    for _ in range(3):
        terms.append(gram.astype(jnp.bfloat16))
        gram = gram - terms[-1].astype(jnp.float32)
    terms = [
        jnp.dot(term, fold, preferred_element_type=jnp.float32) for term in reversed(terms)
    ]
    gram = terms[0] + terms[1] + terms[2]
    for p in range(half):
        row_out[p] = gram[p : p + 1, :]
    for i in range(1, half):
        pltpu.make_async_remote_copy(
            src_ref=row_out.at[place ^ i],
            dst_ref=row_in.at[place],
            send_sem=a2a_send.at[2],
            recv_sem=a2a_recv.at[2],
            device_id={"aux": q ^ i},
            device_id_type=MESH,
        ).start()
    row_in[place] = row_out[place]
    scattered(row_in, a2a_recv.at[2])
    sum_out[...] = jnp.sum(row_in[...], axis=0)
    learn(3)

    for i in range(n_blk - 1, 0, -1):
        pltpu.make_async_remote_copy(
            src_ref=sum_out,
            dst_ref=sum_in.at[b],
            send_sem=a2a_send.at[3],
            recv_sem=a2a_recv.at[3],
            device_id={"blk": b ^ i},
            device_id_type=MESH,
        ).start()
    sum_in[b] = sum_out[...]
    pltpu.make_async_copy(
        sum_in.at[pl.ds(0, n_blk - 1)], sum_in.at[pl.ds(0, n_blk - 1)], a2a_recv.at[3]
    ).wait()
    out_ref[...] = jnp.sum(sum_in[...], axis=0)[:, : out_ref.shape[1]]

    for copy in rims + handed:
        copy.wait_send()
    scattered(all_b, a2a_send.at[0])
    scattered(all_w, a2a_send.at[1])
    scattered(row_in, a2a_send.at[2])
    pltpu.make_async_copy(
        sum_in.at[pl.ds(0, n_blk - 1)], sum_in.at[pl.ds(0, n_blk - 1)], a2a_send.at[3]
    ).wait()


def solution(mesh):
    n_blk, n_aux = mesh.shape["blk"], mesh.shape["aux"]
    rows = 2 * 3 * BS
    half = n_aux // 2
    share = rows // half
    steps = n_blk.bit_length() - 2
    hbm = pl.BlockSpec(memory_space=pltpu.HBM)

    def on_device(tensor, intersection, counts, d_occ, d_virt):
        return pl.pallas_call(
            functools.partial(kernel, n_blk, n_aux),
            out_shape=jax.ShapeDtypeStruct((1, n_aux), jnp.float32),
            in_specs=[hbm] * 5,
            out_specs=pl.BlockSpec(memory_space=pltpu.VMEM),
            scratch_shapes=[
                pltpu.SMEM(intersection.shape, jnp.int32),
                pltpu.SMEM(counts.shape, jnp.int32),
                pltpu.VMEM((rows, BS), jnp.bfloat16),
                pltpu.VMEM((2, 6, BS, BS), jnp.bfloat16),
                pltpu.VMEM((8, 4, BS, BS), jnp.bfloat16),
                pltpu.VMEM((2, BS, BS), jnp.bfloat16),
                pltpu.VMEM((3 * rows, BS), jnp.bfloat16),
                pltpu.VMEM((rows, BS), jnp.bfloat16),
                pltpu.VMEM((n_aux, share, BS), jnp.bfloat16),
                pltpu.VMEM((half, share, BS), jnp.bfloat16),
                pltpu.VMEM((half, 1, BS), jnp.float32),
                pltpu.VMEM((half, 1, BS), jnp.float32),
                pltpu.VMEM((1, BS), jnp.float32),
                pltpu.VMEM((n_blk, 1, BS), jnp.float32),
                pltpu.SemaphoreType.DMA((5,)),
                pltpu.SemaphoreType.DMA((4,)),
                pltpu.SemaphoreType.DMA((4,)),
                pltpu.SemaphoreType.DMA((5,)),
                pltpu.SemaphoreType.DMA((5,)),
                pltpu.SemaphoreType.REGULAR((steps,)),
                pltpu.SemaphoreType.DMA((2, TEAM - 1)),
                pltpu.SemaphoreType.DMA((2, TEAM - 1)),
            ],
            compiler_params=pltpu.CompilerParams(
                collective_id=0,
                has_side_effects=True,
                vmem_limit_bytes=56550000,
            ),
        )(
            intersection,
            counts,
            tensor.reshape(rows, BS),
            d_occ,
            d_virt,
        )

    return jax.shard_map(
        on_device,
        mesh=mesh,
        in_specs=(
            P("aux", "blk", None, None, None),
            P("blk", None),
            P(),
            P("blk", None, None, None),
            P("blk", None, None, None),
        ),
        out_specs=P("aux", None),
        check_vma=False,
    )
```

```python
import functools

import jax
import jax.numpy as jnp
from jax import lax
from jax.experimental import pallas as pl
from jax.experimental.pallas import tpu as pltpu
from jax.sharding import PartitionSpec as P

MESH = pl.DeviceIdType.MESH
BS = 128
PACK = 16
TEAM = 2
TRANSPOSED = (((1,), (1,)), ((), ()))


def kernel(
    n_blk,
    n_aux,
    inter_hbm,
    counts_hbm,
    tensor_ref,
    docc_ref,
    dvirt_ref,
    out_ref,
    inter_ref,
    counts_ref,
    raw,
    omat,
    dmat,
    corner,
    ball,
    relay,
    w_own,
    all_b,
    all_w,
    row_out,
    row_in,
    sum_out,
    sum_in,
    load_sem,
    rim_send,
    rim_recv,
    a2a_send,
    a2a_recv,
    known,
    hand_send,
    hand_recv,
    relay_send,
    relay_recv,
):
    b = lax.axis_index("blk")
    q = lax.axis_index("aux")
    seat = q & (TEAM - 1)
    nblocks = counts_ref.shape[0]
    rows = raw.shape[0]
    half = n_aux // 2
    place = q & (half - 1)
    share = rows // half
    z = b & (n_blk // 2 - 1)
    wraps = (z == 0) | (z == n_blk // 2 - 1)
    left = (b - 1) & (n_blk - 1)
    right = (b + 1) & (n_blk - 1)
    own = ball.at[pl.ds(rows, rows)]

    n_z = n_blk // 2
    top = z == n_z - 1
    across = q ^ half
    far_side = jnp.where(top, right, left)
    between = [{"aux": across}, {"blk": b ^ n_z, "aux": across}]
    beyond = [{"blk": far_side, "aux": across}, {"blk": far_side ^ n_z, "aux": across}]

    barrier = pltpu.get_barrier_semaphore()

    def greet(axis, there):
        pl.semaphore_signal(barrier, inc=1, device_id={axis: there}, device_id_type=MESH)

    loads = [
        pltpu.make_async_copy(tensor_ref, raw, load_sem.at[0]),
        pltpu.make_async_copy(inter_hbm, inter_ref, load_sem.at[3]),
        pltpu.make_async_copy(counts_hbm, counts_ref, load_sem.at[4]),
    ]
    for load in loads:
        load.start()

    greet("blk", right)
    greet("blk", left)
    for i in range(1, n_aux):
        greet("aux", q ^ i)

    @pl.when(wraps)
    def _():
        for there in [between[1]] + beyond:
            pl.semaphore_signal(barrier, inc=1, device_id=there, device_id_type=MESH)


    prepare = [
        pltpu.make_async_copy(dvirt_ref.at[0, pl.ds(1, 4)], dmat.at[3], load_sem.at[1]),
        pltpu.make_async_copy(dvirt_ref.at[1, pl.ds(0, 4)], dmat.at[4], load_sem.at[1]),
        pltpu.make_async_copy(dvirt_ref.at[0, 0], corner.at[0], load_sem.at[1]),
        pltpu.make_async_copy(dvirt_ref.at[1, 4], corner.at[1], load_sem.at[1]),
        pltpu.make_async_copy(docc_ref.at[0], omat.at[0, pl.ds(0, 5)], load_sem.at[2]),
        pltpu.make_async_copy(docc_ref.at[1], omat.at[1, pl.ds(1, 5)], load_sem.at[2]),
    ]
    for load in prepare:
        load.start()

    for load in loads:
        load.wait()
    row_ids = lax.broadcasted_iota(jnp.int32, (BS, BS), 0)
    col_ids = lax.broadcasted_iota(jnp.int32, (BS, BS), 1)

    for m in range(2):
        row = 2 * b + m
        own_count = counts_ref[row]
        for w in range(3):
            col_count = counts_ref[lax.rem(row + w - 1 + nblocks, nblocks)]
            if w != 1:
                col_count = col_count * inter_ref[m, w // 2]
            keep = (row_ids < own_count) & (col_ids < col_count)
            at = pl.ds((m * 3 + w) * BS, BS)
            block = jnp.where(keep, raw[at, :].astype(jnp.float32), 0.0)
            own[at, :] = block.astype(jnp.bfloat16)

    pltpu.make_async_copy(dvirt_ref, dvirt_ref, load_sem.at[1]).wait()

    def turn(block):
        return block[...].astype(jnp.float32).T.astype(jnp.bfloat16)

    dmat[5, 1] = turn(dmat.at[3, 3])
    dmat[2, 2] = turn(dmat.at[4, 0])
    pl.semaphore_wait(barrier, 2 + n_aux - 1 + jnp.where(wraps, 3, 0))

    def tell(step):
        if step < known.shape[0]:
            for there in (b + 2**step, b - 2**step):
                pl.semaphore_signal(
                    known.at[step],
                    inc=1,
                    device_id={"blk": there & (n_blk - 1)},
                    device_id_type=MESH,
                )

    def learn(step):
        if step < known.shape[0]:
            pl.semaphore_wait(known.at[step], 2)

    def to_blk(src, dst, sem, there):
        return pltpu.make_async_remote_copy(
            src_ref=src,
            dst_ref=dst,
            send_sem=rim_send.at[sem],
            recv_sem=rim_recv.at[sem],
            device_id={"blk": there},
            device_id_type=MESH,
        )

    def band(r, c):
        strip = BS // TEAM
        return dmat.at[pl.ds(r, 3), c, pl.ds(pl.multiple_of(seat * strip, PACK), strip)]

    rims = [
        to_blk(band(2, 2), band(0, 0), 0, right),
        to_blk(band(3, 1), band(5, 3), 1, left),
        to_blk(own, ball.at[pl.ds(0, rows)], 2, right),
        to_blk(own, ball.at[pl.ds(2 * rows, rows)], 3, left),
    ]
    rims[0].start()
    rims[1].start()
    pl.when(jnp.logical_not(top))(rims[2].start)
    pl.when(z != 0)(rims[3].start)
    part_rows = rows // 2

    def pass_on(src, dst, send, recv, there):
        pltpu.make_async_remote_copy(
            src_ref=src,
            dst_ref=dst,
            send_sem=send,
            recv_sem=recv,
            device_id=there,
            device_id_type=MESH,
        ).start()

    def outward(side):
        for k in range(2):
            pass_on(
                own.at[pl.ds(k * part_rows, part_rows)],
                relay.at[k],
                rim_send.at[side],
                relay_recv.at[k],
                between[k],
            )

    def onward(side):
        for k in range(2):
            pltpu.make_async_copy(relay.at[k], relay.at[k], relay_recv.at[k]).wait()
            pass_on(
                relay.at[k],
                ball.at[pl.ds((side - 2) * 2 * rows + k * part_rows, part_rows)],
                relay_send,
                rim_recv.at[side],
                beyond[k],
            )

    pl.when(top)(functools.partial(outward, 2))
    pl.when(z == 0)(functools.partial(outward, 3))
    tell(0)

    def scatter(src, first, dst, slot, sem, partners):
        for i in partners:
            there = q ^ i
            at = pl.multiple_of(first + (there & (half - 1)) * share, PACK)
            pltpu.make_async_remote_copy(
                src_ref=src.at[pl.ds(at, share)],
                dst_ref=dst.at[slot],
                send_sem=a2a_send.at[sem],
                recv_sem=a2a_recv.at[sem],
                device_id={"aux": there},
                device_id_type=MESH,
            ).start()

    def keep_own(src, first, dst, slot):
        dst[slot] = src[pl.ds(pl.multiple_of(first + place * share, PACK), share), :]

    def scattered(dst, sem):
        others = dst.at[pl.ds(0, dst.shape[0] - 1)]
        pltpu.make_async_copy(others, others, sem).wait()

    def scatter_tensor(partners):
        scatter(ball, rows, all_b, q, 0, partners)

    dmat[1, 1] = turn(corner.at[0])
    dmat[2, 1] = turn(dmat.at[3, 0])
    dmat[5, 2] = turn(dmat.at[4, 3])
    dmat[6, 2] = turn(corner.at[1])
    zero = jnp.zeros((BS, BS), jnp.bfloat16)
    for c in range(4):
        for r in range(8):
            if not 0 <= r - c <= 4:
                dmat[r, c] = zero
    for m in range(2):
        omat[m, 5 - 5 * m] = zero

    learn(0)
    tell(1)

    pltpu.make_async_copy(docc_ref, docc_ref, load_sem.at[2]).wait()
    handed = []
    for side, rim in enumerate((band(0, 0), band(5, 3))):
        rims[side].wait_recv()
        for i in range(1, TEAM):
            handed.append(
                pltpu.make_async_remote_copy(
                    src_ref=rim,
                    dst_ref=rim,
                    send_sem=hand_send.at[side, i - 1],
                    recv_sem=hand_recv.at[side, i - 1],
                    device_id={"aux": q ^ i},
                    device_id_type=MESH,
                )
            )
            handed[-1].start()
    scatter_tensor(range(1, half))
    pl.when(jnp.logical_not(wraps))(lambda: scatter_tensor(range(half, n_aux)))
    keep_own(ball, rows, all_b, q)
    pl.when(top)(functools.partial(onward, 2))
    pl.when(z == 0)(functools.partial(onward, 3))
    learn(1)
    tell(2)
    for copy in handed:
        copy.wait_recv()

    def grid(blocks):
        return jnp.concatenate([jnp.concatenate(row, axis=1) for row in blocks], axis=0)

    def part(pair):
        blocks = [ball[pl.ds((6 * pair + i) * BS, BS), :] for i in range(6)]
        b_pair = grid([blocks[:3] + [zero], [zero] + blocks[3:]])
        d_pair = grid([[dmat[2 * pair + r, c] for c in range(4)] for r in range(4)])
        x_pair = jnp.dot(b_pair, d_pair, preferred_element_type=jnp.float32)
        return jnp.dot(
            grid([[omat[m, 2 * pair + n] for n in range(2)] for m in range(2)]),
            x_pair.astype(jnp.bfloat16),
            preferred_element_type=jnp.float32,
        )

    total = part(1)
    rims[2].wait_recv()
    total = total + part(0)
    rims[3].wait_recv()
    pl.when(wraps)(lambda: scatter_tensor(range(half, n_aux)))
    learn(2)
    tell(3)
    total = total + part(2)
    total = total.astype(jnp.bfloat16)
    for m in range(2):
        for w in range(3):
            w_own[pl.ds((m * 3 + w) * BS, BS), :] = total[
                m * BS : (m + 1) * BS, (m + w) * BS : (m + w + 1) * BS
            ]

    scatter(w_own, 0, all_w, place, 1, range(1, half))
    keep_own(w_own, 0, all_w, place)
    groups = range(share // PACK)
    size = n_aux * PACK

    def flat(ref):
        return jnp.concatenate(
            [ref[:, pl.ds(g * PACK, PACK), :].reshape(ref.shape[0] * PACK, BS) for g in groups],
            axis=1,
        )

    fold = (
        lax.broadcasted_iota(jnp.int32, (size, BS), 0) // PACK
        == lax.broadcasted_iota(jnp.int32, (size, BS), 1)
    ).astype(jnp.bfloat16)
    scattered(all_b, a2a_recv.at[0])
    scattered(all_w, a2a_recv.at[1])
    gram = lax.dot_general(
        flat(all_w), flat(all_b), TRANSPOSED, preferred_element_type=jnp.float32
    )
    same = (lax.broadcasted_iota(jnp.int32, gram.shape, 0) & (PACK - 1)) == (
        lax.broadcasted_iota(jnp.int32, gram.shape, 1) & (PACK - 1)
    )
    gram = jnp.sum(jnp.where(same, gram, 0.0).reshape(half, PACK, size), axis=1)
    terms = []
    for _ in range(3):
        terms.append(gram.astype(jnp.bfloat16))
        gram = gram - terms[-1].astype(jnp.float32)
    terms = [
        jnp.dot(term, fold, preferred_element_type=jnp.float32) for term in reversed(terms)
    ]
    gram = terms[0] + terms[1] + terms[2]
    for p in range(half):
        row_out[p] = gram[p : p + 1, :]
    for i in range(1, half):
        pltpu.make_async_remote_copy(
            src_ref=row_out.at[place ^ i],
            dst_ref=row_in.at[place],
            send_sem=a2a_send.at[2],
            recv_sem=a2a_recv.at[2],
            device_id={"aux": q ^ i},
            device_id_type=MESH,
        ).start()
    row_in[place] = row_out[place]
    scattered(row_in, a2a_recv.at[2])
    sum_out[...] = jnp.sum(row_in[...], axis=0)
    learn(3)

    for i in range(n_blk - 1, 0, -1):
        pltpu.make_async_remote_copy(
            src_ref=sum_out,
            dst_ref=sum_in.at[b],
            send_sem=a2a_send.at[3],
            recv_sem=a2a_recv.at[3],
            device_id={"blk": b ^ i},
            device_id_type=MESH,
        ).start()
    sum_in[b] = sum_out[...]
    pltpu.make_async_copy(
        sum_in.at[pl.ds(0, n_blk - 1)], sum_in.at[pl.ds(0, n_blk - 1)], a2a_recv.at[3]
    ).wait()
    out_ref[...] = jnp.sum(sum_in[...], axis=0)[:, : out_ref.shape[1]]

    for copy in rims + handed:
        copy.wait_send()

    @pl.when(wraps)
    def _():
        pltpu.make_async_copy(relay, relay, relay_send).wait()

    scattered(all_b, a2a_send.at[0])
    scattered(all_w, a2a_send.at[1])
    scattered(row_in, a2a_send.at[2])
    pltpu.make_async_copy(
        sum_in.at[pl.ds(0, n_blk - 1)], sum_in.at[pl.ds(0, n_blk - 1)], a2a_send.at[3]
    ).wait()


def solution(mesh):
    n_blk, n_aux = mesh.shape["blk"], mesh.shape["aux"]
    rows = 2 * 3 * BS
    half = n_aux // 2
    share = rows // half
    steps = n_blk.bit_length() - 2
    hbm = pl.BlockSpec(memory_space=pltpu.HBM)

    def on_device(tensor, intersection, counts, d_occ, d_virt):
        return pl.pallas_call(
            functools.partial(kernel, n_blk, n_aux),
            out_shape=jax.ShapeDtypeStruct((1, n_aux), jnp.float32),
            in_specs=[hbm] * 5,
            out_specs=pl.BlockSpec(memory_space=pltpu.VMEM),
            scratch_shapes=[
                pltpu.SMEM(intersection.shape, jnp.int32),
                pltpu.SMEM(counts.shape, jnp.int32),
                pltpu.VMEM((rows, BS), jnp.bfloat16),
                pltpu.VMEM((2, 6, BS, BS), jnp.bfloat16),
                pltpu.VMEM((8, 4, BS, BS), jnp.bfloat16),
                pltpu.VMEM((2, BS, BS), jnp.bfloat16),
                pltpu.VMEM((3 * rows, BS), jnp.bfloat16),
                pltpu.VMEM((2, rows // 2, BS), jnp.bfloat16),
                pltpu.VMEM((rows, BS), jnp.bfloat16),
                pltpu.VMEM((n_aux, share, BS), jnp.bfloat16),
                pltpu.VMEM((half, share, BS), jnp.bfloat16),
                pltpu.VMEM((half, 1, BS), jnp.float32),
                pltpu.VMEM((half, 1, BS), jnp.float32),
                pltpu.VMEM((1, BS), jnp.float32),
                pltpu.VMEM((n_blk, 1, BS), jnp.float32),
                pltpu.SemaphoreType.DMA((5,)),
                pltpu.SemaphoreType.DMA((4,)),
                pltpu.SemaphoreType.DMA((4,)),
                pltpu.SemaphoreType.DMA((5,)),
                pltpu.SemaphoreType.DMA((5,)),
                pltpu.SemaphoreType.REGULAR((steps,)),
                pltpu.SemaphoreType.DMA((2, TEAM - 1)),
                pltpu.SemaphoreType.DMA((2, TEAM - 1)),
                pltpu.SemaphoreType.DMA,
                pltpu.SemaphoreType.DMA((2,)),
            ],
            compiler_params=pltpu.CompilerParams(
                collective_id=0,
                has_side_effects=True,
                vmem_limit_bytes=56550000,
            ),
        )(
            intersection,
            counts,
            tensor.reshape(rows, BS),
            d_occ,
            d_virt,
        )

    return jax.shard_map(
        on_device,
        mesh=mesh,
        in_specs=(
            P("aux", "blk", None, None, None),
            P("blk", None),
            P(),
            P("blk", None, None, None),
            P("blk", None, None, None),
        ),
        out_specs=P("aux", None),
        check_vma=False,
    )
```

```python
import functools

import jax
import jax.numpy as jnp
from jax import lax
from jax.experimental import pallas as pl
from jax.experimental.pallas import tpu as pltpu
from jax.sharding import PartitionSpec as P

MESH = pl.DeviceIdType.MESH
BS = 128
PACK = 16
TEAM = 2
TRANSPOSED = (((1,), (1,)), ((), ()))


def kernel(
    n_blk,
    n_aux,
    inter_hbm,
    counts_hbm,
    tensor_ref,
    docc_ref,
    dvirt_ref,
    out_ref,
    inter_ref,
    counts_ref,
    raw,
    omat,
    dmat,
    corner,
    ball,
    w_own,
    all_b,
    all_w,
    row_out,
    row_in,
    sum_out,
    sum_in,
    load_sem,
    rim_send,
    rim_recv,
    a2a_send,
    a2a_recv,
    known,
    hand_send,
    hand_recv,
):
    b = lax.axis_index("blk")
    q = lax.axis_index("aux")
    seat = q & (TEAM - 1)
    nblocks = counts_ref.shape[0]
    rows = raw.shape[0]
    half = n_aux // 2
    place = q & (half - 1)
    share = rows // half
    z = b & (n_blk // 2 - 1)
    wraps = (z == 0) | (z == n_blk // 2 - 1)
    left = (b - 1) & (n_blk - 1)
    right = (b + 1) & (n_blk - 1)
    own = ball.at[pl.ds(rows, rows)]

    barrier = pltpu.get_barrier_semaphore()

    def greet(axis, there):
        pl.semaphore_signal(barrier, inc=1, device_id={axis: there}, device_id_type=MESH)

    loads = [
        pltpu.make_async_copy(tensor_ref, raw, load_sem.at[0]),
        pltpu.make_async_copy(inter_hbm, inter_ref, load_sem.at[3]),
        pltpu.make_async_copy(counts_hbm, counts_ref, load_sem.at[4]),
    ]
    for load in loads:
        load.start()

    greet("blk", right)
    greet("blk", left)
    greet("blk", (b + 2) & (n_blk - 1))
    greet("blk", (b - 2) & (n_blk - 1))
    for i in range(1, n_aux):
        greet("aux", q ^ i)

    prepare = [
        pltpu.make_async_copy(dvirt_ref.at[0, pl.ds(1, 4)], dmat.at[3], load_sem.at[1]),
        pltpu.make_async_copy(dvirt_ref.at[1, pl.ds(0, 4)], dmat.at[4], load_sem.at[1]),
        pltpu.make_async_copy(dvirt_ref.at[0, 0], corner.at[0], load_sem.at[1]),
        pltpu.make_async_copy(dvirt_ref.at[1, 4], corner.at[1], load_sem.at[1]),
        pltpu.make_async_copy(docc_ref.at[0], omat.at[0, pl.ds(0, 5)], load_sem.at[2]),
        pltpu.make_async_copy(docc_ref.at[1], omat.at[1, pl.ds(1, 5)], load_sem.at[2]),
    ]
    for load in prepare:
        load.start()

    for load in loads:
        load.wait()
    row_ids = lax.broadcasted_iota(jnp.int32, (BS, BS), 0)
    col_ids = lax.broadcasted_iota(jnp.int32, (BS, BS), 1)

    for m in range(2):
        row = 2 * b + m
        own_count = counts_ref[row]
        for w in range(3):
            col_count = counts_ref[lax.rem(row + w - 1 + nblocks, nblocks)]
            if w != 1:
                col_count = col_count * inter_ref[m, w // 2]
            keep = (row_ids < own_count) & (col_ids < col_count)
            at = pl.ds((m * 3 + w) * BS, BS)
            block = jnp.where(keep, raw[at, :].astype(jnp.float32), 0.0)
            own[at, :] = block.astype(jnp.bfloat16)

    pltpu.make_async_copy(dvirt_ref, dvirt_ref, load_sem.at[1]).wait()

    def turn(block):
        return block[...].astype(jnp.float32).T.astype(jnp.bfloat16)

    dmat[5, 1] = turn(dmat.at[3, 3])
    dmat[2, 2] = turn(dmat.at[4, 0])
    pl.semaphore_wait(barrier, 4 + n_aux - 1)

    steps = n_blk.bit_length() - 3

    def tell(step):
        if step < steps:
            for there in (b + 2 ** (step + 1), b - 2 ** (step + 1)):
                pl.semaphore_signal(
                    known.at[step],
                    inc=1,
                    device_id={"blk": there & (n_blk - 1)},
                    device_id_type=MESH,
                )

    def learn(step):
        if step < steps:
            pl.semaphore_wait(known.at[step], 2)

    def to_blk(src, dst, sem, there):
        return pltpu.make_async_remote_copy(
            src_ref=src,
            dst_ref=dst,
            send_sem=rim_send.at[sem],
            recv_sem=rim_recv.at[sem],
            device_id={"blk": there},
            device_id_type=MESH,
        )

    def band(r, c):
        strip = BS // TEAM
        return dmat.at[pl.ds(r, 3), c, pl.ds(pl.multiple_of(seat * strip, PACK), strip)]

    rims = [
        to_blk(band(2, 2), band(0, 0), 0, right),
        to_blk(band(3, 1), band(5, 3), 1, left),
        to_blk(own, ball.at[pl.ds(0, rows)], 2, right),
        to_blk(own, ball.at[pl.ds(2 * rows, rows)], 3, left),
    ]
    for rim in rims:
        rim.start()
    tell(0)

    def scatter(src, first, dst, slot, sem, partners):
        for i in partners:
            there = q ^ i
            at = pl.multiple_of(first + (there & (half - 1)) * share, PACK)
            pltpu.make_async_remote_copy(
                src_ref=src.at[pl.ds(at, share)],
                dst_ref=dst.at[slot],
                send_sem=a2a_send.at[sem],
                recv_sem=a2a_recv.at[sem],
                device_id={"aux": there},
                device_id_type=MESH,
            ).start()

    def keep_own(src, first, dst, slot):
        dst[slot] = src[pl.ds(pl.multiple_of(first + place * share, PACK), share), :]

    def scattered(dst, sem):
        others = dst.at[pl.ds(0, dst.shape[0] - 1)]
        pltpu.make_async_copy(others, others, sem).wait()

    def scatter_tensor(partners):
        scatter(ball, rows, all_b, q, 0, partners)

    dmat[1, 1] = turn(corner.at[0])
    dmat[2, 1] = turn(dmat.at[3, 0])
    dmat[5, 2] = turn(dmat.at[4, 3])
    dmat[6, 2] = turn(corner.at[1])
    zero = jnp.zeros((BS, BS), jnp.bfloat16)
    for c in range(4):
        for r in range(8):
            if not 0 <= r - c <= 4:
                dmat[r, c] = zero
    for m in range(2):
        omat[m, 5 - 5 * m] = zero


    pltpu.make_async_copy(docc_ref, docc_ref, load_sem.at[2]).wait()
    handed = []
    for side, rim in enumerate((band(0, 0), band(5, 3))):
        rims[side].wait_recv()
        for i in range(1, TEAM):
            handed.append(
                pltpu.make_async_remote_copy(
                    src_ref=rim,
                    dst_ref=rim,
                    send_sem=hand_send.at[side, i - 1],
                    recv_sem=hand_recv.at[side, i - 1],
                    device_id={"aux": q ^ i},
                    device_id_type=MESH,
                )
            )
            handed[-1].start()
    scatter_tensor(range(1, half))
    pl.when(jnp.logical_not(wraps))(lambda: scatter_tensor(range(half, n_aux)))
    keep_own(ball, rows, all_b, q)
    learn(0)
    tell(1)
    for copy in handed:
        copy.wait_recv()

    def grid(blocks):
        return jnp.concatenate([jnp.concatenate(row, axis=1) for row in blocks], axis=0)

    def part(pair):
        blocks = [ball[pl.ds((6 * pair + i) * BS, BS), :] for i in range(6)]
        b_pair = grid([blocks[:3] + [zero], [zero] + blocks[3:]])
        d_pair = grid([[dmat[2 * pair + r, c] for c in range(4)] for r in range(4)])
        x_pair = jnp.dot(b_pair, d_pair, preferred_element_type=jnp.float32)
        return jnp.dot(
            grid([[omat[m, 2 * pair + n] for n in range(2)] for m in range(2)]),
            x_pair.astype(jnp.bfloat16),
            preferred_element_type=jnp.float32,
        )

    total = part(1)
    rims[2].wait_recv()
    total = total + part(0)
    rims[3].wait_recv()
    pl.when(wraps)(lambda: scatter_tensor(range(half, n_aux)))
    total = total + part(2)
    total = total.astype(jnp.bfloat16)
    for m in range(2):
        for w in range(3):
            w_own[pl.ds((m * 3 + w) * BS, BS), :] = total[
                m * BS : (m + 1) * BS, (m + w) * BS : (m + w + 1) * BS
            ]

    scatter(w_own, 0, all_w, place, 1, range(1, half))
    keep_own(w_own, 0, all_w, place)
    learn(1)
    tell(2)
    groups = range(share // PACK)
    size = n_aux * PACK

    def flat(ref):
        return jnp.concatenate(
            [ref[:, pl.ds(g * PACK, PACK), :].reshape(ref.shape[0] * PACK, BS) for g in groups],
            axis=1,
        )

    fold = (
        lax.broadcasted_iota(jnp.int32, (size, BS), 0) // PACK
        == lax.broadcasted_iota(jnp.int32, (size, BS), 1)
    ).astype(jnp.bfloat16)
    scattered(all_b, a2a_recv.at[0])
    scattered(all_w, a2a_recv.at[1])
    gram = lax.dot_general(
        flat(all_w), flat(all_b), TRANSPOSED, preferred_element_type=jnp.float32
    )
    same = (lax.broadcasted_iota(jnp.int32, gram.shape, 0) & (PACK - 1)) == (
        lax.broadcasted_iota(jnp.int32, gram.shape, 1) & (PACK - 1)
    )
    gram = jnp.sum(jnp.where(same, gram, 0.0).reshape(half, PACK, size), axis=1)
    terms = []
    for _ in range(3):
        terms.append(gram.astype(jnp.bfloat16))
        gram = gram - terms[-1].astype(jnp.float32)
    terms = [
        jnp.dot(term, fold, preferred_element_type=jnp.float32) for term in reversed(terms)
    ]
    gram = terms[0] + terms[1] + terms[2]
    for p in range(half):
        row_out[p] = gram[p : p + 1, :]
    for i in range(1, half):
        pltpu.make_async_remote_copy(
            src_ref=row_out.at[place ^ i],
            dst_ref=row_in.at[place],
            send_sem=a2a_send.at[2],
            recv_sem=a2a_recv.at[2],
            device_id={"aux": q ^ i},
            device_id_type=MESH,
        ).start()
    row_in[place] = row_out[place]
    scattered(row_in, a2a_recv.at[2])
    sum_out[...] = jnp.sum(row_in[...], axis=0)
    learn(2)

    for i in range(n_blk - 1, 0, -1):
        pltpu.make_async_remote_copy(
            src_ref=sum_out,
            dst_ref=sum_in.at[b],
            send_sem=a2a_send.at[3],
            recv_sem=a2a_recv.at[3],
            device_id={"blk": b ^ i},
            device_id_type=MESH,
        ).start()
    sum_in[b] = sum_out[...]
    pltpu.make_async_copy(
        sum_in.at[pl.ds(0, n_blk - 1)], sum_in.at[pl.ds(0, n_blk - 1)], a2a_recv.at[3]
    ).wait()
    out_ref[...] = jnp.sum(sum_in[...], axis=0)[:, : out_ref.shape[1]]

    for copy in rims + handed:
        copy.wait_send()
    scattered(all_b, a2a_send.at[0])
    scattered(all_w, a2a_send.at[1])
    scattered(row_in, a2a_send.at[2])
    pltpu.make_async_copy(
        sum_in.at[pl.ds(0, n_blk - 1)], sum_in.at[pl.ds(0, n_blk - 1)], a2a_send.at[3]
    ).wait()


def solution(mesh):
    n_blk, n_aux = mesh.shape["blk"], mesh.shape["aux"]
    rows = 2 * 3 * BS
    half = n_aux // 2
    share = rows // half
    steps = max(1, n_blk.bit_length() - 3)
    hbm = pl.BlockSpec(memory_space=pltpu.HBM)

    def on_device(tensor, intersection, counts, d_occ, d_virt):
        return pl.pallas_call(
            functools.partial(kernel, n_blk, n_aux),
            out_shape=jax.ShapeDtypeStruct((1, n_aux), jnp.float32),
            in_specs=[hbm] * 5,
            out_specs=pl.BlockSpec(memory_space=pltpu.VMEM),
            scratch_shapes=[
                pltpu.SMEM(intersection.shape, jnp.int32),
                pltpu.SMEM(counts.shape, jnp.int32),
                pltpu.VMEM((rows, BS), jnp.bfloat16),
                pltpu.VMEM((2, 6, BS, BS), jnp.bfloat16),
                pltpu.VMEM((8, 4, BS, BS), jnp.bfloat16),
                pltpu.VMEM((2, BS, BS), jnp.bfloat16),
                pltpu.VMEM((3 * rows, BS), jnp.bfloat16),
                pltpu.VMEM((rows, BS), jnp.bfloat16),
                pltpu.VMEM((n_aux, share, BS), jnp.bfloat16),
                pltpu.VMEM((half, share, BS), jnp.bfloat16),
                pltpu.VMEM((half, 1, BS), jnp.float32),
                pltpu.VMEM((half, 1, BS), jnp.float32),
                pltpu.VMEM((1, BS), jnp.float32),
                pltpu.VMEM((n_blk, 1, BS), jnp.float32),
                pltpu.SemaphoreType.DMA((5,)),
                pltpu.SemaphoreType.DMA((4,)),
                pltpu.SemaphoreType.DMA((4,)),
                pltpu.SemaphoreType.DMA((5,)),
                pltpu.SemaphoreType.DMA((5,)),
                pltpu.SemaphoreType.REGULAR((steps,)),
                pltpu.SemaphoreType.DMA((2, TEAM - 1)),
                pltpu.SemaphoreType.DMA((2, TEAM - 1)),
            ],
            compiler_params=pltpu.CompilerParams(
                collective_id=0,
                has_side_effects=True,
                vmem_limit_bytes=56550000,
            ),
        )(
            intersection,
            counts,
            tensor.reshape(rows, BS),
            d_occ,
            d_virt,
        )

    return jax.shard_map(
        on_device,
        mesh=mesh,
        in_specs=(
            P("aux", "blk", None, None, None),
            P("blk", None),
            P(),
            P("blk", None, None, None),
            P("blk", None, None, None),
        ),
        out_specs=P("aux", None),
        check_vma=False,
    )
```

```python
import functools

import jax
import jax.numpy as jnp
from jax import lax
from jax.experimental import pallas as pl
from jax.experimental.pallas import tpu as pltpu
from jax.sharding import PartitionSpec as P

MESH = pl.DeviceIdType.MESH
BS = 128
PACK = 16
TEAM = 4
TRANSPOSED = (((1,), (1,)), ((), ()))


def kernel(
    n_blk,
    n_aux,
    inter_hbm,
    counts_hbm,
    tensor_ref,
    docc_ref,
    dvirt_ref,
    out_ref,
    inter_ref,
    counts_ref,
    raw,
    omat,
    dmat,
    corner,
    ball,
    w_own,
    all_b,
    all_w,
    row_out,
    row_in,
    sum_out,
    sum_in,
    load_sem,
    rim_send,
    rim_recv,
    a2a_send,
    a2a_recv,
    known,
    hand_send,
    hand_recv,
):
    b = lax.axis_index("blk")
    q = lax.axis_index("aux")
    seat = q & (TEAM - 1)
    nblocks = counts_ref.shape[0]
    rows = raw.shape[0]
    half = n_aux // 2
    place = q & (half - 1)
    share = rows // half
    z = b & (n_blk // 2 - 1)
    wraps = (z == 0) | (z == n_blk // 2 - 1)
    left = (b - 1) & (n_blk - 1)
    right = (b + 1) & (n_blk - 1)
    own = ball.at[pl.ds(rows, rows)]

    barrier = pltpu.get_barrier_semaphore()

    def greet(axis, there):
        pl.semaphore_signal(barrier, inc=1, device_id={axis: there}, device_id_type=MESH)

    loads = [
        pltpu.make_async_copy(tensor_ref, raw, load_sem.at[0]),
        pltpu.make_async_copy(inter_hbm, inter_ref, load_sem.at[3]),
        pltpu.make_async_copy(counts_hbm, counts_ref, load_sem.at[4]),
    ]
    for load in loads:
        load.start()

    greet("blk", right)
    greet("blk", left)
    greet("blk", (b + 2) & (n_blk - 1))
    greet("blk", (b - 2) & (n_blk - 1))
    for i in range(1, n_aux):
        greet("aux", q ^ i)

    prepare = [
        pltpu.make_async_copy(dvirt_ref.at[0, pl.ds(1, 4)], dmat.at[3], load_sem.at[1]),
        pltpu.make_async_copy(dvirt_ref.at[1, pl.ds(0, 4)], dmat.at[4], load_sem.at[1]),
        pltpu.make_async_copy(dvirt_ref.at[0, 0], corner.at[0], load_sem.at[1]),
        pltpu.make_async_copy(dvirt_ref.at[1, 4], corner.at[1], load_sem.at[1]),
        pltpu.make_async_copy(docc_ref.at[0], omat.at[0, pl.ds(0, 5)], load_sem.at[2]),
        pltpu.make_async_copy(docc_ref.at[1], omat.at[1, pl.ds(1, 5)], load_sem.at[2]),
    ]
    for load in prepare:
        load.start()

    for load in loads:
        load.wait()
    row_ids = lax.broadcasted_iota(jnp.int32, (BS, BS), 0)
    col_ids = lax.broadcasted_iota(jnp.int32, (BS, BS), 1)

    for m in range(2):
        row = 2 * b + m
        own_count = counts_ref[row]
        for w in range(3):
            col_count = counts_ref[lax.rem(row + w - 1 + nblocks, nblocks)]
            if w != 1:
                col_count = col_count * inter_ref[m, w // 2]
            keep = (row_ids < own_count) & (col_ids < col_count)
            at = pl.ds((m * 3 + w) * BS, BS)
            block = jnp.where(keep, raw[at, :].astype(jnp.float32), 0.0)
            own[at, :] = block.astype(jnp.bfloat16)

    pltpu.make_async_copy(dvirt_ref, dvirt_ref, load_sem.at[1]).wait()

    def turn(block):
        return block[...].astype(jnp.float32).T.astype(jnp.bfloat16)

    dmat[5, 1] = turn(dmat.at[3, 3])
    dmat[2, 2] = turn(dmat.at[4, 0])
    pl.semaphore_wait(barrier, 4 + n_aux - 1)

    steps = n_blk.bit_length() - 3

    def tell(step):
        if step < steps:
            for there in (b + 2 ** (step + 1), b - 2 ** (step + 1)):
                pl.semaphore_signal(
                    known.at[step],
                    inc=1,
                    device_id={"blk": there & (n_blk - 1)},
                    device_id_type=MESH,
                )

    def learn(step):
        if step < steps:
            pl.semaphore_wait(known.at[step], 2)

    def to_blk(src, dst, sem, there):
        return pltpu.make_async_remote_copy(
            src_ref=src,
            dst_ref=dst,
            send_sem=rim_send.at[sem],
            recv_sem=rim_recv.at[sem],
            device_id={"blk": there},
            device_id_type=MESH,
        )

    def band(r, c):
        strip = BS // TEAM
        return dmat.at[pl.ds(r, 3), c, pl.ds(pl.multiple_of(seat * strip, PACK), strip)]

    rims = [
        to_blk(band(2, 2), band(0, 0), 0, right),
        to_blk(band(3, 1), band(5, 3), 1, left),
        to_blk(own, ball.at[pl.ds(0, rows)], 2, right),
        to_blk(own, ball.at[pl.ds(2 * rows, rows)], 3, left),
    ]
    for rim in rims:
        rim.start()
    tell(0)

    def scatter(src, first, dst, slot, sem, partners):
        for i in partners:
            there = q ^ i
            at = pl.multiple_of(first + (there & (half - 1)) * share, PACK)
            pltpu.make_async_remote_copy(
                src_ref=src.at[pl.ds(at, share)],
                dst_ref=dst.at[slot],
                send_sem=a2a_send.at[sem],
                recv_sem=a2a_recv.at[sem],
                device_id={"aux": there},
                device_id_type=MESH,
            ).start()

    def keep_own(src, first, dst, slot):
        dst[slot] = src[pl.ds(pl.multiple_of(first + place * share, PACK), share), :]

    def scattered(dst, sem):
        others = dst.at[pl.ds(0, dst.shape[0] - 1)]
        pltpu.make_async_copy(others, others, sem).wait()

    def scatter_tensor(partners):
        scatter(ball, rows, all_b, q, 0, partners)

    dmat[1, 1] = turn(corner.at[0])
    dmat[2, 1] = turn(dmat.at[3, 0])
    dmat[5, 2] = turn(dmat.at[4, 3])
    dmat[6, 2] = turn(corner.at[1])
    zero = jnp.zeros((BS, BS), jnp.bfloat16)
    for c in range(4):
        for r in range(8):
            if not 0 <= r - c <= 4:
                dmat[r, c] = zero
    for m in range(2):
        omat[m, 5 - 5 * m] = zero


    pltpu.make_async_copy(docc_ref, docc_ref, load_sem.at[2]).wait()
    handed = []
    for side, rim in enumerate((band(0, 0), band(5, 3))):
        rims[side].wait_recv()
        for i in range(1, TEAM):
            handed.append(
                pltpu.make_async_remote_copy(
                    src_ref=rim,
                    dst_ref=rim,
                    send_sem=hand_send.at[side, i - 1],
                    recv_sem=hand_recv.at[side, i - 1],
                    device_id={"aux": q ^ i},
                    device_id_type=MESH,
                )
            )
            handed[-1].start()
    scatter_tensor(range(1, half))
    pl.when(jnp.logical_not(wraps))(lambda: scatter_tensor(range(half, n_aux)))
    keep_own(ball, rows, all_b, q)
    learn(0)
    tell(1)
    for copy in handed:
        copy.wait_recv()

    def grid(blocks):
        return jnp.concatenate([jnp.concatenate(row, axis=1) for row in blocks], axis=0)

    def part(pair):
        blocks = [ball[pl.ds((6 * pair + i) * BS, BS), :] for i in range(6)]
        b_pair = grid([blocks[:3] + [zero], [zero] + blocks[3:]])
        d_pair = grid([[dmat[2 * pair + r, c] for c in range(4)] for r in range(4)])
        x_pair = jnp.dot(b_pair, d_pair, preferred_element_type=jnp.float32)
        return x_pair.astype(jnp.bfloat16)

    def pull(places, x_rows):
        o_rows = grid([[omat[m, n] for n in places] for m in range(2)])
        return jnp.dot(o_rows, x_rows, preferred_element_type=jnp.float32)

    total = pull((2, 3), part(1))
    rims[2].wait_recv()
    x_left = part(0)
    rims[3].wait_recv()
    pl.when(wraps)(lambda: scatter_tensor(range(half, n_aux)))
    x_rim = jnp.concatenate([x_left, part(2)], axis=0)
    total = total + pull((0, 1, 4, 5), x_rim)
    total = total.astype(jnp.bfloat16)
    for m in range(2):
        for w in range(3):
            w_own[pl.ds((m * 3 + w) * BS, BS), :] = total[
                m * BS : (m + 1) * BS, (m + w) * BS : (m + w + 1) * BS
            ]

    scatter(w_own, 0, all_w, place, 1, range(1, half))
    keep_own(w_own, 0, all_w, place)
    learn(1)
    tell(2)
    groups = range(share // PACK)
    size = n_aux * PACK

    def flat(ref):
        return jnp.concatenate(
            [ref[:, pl.ds(g * PACK, PACK), :].reshape(ref.shape[0] * PACK, BS) for g in groups],
            axis=1,
        )

    fold = (
        lax.broadcasted_iota(jnp.int32, (size, BS), 0) // PACK
        == lax.broadcasted_iota(jnp.int32, (size, BS), 1)
    ).astype(jnp.bfloat16)
    scattered(all_b, a2a_recv.at[0])
    scattered(all_w, a2a_recv.at[1])
    gram = lax.dot_general(
        flat(all_w), flat(all_b), TRANSPOSED, preferred_element_type=jnp.float32
    )
    same = (lax.broadcasted_iota(jnp.int32, gram.shape, 0) & (PACK - 1)) == (
        lax.broadcasted_iota(jnp.int32, gram.shape, 1) & (PACK - 1)
    )
    gram = jnp.sum(jnp.where(same, gram, 0.0).reshape(half, PACK, size), axis=1)
    terms = []
    for _ in range(3):
        terms.append(gram.astype(jnp.bfloat16))
        gram = gram - terms[-1].astype(jnp.float32)
    terms = [
        jnp.dot(term, fold, preferred_element_type=jnp.float32) for term in reversed(terms)
    ]
    gram = terms[0] + terms[1] + terms[2]
    for p in range(half):
        row_out[p] = gram[p : p + 1, :]
    for i in range(1, half):
        pltpu.make_async_remote_copy(
            src_ref=row_out.at[place ^ i],
            dst_ref=row_in.at[place],
            send_sem=a2a_send.at[2],
            recv_sem=a2a_recv.at[2],
            device_id={"aux": q ^ i},
            device_id_type=MESH,
        ).start()
    row_in[place] = row_out[place]
    scattered(row_in, a2a_recv.at[2])
    sum_out[...] = jnp.sum(row_in[...], axis=0)
    learn(2)

    for i in range(n_blk - 1, 0, -1):
        pltpu.make_async_remote_copy(
            src_ref=sum_out,
            dst_ref=sum_in.at[b],
            send_sem=a2a_send.at[3],
            recv_sem=a2a_recv.at[3],
            device_id={"blk": b ^ i},
            device_id_type=MESH,
        ).start()
    sum_in[b] = sum_out[...]
    pltpu.make_async_copy(
        sum_in.at[pl.ds(0, n_blk - 1)], sum_in.at[pl.ds(0, n_blk - 1)], a2a_recv.at[3]
    ).wait()
    out_ref[...] = jnp.sum(sum_in[...], axis=0)[:, : out_ref.shape[1]]

    for copy in rims + handed:
        copy.wait_send()
    scattered(all_b, a2a_send.at[0])
    scattered(all_w, a2a_send.at[1])
    scattered(row_in, a2a_send.at[2])
    pltpu.make_async_copy(
        sum_in.at[pl.ds(0, n_blk - 1)], sum_in.at[pl.ds(0, n_blk - 1)], a2a_send.at[3]
    ).wait()


def solution(mesh):
    n_blk, n_aux = mesh.shape["blk"], mesh.shape["aux"]
    rows = 2 * 3 * BS
    half = n_aux // 2
    share = rows // half
    steps = max(1, n_blk.bit_length() - 3)
    hbm = pl.BlockSpec(memory_space=pltpu.HBM)

    def on_device(tensor, intersection, counts, d_occ, d_virt):
        return pl.pallas_call(
            functools.partial(kernel, n_blk, n_aux),
            out_shape=jax.ShapeDtypeStruct((1, n_aux), jnp.float32),
            in_specs=[hbm] * 5,
            out_specs=pl.BlockSpec(memory_space=pltpu.VMEM),
            scratch_shapes=[
                pltpu.SMEM(intersection.shape, jnp.int32),
                pltpu.SMEM(counts.shape, jnp.int32),
                pltpu.VMEM((rows, BS), jnp.bfloat16),
                pltpu.VMEM((2, 6, BS, BS), jnp.bfloat16),
                pltpu.VMEM((8, 4, BS, BS), jnp.bfloat16),
                pltpu.VMEM((2, BS, BS), jnp.bfloat16),
                pltpu.VMEM((3 * rows, BS), jnp.bfloat16),
                pltpu.VMEM((rows, BS), jnp.bfloat16),
                pltpu.VMEM((n_aux, share, BS), jnp.bfloat16),
                pltpu.VMEM((half, share, BS), jnp.bfloat16),
                pltpu.VMEM((half, 1, BS), jnp.float32),
                pltpu.VMEM((half, 1, BS), jnp.float32),
                pltpu.VMEM((1, BS), jnp.float32),
                pltpu.VMEM((n_blk, 1, BS), jnp.float32),
                pltpu.SemaphoreType.DMA((5,)),
                pltpu.SemaphoreType.DMA((4,)),
                pltpu.SemaphoreType.DMA((4,)),
                pltpu.SemaphoreType.DMA((5,)),
                pltpu.SemaphoreType.DMA((5,)),
                pltpu.SemaphoreType.REGULAR((steps,)),
                pltpu.SemaphoreType.DMA((2, TEAM - 1)),
                pltpu.SemaphoreType.DMA((2, TEAM - 1)),
            ],
            compiler_params=pltpu.CompilerParams(
                collective_id=0,
                has_side_effects=True,
                vmem_limit_bytes=56550000,
            ),
        )(
            intersection,
            counts,
            tensor.reshape(rows, BS),
            d_occ,
            d_virt,
        )

    return jax.shard_map(
        on_device,
        mesh=mesh,
        in_specs=(
            P("aux", "blk", None, None, None),
            P("blk", None),
            P(),
            P("blk", None, None, None),
            P("blk", None, None, None),
        ),
        out_specs=P("aux", None),
        check_vma=False,
    )
```

```python
import functools

import jax
import jax.numpy as jnp
from jax import lax
from jax.experimental import pallas as pl
from jax.experimental.pallas import tpu as pltpu
from jax.sharding import PartitionSpec as P

MESH = pl.DeviceIdType.MESH
BS = 128
PACK = 16
TRANSPOSED = (((1,), (1,)), ((), ()))


def kernel(
    n_blk,
    n_aux,
    inter_hbm,
    counts_hbm,
    tensor_ref,
    docc_ref,
    dvirt_ref,
    out_ref,
    inter_ref,
    counts_ref,
    raw,
    omat,
    dmat,
    corner,
    ball,
    w_own,
    all_b,
    all_w,
    row_out,
    row_in,
    sum_out,
    sum_in,
    load_sem,
    rim_send,
    rim_recv,
    a2a_send,
    a2a_recv,
    known,
):
    b = lax.axis_index("blk")
    q = lax.axis_index("aux")
    nblocks = counts_ref.shape[0]
    rows = raw.shape[0]
    half = n_aux // 2
    place = q & (half - 1)
    share = rows // half
    z = b & (n_blk // 2 - 1)
    wraps = (z == 0) | (z == n_blk // 2 - 1)
    left = (b - 1) & (n_blk - 1)
    right = (b + 1) & (n_blk - 1)
    own = ball.at[pl.ds(rows, rows)]

    barrier = pltpu.get_barrier_semaphore()

    def greet(axis, there):
        pl.semaphore_signal(barrier, inc=1, device_id={axis: there}, device_id_type=MESH)

    loads = [
        pltpu.make_async_copy(tensor_ref, raw, load_sem.at[0]),
        pltpu.make_async_copy(inter_hbm, inter_ref, load_sem.at[3]),
        pltpu.make_async_copy(counts_hbm, counts_ref, load_sem.at[4]),
    ]
    for load in loads:
        load.start()

    greet("blk", right)
    greet("blk", left)
    greet("blk", (b + 2) & (n_blk - 1))
    greet("blk", (b - 2) & (n_blk - 1))
    for i in range(1, n_aux):
        greet("aux", q ^ i)

    prepare = [
        pltpu.make_async_copy(dvirt_ref.at[0, pl.ds(1, 4)], dmat.at[3], load_sem.at[1]),
        pltpu.make_async_copy(dvirt_ref.at[1, pl.ds(0, 4)], dmat.at[4], load_sem.at[1]),
        pltpu.make_async_copy(dvirt_ref.at[0, 0], corner.at[0], load_sem.at[1]),
        pltpu.make_async_copy(dvirt_ref.at[1, 4], corner.at[1], load_sem.at[1]),
        pltpu.make_async_copy(docc_ref.at[0], omat.at[0, pl.ds(0, 5)], load_sem.at[2]),
        pltpu.make_async_copy(docc_ref.at[1], omat.at[1, pl.ds(1, 5)], load_sem.at[2]),
    ]
    for load in prepare:
        load.start()

    for load in loads:
        load.wait()
    row_ids = lax.broadcasted_iota(jnp.int32, (BS, BS), 0)
    col_ids = lax.broadcasted_iota(jnp.int32, (BS, BS), 1)

    for m in range(2):
        row = 2 * b + m
        own_count = counts_ref[row]
        for w in range(3):
            col_count = counts_ref[lax.rem(row + w - 1 + nblocks, nblocks)]
            if w != 1:
                col_count = col_count * inter_ref[m, w // 2]
            keep = (row_ids < own_count) & (col_ids < col_count)
            at = pl.ds((m * 3 + w) * BS, BS)
            block = jnp.where(keep, raw[at, :].astype(jnp.float32), 0.0)
            own[at, :] = block.astype(jnp.bfloat16)

    pltpu.make_async_copy(dvirt_ref, dvirt_ref, load_sem.at[1]).wait()

    def turn(block):
        return block[...].astype(jnp.float32).T.astype(jnp.bfloat16)

    dmat[5, 1] = turn(dmat.at[3, 3])
    dmat[2, 2] = turn(dmat.at[4, 0])
    pl.semaphore_wait(barrier, 4 + n_aux - 1)

    steps = n_blk.bit_length() - 3

    def tell(step):
        if step < steps:
            for there in (b + 2 ** (step + 1), b - 2 ** (step + 1)):
                pl.semaphore_signal(
                    known.at[step],
                    inc=1,
                    device_id={"blk": there & (n_blk - 1)},
                    device_id_type=MESH,
                )

    def learn(step):
        if step < steps:
            pl.semaphore_wait(known.at[step], 2)

    def to_blk(src, dst, sem, there):
        return pltpu.make_async_remote_copy(
            src_ref=src,
            dst_ref=dst,
            send_sem=rim_send.at[sem],
            recv_sem=rim_recv.at[sem],
            device_id={"blk": there},
            device_id_type=MESH,
        )

    def band(r, c):
        return dmat.at[pl.ds(r, 3), c]

    rims = [
        to_blk(band(2, 2), band(0, 0), 0, right),
        to_blk(band(3, 1), band(5, 3), 1, left),
        to_blk(own, ball.at[pl.ds(0, rows)], 2, right),
        to_blk(own, ball.at[pl.ds(2 * rows, rows)], 3, left),
    ]
    for rim in rims:
        rim.start()
    tell(0)

    def scatter(src, first, dst, slot, sem, partners):
        for i in partners:
            there = q ^ i
            at = pl.multiple_of(first + (there & (half - 1)) * share, PACK)
            pltpu.make_async_remote_copy(
                src_ref=src.at[pl.ds(at, share)],
                dst_ref=dst.at[slot],
                send_sem=a2a_send.at[sem],
                recv_sem=a2a_recv.at[sem],
                device_id={"aux": there},
                device_id_type=MESH,
            ).start()

    def keep_own(src, first, dst, slot):
        dst[slot] = src[pl.ds(pl.multiple_of(first + place * share, PACK), share), :]

    def scattered(dst, sem):
        others = dst.at[pl.ds(0, dst.shape[0] - 1)]
        pltpu.make_async_copy(others, others, sem).wait()

    def scatter_tensor(partners):
        scatter(ball, rows, all_b, q, 0, partners)

    dmat[1, 1] = turn(corner.at[0])
    dmat[2, 1] = turn(dmat.at[3, 0])
    dmat[5, 2] = turn(dmat.at[4, 3])
    dmat[6, 2] = turn(corner.at[1])
    zero = jnp.zeros((BS, BS), jnp.bfloat16)
    for c in range(4):
        for r in range(8):
            if not 0 <= r - c <= 4:
                dmat[r, c] = zero
    for m in range(2):
        omat[m, 5 - 5 * m] = zero


    pltpu.make_async_copy(docc_ref, docc_ref, load_sem.at[2]).wait()
    scatter_tensor(range(1, half))
    pl.when(jnp.logical_not(wraps))(lambda: scatter_tensor(range(half, n_aux)))
    keep_own(ball, rows, all_b, q)
    learn(0)
    tell(1)
    rims[0].wait_recv()
    rims[1].wait_recv()

    def grid(blocks):
        return jnp.concatenate([jnp.concatenate(row, axis=1) for row in blocks], axis=0)

    def part(pair):
        blocks = [ball[pl.ds((6 * pair + i) * BS, BS), :] for i in range(6)]
        b_pair = grid([blocks[:3] + [zero], [zero] + blocks[3:]])
        d_pair = grid([[dmat[2 * pair + r, c] for c in range(4)] for r in range(4)])
        x_pair = jnp.dot(b_pair, d_pair, preferred_element_type=jnp.float32)
        return jnp.dot(
            grid([[omat[m, 2 * pair + n] for n in range(2)] for m in range(2)]),
            x_pair.astype(jnp.bfloat16),
            preferred_element_type=jnp.float32,
        )

    total = part(1)
    rims[2].wait_recv()
    total = total + part(0)
    rims[3].wait_recv()
    pl.when(wraps)(lambda: scatter_tensor(range(half, n_aux)))
    total = total + part(2)
    total = total.astype(jnp.bfloat16)
    for m in range(2):
        for w in range(3):
            w_own[pl.ds((m * 3 + w) * BS, BS), :] = total[
                m * BS : (m + 1) * BS, (m + w) * BS : (m + w + 1) * BS
            ]

    scatter(w_own, 0, all_w, place, 1, range(1, half))
    keep_own(w_own, 0, all_w, place)
    learn(1)
    tell(2)
    groups = range(share // PACK)
    size = n_aux * PACK

    def flat(ref):
        return jnp.concatenate(
            [ref[:, pl.ds(g * PACK, PACK), :].reshape(ref.shape[0] * PACK, BS) for g in groups],
            axis=1,
        )

    fold = (
        lax.broadcasted_iota(jnp.int32, (size, BS), 0) // PACK
        == lax.broadcasted_iota(jnp.int32, (size, BS), 1)
    ).astype(jnp.bfloat16)
    scattered(all_b, a2a_recv.at[0])
    scattered(all_w, a2a_recv.at[1])
    gram = lax.dot_general(
        flat(all_w), flat(all_b), TRANSPOSED, preferred_element_type=jnp.float32
    )
    same = (lax.broadcasted_iota(jnp.int32, gram.shape, 0) & (PACK - 1)) == (
        lax.broadcasted_iota(jnp.int32, gram.shape, 1) & (PACK - 1)
    )
    gram = jnp.sum(jnp.where(same, gram, 0.0).reshape(half, PACK, size), axis=1)
    terms = []
    for _ in range(3):
        terms.append(gram.astype(jnp.bfloat16))
        gram = gram - terms[-1].astype(jnp.float32)
    terms = [
        jnp.dot(term, fold, preferred_element_type=jnp.float32) for term in reversed(terms)
    ]
    gram = terms[0] + terms[1] + terms[2]
    for p in range(half):
        row_out[p] = gram[p : p + 1, :]
    for i in range(1, half):
        pltpu.make_async_remote_copy(
            src_ref=row_out.at[place ^ i],
            dst_ref=row_in.at[place],
            send_sem=a2a_send.at[2],
            recv_sem=a2a_recv.at[2],
            device_id={"aux": q ^ i},
            device_id_type=MESH,
        ).start()
    row_in[place] = row_out[place]
    scattered(row_in, a2a_recv.at[2])
    sum_out[...] = jnp.sum(row_in[...], axis=0)
    learn(2)

    for i in range(n_blk - 1, 0, -1):
        pltpu.make_async_remote_copy(
            src_ref=sum_out,
            dst_ref=sum_in.at[b],
            send_sem=a2a_send.at[3],
            recv_sem=a2a_recv.at[3],
            device_id={"blk": b ^ i},
            device_id_type=MESH,
        ).start()
    sum_in[b] = sum_out[...]
    pltpu.make_async_copy(
        sum_in.at[pl.ds(0, n_blk - 1)], sum_in.at[pl.ds(0, n_blk - 1)], a2a_recv.at[3]
    ).wait()
    out_ref[...] = jnp.sum(sum_in[...], axis=0)[:, : out_ref.shape[1]]

    for copy in rims:
        copy.wait_send()
    scattered(all_b, a2a_send.at[0])
    scattered(all_w, a2a_send.at[1])
    scattered(row_in, a2a_send.at[2])
    pltpu.make_async_copy(
        sum_in.at[pl.ds(0, n_blk - 1)], sum_in.at[pl.ds(0, n_blk - 1)], a2a_send.at[3]
    ).wait()


def solution(mesh):
    n_blk, n_aux = mesh.shape["blk"], mesh.shape["aux"]
    rows = 2 * 3 * BS
    half = n_aux // 2
    share = rows // half
    steps = max(1, n_blk.bit_length() - 3)
    hbm = pl.BlockSpec(memory_space=pltpu.HBM)

    def on_device(tensor, intersection, counts, d_occ, d_virt):
        return pl.pallas_call(
            functools.partial(kernel, n_blk, n_aux),
            out_shape=jax.ShapeDtypeStruct((1, n_aux), jnp.float32),
            in_specs=[hbm] * 5,
            out_specs=pl.BlockSpec(memory_space=pltpu.VMEM),
            scratch_shapes=[
                pltpu.SMEM(intersection.shape, jnp.int32),
                pltpu.SMEM(counts.shape, jnp.int32),
                pltpu.VMEM((rows, BS), jnp.bfloat16),
                pltpu.VMEM((2, 6, BS, BS), jnp.bfloat16),
                pltpu.VMEM((8, 4, BS, BS), jnp.bfloat16),
                pltpu.VMEM((2, BS, BS), jnp.bfloat16),
                pltpu.VMEM((3 * rows, BS), jnp.bfloat16),
                pltpu.VMEM((rows, BS), jnp.bfloat16),
                pltpu.VMEM((n_aux, share, BS), jnp.bfloat16),
                pltpu.VMEM((half, share, BS), jnp.bfloat16),
                pltpu.VMEM((half, 1, BS), jnp.float32),
                pltpu.VMEM((half, 1, BS), jnp.float32),
                pltpu.VMEM((1, BS), jnp.float32),
                pltpu.VMEM((n_blk, 1, BS), jnp.float32),
                pltpu.SemaphoreType.DMA((5,)),
                pltpu.SemaphoreType.DMA((4,)),
                pltpu.SemaphoreType.DMA((4,)),
                pltpu.SemaphoreType.DMA((5,)),
                pltpu.SemaphoreType.DMA((5,)),
                pltpu.SemaphoreType.REGULAR((steps,)),
            ],
            compiler_params=pltpu.CompilerParams(
                collective_id=0,
                has_side_effects=True,
                vmem_limit_bytes=56550000,
            ),
        )(
            intersection,
            counts,
            tensor.reshape(rows, BS),
            d_occ,
            d_virt,
        )

    return jax.shard_map(
        on_device,
        mesh=mesh,
        in_specs=(
            P("aux", "blk", None, None, None),
            P("blk", None),
            P(),
            P("blk", None, None, None),
            P("blk", None, None, None),
        ),
        out_specs=P("aux", None),
        check_vma=False,
    )
```

```python
import functools

import jax
import jax.numpy as jnp
from jax import lax
from jax.experimental import pallas as pl
from jax.experimental.pallas import tpu as pltpu
from jax.sharding import PartitionSpec as P

MESH = pl.DeviceIdType.MESH
BS = 128
PACK = 16
TEAM = 2
TRANSPOSED = (((1,), (1,)), ((), ()))


def kernel(
    n_blk,
    n_aux,
    inter_hbm,
    counts_hbm,
    tensor_ref,
    docc_ref,
    dvirt_ref,
    out_ref,
    inter_ref,
    counts_ref,
    raw,
    omat,
    dmat,
    corner,
    ball,
    w_own,
    all_b,
    all_w,
    row_out,
    row_in,
    sum_out,
    sum_in,
    load_sem,
    rim_send,
    rim_recv,
    a2a_send,
    a2a_recv,
    known,
    hand_send,
    hand_recv,
):
    b = lax.axis_index("blk")
    q = lax.axis_index("aux")
    seat = q & (TEAM - 1)
    nblocks = counts_ref.shape[0]
    rows = raw.shape[0]
    half = n_aux // 2
    place = q & (half - 1)
    share = rows // half
    z = b & (n_blk // 2 - 1)
    wraps = (z == 0) | (z == n_blk // 2 - 1)
    left = (b - 1) & (n_blk - 1)
    right = (b + 1) & (n_blk - 1)
    own = ball.at[pl.ds(rows, rows)]

    barrier = pltpu.get_barrier_semaphore()

    def greet(axis, there):
        pl.semaphore_signal(barrier, inc=1, device_id={axis: there}, device_id_type=MESH)

    loads = [
        pltpu.make_async_copy(tensor_ref, raw, load_sem.at[0]),
        pltpu.make_async_copy(inter_hbm, inter_ref, load_sem.at[3]),
        pltpu.make_async_copy(counts_hbm, counts_ref, load_sem.at[4]),
    ]
    for load in loads:
        load.start()

    greet("blk", right)
    greet("blk", left)
    greet("blk", (b + 2) & (n_blk - 1))
    greet("blk", (b - 2) & (n_blk - 1))
    for i in range(1, n_aux):
        greet("aux", q ^ i)

    prepare = [
        pltpu.make_async_copy(dvirt_ref.at[0, pl.ds(1, 4)], dmat.at[3], load_sem.at[1]),
        pltpu.make_async_copy(dvirt_ref.at[1, pl.ds(0, 4)], dmat.at[4], load_sem.at[1]),
        pltpu.make_async_copy(dvirt_ref.at[0, 0], corner.at[0], load_sem.at[1]),
        pltpu.make_async_copy(dvirt_ref.at[1, 4], corner.at[1], load_sem.at[1]),
        pltpu.make_async_copy(docc_ref.at[0], omat.at[0, pl.ds(0, 5)], load_sem.at[2]),
        pltpu.make_async_copy(docc_ref.at[1], omat.at[1, pl.ds(1, 5)], load_sem.at[2]),
    ]
    for load in prepare:
        load.start()

    for load in loads:
        load.wait()
    row_ids = lax.broadcasted_iota(jnp.int32, (BS, BS), 0)
    col_ids = lax.broadcasted_iota(jnp.int32, (BS, BS), 1)

    for m in range(2):
        row = 2 * b + m
        own_count = counts_ref[row]
        for w in range(3):
            col_count = counts_ref[lax.rem(row + w - 1 + nblocks, nblocks)]
            if w != 1:
                col_count = col_count * inter_ref[m, w // 2]
            keep = (row_ids < own_count) & (col_ids < col_count)
            at = pl.ds((m * 3 + w) * BS, BS)
            block = jnp.where(keep, raw[at, :].astype(jnp.float32), 0.0)
            own[at, :] = block.astype(jnp.bfloat16)

    pltpu.make_async_copy(dvirt_ref, dvirt_ref, load_sem.at[1]).wait()

    def turn(block):
        return block[...].astype(jnp.float32).T.astype(jnp.bfloat16)

    dmat[5, 1] = turn(dmat.at[3, 3])
    dmat[2, 2] = turn(dmat.at[4, 0])
    pl.semaphore_wait(barrier, 4 + n_aux - 1)

    steps = n_blk.bit_length() - 3

    def tell(step):
        if step < steps:
            for there in (b + 2 ** (step + 1), b - 2 ** (step + 1)):
                pl.semaphore_signal(
                    known.at[step],
                    inc=1,
                    device_id={"blk": there & (n_blk - 1)},
                    device_id_type=MESH,
                )

    def learn(step):
        if step < steps:
            pl.semaphore_wait(known.at[step], 2)

    def to_blk(src, dst, sem, there):
        return pltpu.make_async_remote_copy(
            src_ref=src,
            dst_ref=dst,
            send_sem=rim_send.at[sem],
            recv_sem=rim_recv.at[sem],
            device_id={"blk": there},
            device_id_type=MESH,
        )

    def band(r, c):
        strip = BS // TEAM
        return dmat.at[pl.ds(r, 3), c, pl.ds(pl.multiple_of(seat * strip, PACK), strip)]

    rims = [
        to_blk(band(2, 2), band(0, 0), 0, right),
        to_blk(band(3, 1), band(5, 3), 1, left),
        to_blk(own, ball.at[pl.ds(0, rows)], 2, right),
        to_blk(own, ball.at[pl.ds(2 * rows, rows)], 3, left),
    ]
    for rim in rims:
        rim.start()
    tell(0)

    def scatter(src, first, dst, slot, sem, partners):
        for i in partners:
            there = q ^ i
            at = pl.multiple_of(first + (there & (half - 1)) * share, PACK)
            pltpu.make_async_remote_copy(
                src_ref=src.at[pl.ds(at, share)],
                dst_ref=dst.at[slot],
                send_sem=a2a_send.at[sem],
                recv_sem=a2a_recv.at[sem],
                device_id={"aux": there},
                device_id_type=MESH,
            ).start()

    def keep_own(src, first, dst, slot):
        dst[slot] = src[pl.ds(pl.multiple_of(first + place * share, PACK), share), :]

    def scattered(dst, sem):
        others = dst.at[pl.ds(0, dst.shape[0] - 1)]
        pltpu.make_async_copy(others, others, sem).wait()

    def scatter_tensor(partners):
        scatter(ball, rows, all_b, q, 0, partners)

    dmat[1, 1] = turn(corner.at[0])
    dmat[2, 1] = turn(dmat.at[3, 0])
    dmat[5, 2] = turn(dmat.at[4, 3])
    dmat[6, 2] = turn(corner.at[1])
    zero = jnp.zeros((BS, BS), jnp.bfloat16)
    for c in range(4):
        for r in range(8):
            if not 0 <= r - c <= 4:
                dmat[r, c] = zero
    for m in range(2):
        omat[m, 5 - 5 * m] = zero


    pltpu.make_async_copy(docc_ref, docc_ref, load_sem.at[2]).wait()
    handed = []
    for side, rim in enumerate((band(0, 0), band(5, 3))):
        rims[side].wait_recv()
        for i in range(1, TEAM):
            handed.append(
                pltpu.make_async_remote_copy(
                    src_ref=rim,
                    dst_ref=rim,
                    send_sem=hand_send.at[side, i - 1],
                    recv_sem=hand_recv.at[side, i - 1],
                    device_id={"aux": q ^ i},
                    device_id_type=MESH,
                )
            )
            handed[-1].start()
    scatter_tensor(range(1, half))
    pl.when(jnp.logical_not(wraps))(lambda: scatter_tensor(range(half, n_aux)))
    keep_own(ball, rows, all_b, q)
    learn(0)
    tell(1)
    for copy in handed:
        copy.wait_recv()

    def grid(blocks):
        return jnp.concatenate([jnp.concatenate(row, axis=1) for row in blocks], axis=0)

    def part(pair):
        blocks = [ball[pl.ds((6 * pair + i) * BS, BS), :] for i in range(6)]
        b_pair = grid([blocks[:3] + [zero], [zero] + blocks[3:]])
        d_pair = grid([[dmat[2 * pair + r, c] for c in range(4)] for r in range(4)])
        x_pair = jnp.dot(b_pair, d_pair, preferred_element_type=jnp.float32)
        return x_pair.astype(jnp.bfloat16)

    def pull(places, x_rows):
        o_rows = grid([[omat[m, n] for n in places] for m in range(2)])
        return jnp.dot(o_rows, x_rows, preferred_element_type=jnp.float32)

    total = pull((2, 3), part(1))
    rims[2].wait_recv()
    x_left = part(0)
    rims[3].wait_recv()
    pl.when(wraps)(lambda: scatter_tensor(range(half, n_aux)))
    x_rim = jnp.concatenate([x_left, part(2)], axis=0)
    total = total + pull((0, 1, 4, 5), x_rim)
    total = total.astype(jnp.bfloat16)
    for m in range(2):
        for w in range(3):
            w_own[pl.ds((m * 3 + w) * BS, BS), :] = total[
                m * BS : (m + 1) * BS, (m + w) * BS : (m + w + 1) * BS
            ]

    scatter(w_own, 0, all_w, place, 1, range(1, half))
    keep_own(w_own, 0, all_w, place)
    learn(1)
    tell(2)
    groups = range(share // PACK)
    size = n_aux * PACK

    def flat(ref):
        return jnp.concatenate(
            [ref[:, pl.ds(g * PACK, PACK), :].reshape(ref.shape[0] * PACK, BS) for g in groups],
            axis=1,
        )

    fold = (
        lax.broadcasted_iota(jnp.int32, (size, BS), 0) // PACK
        == lax.broadcasted_iota(jnp.int32, (size, BS), 1)
    ).astype(jnp.bfloat16)
    scattered(all_b, a2a_recv.at[0])
    scattered(all_w, a2a_recv.at[1])
    gram = lax.dot_general(
        flat(all_w), flat(all_b), TRANSPOSED, preferred_element_type=jnp.float32
    )
    same = (lax.broadcasted_iota(jnp.int32, gram.shape, 0) & (PACK - 1)) == (
        lax.broadcasted_iota(jnp.int32, gram.shape, 1) & (PACK - 1)
    )
    gram = jnp.sum(jnp.where(same, gram, 0.0).reshape(half, PACK, size), axis=1)
    terms = []
    for _ in range(3):
        terms.append(gram.astype(jnp.bfloat16))
        gram = gram - terms[-1].astype(jnp.float32)
    terms = [
        jnp.dot(term, fold, preferred_element_type=jnp.float32) for term in reversed(terms)
    ]
    gram = terms[0] + terms[1] + terms[2]
    for p in range(half):
        row_out[p] = gram[p : p + 1, :]
    for i in range(1, half):
        pltpu.make_async_remote_copy(
            src_ref=row_out.at[place ^ i],
            dst_ref=row_in.at[place],
            send_sem=a2a_send.at[2],
            recv_sem=a2a_recv.at[2],
            device_id={"aux": q ^ i},
            device_id_type=MESH,
        ).start()
    row_in[place] = row_out[place]
    scattered(row_in, a2a_recv.at[2])
    sum_out[...] = jnp.sum(row_in[...], axis=0)
    learn(2)

    for i in range(n_blk - 1, 0, -1):
        pltpu.make_async_remote_copy(
            src_ref=sum_out,
            dst_ref=sum_in.at[b],
            send_sem=a2a_send.at[3],
            recv_sem=a2a_recv.at[3],
            device_id={"blk": b ^ i},
            device_id_type=MESH,
        ).start()
    sum_in[b] = sum_out[...]
    pltpu.make_async_copy(
        sum_in.at[pl.ds(0, n_blk - 1)], sum_in.at[pl.ds(0, n_blk - 1)], a2a_recv.at[3]
    ).wait()
    out_ref[...] = jnp.sum(sum_in[...], axis=0)[:, : out_ref.shape[1]]

    for copy in rims + handed:
        copy.wait_send()
    scattered(all_b, a2a_send.at[0])
    scattered(all_w, a2a_send.at[1])
    scattered(row_in, a2a_send.at[2])
    pltpu.make_async_copy(
        sum_in.at[pl.ds(0, n_blk - 1)], sum_in.at[pl.ds(0, n_blk - 1)], a2a_send.at[3]
    ).wait()


def solution(mesh):
    n_blk, n_aux = mesh.shape["blk"], mesh.shape["aux"]
    rows = 2 * 3 * BS
    half = n_aux // 2
    share = rows // half
    steps = max(1, n_blk.bit_length() - 3)
    hbm = pl.BlockSpec(memory_space=pltpu.HBM)

    def on_device(tensor, intersection, counts, d_occ, d_virt):
        return pl.pallas_call(
            functools.partial(kernel, n_blk, n_aux),
            out_shape=jax.ShapeDtypeStruct((1, n_aux), jnp.float32),
            in_specs=[hbm] * 5,
            out_specs=pl.BlockSpec(memory_space=pltpu.VMEM),
            scratch_shapes=[
                pltpu.SMEM(intersection.shape, jnp.int32),
                pltpu.SMEM(counts.shape, jnp.int32),
                pltpu.VMEM((rows, BS), jnp.bfloat16),
                pltpu.VMEM((2, 6, BS, BS), jnp.bfloat16),
                pltpu.VMEM((8, 4, BS, BS), jnp.bfloat16),
                pltpu.VMEM((2, BS, BS), jnp.bfloat16),
                pltpu.VMEM((3 * rows, BS), jnp.bfloat16),
                pltpu.VMEM((rows, BS), jnp.bfloat16),
                pltpu.VMEM((n_aux, share, BS), jnp.bfloat16),
                pltpu.VMEM((half, share, BS), jnp.bfloat16),
                pltpu.VMEM((half, 1, BS), jnp.float32),
                pltpu.VMEM((half, 1, BS), jnp.float32),
                pltpu.VMEM((1, BS), jnp.float32),
                pltpu.VMEM((n_blk, 1, BS), jnp.float32),
                pltpu.SemaphoreType.DMA((5,)),
                pltpu.SemaphoreType.DMA((4,)),
                pltpu.SemaphoreType.DMA((4,)),
                pltpu.SemaphoreType.DMA((5,)),
                pltpu.SemaphoreType.DMA((5,)),
                pltpu.SemaphoreType.REGULAR((steps,)),
                pltpu.SemaphoreType.DMA((2, TEAM - 1)),
                pltpu.SemaphoreType.DMA((2, TEAM - 1)),
            ],
            compiler_params=pltpu.CompilerParams(
                collective_id=0,
                has_side_effects=True,
                vmem_limit_bytes=56550000,
            ),
        )(
            intersection,
            counts,
            tensor.reshape(rows, BS),
            d_occ,
            d_virt,
        )

    return jax.shard_map(
        on_device,
        mesh=mesh,
        in_specs=(
            P("aux", "blk", None, None, None),
            P("blk", None),
            P(),
            P("blk", None, None, None),
            P("blk", None, None, None),
        ),
        out_specs=P("aux", None),
        check_vma=False,
    )
```

```python
import functools

import jax
import jax.numpy as jnp
from jax import lax
from jax.experimental import pallas as pl
from jax.experimental.pallas import tpu as pltpu
from jax.sharding import PartitionSpec as P

MESH = pl.DeviceIdType.MESH
BS = 128
PACK = 16
TEAM = 2
TRANSPOSED = (((1,), (1,)), ((), ()))


def kernel(
    n_blk,
    n_aux,
    inter_hbm,
    counts_hbm,
    tensor_ref,
    docc_ref,
    dvirt_ref,
    out_ref,
    inter_ref,
    counts_ref,
    raw,
    omat,
    dmat,
    corner,
    ball,
    w_own,
    all_b,
    all_w,
    row_out,
    row_in,
    sum_out,
    sum_in,
    load_sem,
    rim_send,
    rim_recv,
    a2a_send,
    a2a_recv,
    known,
    hand_send,
    hand_recv,
):
    b = lax.axis_index("blk")
    q = lax.axis_index("aux")
    seat = q & (TEAM - 1)
    nblocks = counts_ref.shape[0]
    rows = raw.shape[0]
    half = n_aux // 2
    place = q & (half - 1)
    share = rows // half
    z = b & (n_blk // 2 - 1)
    wraps = (z == 0) | (z == n_blk // 2 - 1)
    left = (b - 1) & (n_blk - 1)
    right = (b + 1) & (n_blk - 1)
    own = ball.at[pl.ds(rows, rows)]

    barrier = pltpu.get_barrier_semaphore()

    def greet(axis, there):
        pl.semaphore_signal(barrier, inc=1, device_id={axis: there}, device_id_type=MESH)

    loads = [
        pltpu.make_async_copy(tensor_ref, raw, load_sem.at[0]),
        pltpu.make_async_copy(inter_hbm, inter_ref, load_sem.at[3]),
        pltpu.make_async_copy(counts_hbm, counts_ref, load_sem.at[4]),
    ]
    for load in loads:
        load.start()

    greet("blk", right)
    greet("blk", left)
    greet("blk", (b + 2) & (n_blk - 1))
    greet("blk", (b - 2) & (n_blk - 1))
    for i in range(1, n_aux):
        greet("aux", q ^ i)

    prepare = [
        pltpu.make_async_copy(dvirt_ref.at[0, pl.ds(1, 4)], dmat.at[3], load_sem.at[1]),
        pltpu.make_async_copy(dvirt_ref.at[1, pl.ds(0, 4)], dmat.at[4], load_sem.at[1]),
        pltpu.make_async_copy(dvirt_ref.at[0, 0], corner.at[0], load_sem.at[1]),
        pltpu.make_async_copy(dvirt_ref.at[1, 4], corner.at[1], load_sem.at[1]),
        pltpu.make_async_copy(docc_ref.at[0], omat.at[0, pl.ds(0, 5)], load_sem.at[2]),
        pltpu.make_async_copy(docc_ref.at[1], omat.at[1, pl.ds(1, 5)], load_sem.at[2]),
    ]
    for load in prepare:
        load.start()

    for load in loads:
        load.wait()
    row_ids = lax.broadcasted_iota(jnp.int32, (BS, BS), 0)
    col_ids = lax.broadcasted_iota(jnp.int32, (BS, BS), 1)

    for m in range(2):
        row = 2 * b + m
        own_count = counts_ref[row]
        for w in range(3):
            col_count = counts_ref[lax.rem(row + w - 1 + nblocks, nblocks)]
            if w != 1:
                col_count = col_count * inter_ref[m, w // 2]
            keep = (row_ids < own_count) & (col_ids < col_count)
            at = pl.ds((m * 3 + w) * BS, BS)
            block = jnp.where(keep, raw[at, :].astype(jnp.float32), 0.0)
            own[at, :] = block.astype(jnp.bfloat16)

    pltpu.make_async_copy(dvirt_ref, dvirt_ref, load_sem.at[1]).wait()

    def turn(block):
        return block[...].astype(jnp.float32).T.astype(jnp.bfloat16)

    dmat[5, 1] = turn(dmat.at[3, 3])
    dmat[2, 2] = turn(dmat.at[4, 0])
    pl.semaphore_wait(barrier, 4 + n_aux - 1)

    steps = n_blk.bit_length() - 3

    def tell(step):
        if step < steps:
            for there in (b + 2 ** (step + 1), b - 2 ** (step + 1)):
                pl.semaphore_signal(
                    known.at[step],
                    inc=1,
                    device_id={"blk": there & (n_blk - 1)},
                    device_id_type=MESH,
                )

    def learn(step):
        if step < steps:
            pl.semaphore_wait(known.at[step], 2)

    def to_blk(src, dst, sem, there):
        return pltpu.make_async_remote_copy(
            src_ref=src,
            dst_ref=dst,
            send_sem=rim_send.at[sem],
            recv_sem=rim_recv.at[sem],
            device_id={"blk": there},
            device_id_type=MESH,
        )

    def band(r, c):
        strip = BS // TEAM
        return dmat.at[pl.ds(r, 3), c, pl.ds(pl.multiple_of(seat * strip, PACK), strip)]

    rims = [
        to_blk(band(2, 2), band(0, 0), 0, right),
        to_blk(band(3, 1), band(5, 3), 1, left),
        to_blk(own, ball.at[pl.ds(0, rows)], 2, right),
        to_blk(own, ball.at[pl.ds(2 * rows, rows)], 3, left),
    ]
    for rim in rims:
        rim.start()
    tell(0)

    def scatter(src, first, dst, slot, sem, partners):
        for i in partners:
            there = q ^ i
            at = pl.multiple_of(first + (there & (half - 1)) * share, PACK)
            pltpu.make_async_remote_copy(
                src_ref=src.at[pl.ds(at, share)],
                dst_ref=dst.at[slot],
                send_sem=a2a_send.at[sem],
                recv_sem=a2a_recv.at[sem],
                device_id={"aux": there},
                device_id_type=MESH,
            ).start()

    def keep_own(src, first, dst, slot):
        dst[slot] = src[pl.ds(pl.multiple_of(first + place * share, PACK), share), :]

    def scattered(dst, sem):
        others = dst.at[pl.ds(0, dst.shape[0] - 1)]
        pltpu.make_async_copy(others, others, sem).wait()

    def scatter_tensor(partners):
        scatter(ball, rows, all_b, q, 0, partners)

    dmat[1, 1] = turn(corner.at[0])
    dmat[2, 1] = turn(dmat.at[3, 0])
    dmat[5, 2] = turn(dmat.at[4, 3])
    dmat[6, 2] = turn(corner.at[1])
    zero = jnp.zeros((BS, BS), jnp.bfloat16)
    for c in range(4):
        for r in range(8):
            if not 0 <= r - c <= 4:
                dmat[r, c] = zero
    for m in range(2):
        omat[m, 5 - 5 * m] = zero


    pltpu.make_async_copy(docc_ref, docc_ref, load_sem.at[2]).wait()
    handed = []
    for side, rim in enumerate((band(0, 0), band(5, 3))):
        rims[side].wait_recv()
        for i in range(1, TEAM):
            handed.append(
                pltpu.make_async_remote_copy(
                    src_ref=rim,
                    dst_ref=rim,
                    send_sem=hand_send.at[side, i - 1],
                    recv_sem=hand_recv.at[side, i - 1],
                    device_id={"aux": q ^ i},
                    device_id_type=MESH,
                )
            )
            handed[-1].start()
    scatter_tensor(range(1, half))
    pl.when(jnp.logical_not(wraps))(lambda: scatter_tensor(range(half, n_aux)))
    keep_own(ball, rows, all_b, q)
    learn(0)
    tell(1)
    for copy in handed:
        copy.wait_recv()

    def grid(blocks):
        return jnp.concatenate([jnp.concatenate(row, axis=1) for row in blocks], axis=0)

    def part(pair):
        blocks = [ball[pl.ds((6 * pair + i) * BS, BS), :] for i in range(6)]
        b_pair = grid([blocks[:3] + [zero], [zero] + blocks[3:]])
        d_pair = grid([[dmat[2 * pair + r, c] for c in range(4)] for r in range(4)])
        x_pair = jnp.dot(b_pair, d_pair, preferred_element_type=jnp.float32)
        return x_pair.astype(jnp.bfloat16)

    def pull(places, x_rows):
        o_rows = grid([[omat[m, n] for n in places] for m in range(2)])
        return jnp.dot(o_rows, x_rows, preferred_element_type=jnp.float32)

    total = pull((2, 3), part(1))
    rims[2].wait_recv()
    x_left = part(0)
    rims[3].wait_recv()
    pl.when(wraps)(lambda: scatter_tensor(range(half, n_aux)))
    x_rim = jnp.concatenate([x_left, part(2)], axis=0)
    total = total + pull((0, 1, 4, 5), x_rim)
    total = total.astype(jnp.bfloat16)
    for m in range(2):
        for w in range(3):
            w_own[pl.ds((m * 3 + w) * BS, BS), :] = total[
                m * BS : (m + 1) * BS, (m + w) * BS : (m + w + 1) * BS
            ]

    scatter(w_own, 0, all_w, place, 1, range(1, half))
    keep_own(w_own, 0, all_w, place)
    learn(1)
    tell(2)
    groups = range(share // PACK)
    size = n_aux * PACK

    def flat(ref):
        return jnp.concatenate(
            [ref[:, pl.ds(g * PACK, PACK), :].reshape(ref.shape[0] * PACK, BS) for g in groups],
            axis=1,
        )

    fold = (
        lax.broadcasted_iota(jnp.int32, (size, BS), 0) // PACK
        == lax.broadcasted_iota(jnp.int32, (size, BS), 1)
    ).astype(jnp.bfloat16)
    scattered(all_b, a2a_recv.at[0])
    scattered(all_w, a2a_recv.at[1])
    gram = lax.dot_general(
        flat(all_w), flat(all_b), TRANSPOSED, preferred_element_type=jnp.float32
    )
    same = (lax.broadcasted_iota(jnp.int32, gram.shape, 0) & (PACK - 1)) == (
        lax.broadcasted_iota(jnp.int32, gram.shape, 1) & (PACK - 1)
    )
    gram = jnp.sum(jnp.where(same, gram, 0.0).reshape(half, PACK, size), axis=1)
    terms = []
    for _ in range(3):
        terms.append(gram.astype(jnp.bfloat16).astype(jnp.float32))
        gram = gram - terms[-1]
    terms = jnp.dot(
        jnp.concatenate(terms[::-1], axis=0).astype(jnp.bfloat16),
        fold,
        preferred_element_type=jnp.float32,
    )
    gram = terms[:half] + terms[half : 2 * half] + terms[2 * half :]
    for p in range(half):
        row_out[p] = gram[p : p + 1, :]
    for i in range(1, half):
        pltpu.make_async_remote_copy(
            src_ref=row_out.at[place ^ i],
            dst_ref=row_in.at[place],
            send_sem=a2a_send.at[2],
            recv_sem=a2a_recv.at[2],
            device_id={"aux": q ^ i},
            device_id_type=MESH,
        ).start()
    row_in[place] = row_out[place]
    scattered(row_in, a2a_recv.at[2])
    sum_out[...] = jnp.sum(row_in[...], axis=0)
    learn(2)

    for i in range(n_blk - 1, 0, -1):
        pltpu.make_async_remote_copy(
            src_ref=sum_out,
            dst_ref=sum_in.at[b],
            send_sem=a2a_send.at[3],
            recv_sem=a2a_recv.at[3],
            device_id={"blk": b ^ i},
            device_id_type=MESH,
        ).start()
    sum_in[b] = sum_out[...]
    pltpu.make_async_copy(
        sum_in.at[pl.ds(0, n_blk - 1)], sum_in.at[pl.ds(0, n_blk - 1)], a2a_recv.at[3]
    ).wait()
    out_ref[...] = jnp.sum(sum_in[...], axis=0)[:, : out_ref.shape[1]]

    for copy in rims + handed:
        copy.wait_send()
    scattered(all_b, a2a_send.at[0])
    scattered(all_w, a2a_send.at[1])
    scattered(row_in, a2a_send.at[2])
    pltpu.make_async_copy(
        sum_in.at[pl.ds(0, n_blk - 1)], sum_in.at[pl.ds(0, n_blk - 1)], a2a_send.at[3]
    ).wait()


def solution(mesh):
    n_blk, n_aux = mesh.shape["blk"], mesh.shape["aux"]
    rows = 2 * 3 * BS
    half = n_aux // 2
    share = rows // half
    steps = max(1, n_blk.bit_length() - 3)
    hbm = pl.BlockSpec(memory_space=pltpu.HBM)

    def on_device(tensor, intersection, counts, d_occ, d_virt):
        return pl.pallas_call(
            functools.partial(kernel, n_blk, n_aux),
            out_shape=jax.ShapeDtypeStruct((1, n_aux), jnp.float32),
            in_specs=[hbm] * 5,
            out_specs=pl.BlockSpec(memory_space=pltpu.VMEM),
            scratch_shapes=[
                pltpu.SMEM(intersection.shape, jnp.int32),
                pltpu.SMEM(counts.shape, jnp.int32),
                pltpu.VMEM((rows, BS), jnp.bfloat16),
                pltpu.VMEM((2, 6, BS, BS), jnp.bfloat16),
                pltpu.VMEM((8, 4, BS, BS), jnp.bfloat16),
                pltpu.VMEM((2, BS, BS), jnp.bfloat16),
                pltpu.VMEM((3 * rows, BS), jnp.bfloat16),
                pltpu.VMEM((rows, BS), jnp.bfloat16),
                pltpu.VMEM((n_aux, share, BS), jnp.bfloat16),
                pltpu.VMEM((half, share, BS), jnp.bfloat16),
                pltpu.VMEM((half, 1, BS), jnp.float32),
                pltpu.VMEM((half, 1, BS), jnp.float32),
                pltpu.VMEM((1, BS), jnp.float32),
                pltpu.VMEM((n_blk, 1, BS), jnp.float32),
                pltpu.SemaphoreType.DMA((5,)),
                pltpu.SemaphoreType.DMA((4,)),
                pltpu.SemaphoreType.DMA((4,)),
                pltpu.SemaphoreType.DMA((5,)),
                pltpu.SemaphoreType.DMA((5,)),
                pltpu.SemaphoreType.REGULAR((steps,)),
                pltpu.SemaphoreType.DMA((2, TEAM - 1)),
                pltpu.SemaphoreType.DMA((2, TEAM - 1)),
            ],
            compiler_params=pltpu.CompilerParams(
                collective_id=0,
                has_side_effects=True,
                vmem_limit_bytes=56550000,
            ),
        )(
            intersection,
            counts,
            tensor.reshape(rows, BS),
            d_occ,
            d_virt,
        )

    return jax.shard_map(
        on_device,
        mesh=mesh,
        in_specs=(
            P("aux", "blk", None, None, None),
            P("blk", None),
            P(),
            P("blk", None, None, None),
            P("blk", None, None, None),
        ),
        out_specs=P("aux", None),
        check_vma=False,
    )
```
